32 devices in a mesh: gy: 4 (over y, x), gx: 8 (over z, core).
Axes of the slice: x: 2, y: 2, z: 4, core: 2. Of those that a mesh axis runs over, the one named last changes fastest.
Arguments:
- pixels: bfloat16 [6, 32, 64, 1536], P(None, 'gy', 'gx'), may hold values from -6 to 6
- pad_mask: int32 [6, 32, 64], P(None, 'gy', 'gx'), may hold values 0 or 1
- timestamps: int32 [5, 6], replicated, may hold values from 0 to 1999
- scene_dates: int32 [5], replicated, may hold values from 1 to 6, as said below
- scene_map: int32 [4, 8], replicated, may hold values from 0 to 4, as said below
- blend_weight: int32 [48, 96], P('gy', 'gx'), may hold values from 1 to 3
- cotangent: bfloat16 [6, 32, 64, 1536], P(None, 'gy', 'gx'), may hold values from -6 to 6
- patch_w: bfloat16 [1536, 768], P('gx'), may hold values from -0.15625 to 0.15625
- norm1_gain: bfloat16 [768], P('gx'), may hold values from 0.099609375 to 1.8984375
- norm1_bias: bfloat16 [768], P('gx'), may hold values from -2 to 2
- qkv_w: bfloat16 [768, 2304], P('gx'), may hold values from -0.3125 to 0.3125
- proj_w: bfloat16 [768, 768], P('gx'), may hold values from -1.25 to 1.25
- norm2_gain: bfloat16 [768], P('gx'), may hold values from 0.099609375 to 1.8984375
- norm2_bias: bfloat16 [768], P('gx'), may hold values from -2 to 2
- fc1_w: bfloat16 [768, 3072], P('gx'), may hold values from -0.21875 to 0.21875
- fc1_b: bfloat16 [3072], P('gx'), may hold values from -3 to 3
- fc2_w: bfloat16 [3072, 768], P('gx'), may hold values from -0.109375 to 0.109375
- dec_w: bfloat16 [768, 512], P('gx'), may hold values from -0.21875 to 0.21875
- head_w: bfloat16 [512, 1536], P('gx'), may hold values from -0.25 to 0.25
Outputs:
- recon: bfloat16 [6, 32, 64, 1536], P(None, 'gy', 'gx')
- pixel_grad: float32 [6, 32, 64, 1536], P(None, 'gy', 'gx')
- grad_patch_w: float32 [1536, 768], P('gx')
- grad_norm1_gain: float32 [768], P('gx')
- grad_norm1_bias: float32 [768], P('gx')
- grad_qkv_w: float32 [768, 2304], P('gx')
- grad_proj_w: float32 [768, 768], P('gx')
- grad_norm2_gain: float32 [768], P('gx')
- grad_norm2_bias: float32 [768], P('gx')
- grad_fc1_w: float32 [768, 3072], P('gx')
- grad_fc1_b: float32 [3072], P('gx')
- grad_fc2_w: float32 [3072, 768], P('gx')
- grad_dec_w: float32 [768, 512], P('gx')
- grad_head_w: float32 [512, 1536], P('gx')
The draws below stay inside these ranges and needn't reach their ends.
Inputs may be any that keep to these rules, and one draw needn't show every extreme that they name: `scene_dates`: dates of each scene; scene 0 has all 6. `scene_map`: scene number of each tile; scene 0 holds a whole tile row and a whole tile column.
All inputs are finite; a program needn't handle non-finite values. No bound on the sum of `pad_mask` on one device may be relied on, other than what follows from the above.
Results may differ from the reference program's by a relative error of at most 0.02.
Values may be sent and summed in bfloat16 or wider, within the bound.
No kernel may reach another device: no remote copies, remote signals or barrier semaphores. Data moves between devices by JAX's collectives and lax.ppermute only.
A program may use at most 256 MiB of HBM per device.

```python
import jax
import jax.numpy as jnp
import numpy as np
from jax import lax

P_SIZE = 1536
D = 768
HEADS = 12
FF = 3072
DEC = 512
DATES = 6
SCENES = 5
MARGIN = 2
TILE = 8
TILES_Y = 4
TILES_X = 8
EXT = 12
ROWS = 32
COLS = 64


def draw_scene_dates(key, part):
    key = jax.random.fold_in(key, 11)
    counts = jax.random.randint(key, (SCENES,), 1, DATES + 1).astype(jnp.int32)
    return counts.at[0].set(DATES)


def draw_scene_map(key, part):
    key = jax.random.fold_in(key, 23)
    keys_four = jax.random.split(key, 4)
    row_cut = jax.random.randint(keys_four[2], (), 1, TILES_Y)
    col_cut = jax.random.randint(keys_four[3], (), 1, TILES_X)
    row_pick = jax.random.randint(keys_four[0], (), 0, row_cut)
    col_pick = jax.random.randint(keys_four[1], (), 0, col_cut)
    row_ids = jnp.arange(TILES_Y, dtype=jnp.int32)[:, None]
    col_ids = jnp.arange(TILES_X, dtype=jnp.int32)[None, :]
    blocks = 1 + 2 * (row_ids >= row_cut).astype(jnp.int32) + (col_ids >= col_cut).astype(jnp.int32)
    crossing = (row_ids == row_pick) | (col_ids == col_pick)
    return jnp.where(crossing, 0, blocks).astype(jnp.int32)


def set_ends(values, rng, least, high):
    longest = values.shape.index(max(values.shape))
    spots = []
    for shift in (0, 1):
        where = [jax.random.randint(jax.random.fold_in(rng, axis), (), 0, length) for axis, length in enumerate(values.shape)]
        where[longest] = (where[longest] + shift) % values.shape[longest]
        spots.append(tuple(where))
    return values.at[spots[0]].set(least).at[spots[1]].set(high)


def block_scale(rng, dims, pieces, smallest, high):
    factor_of, own = 1.0, jax.random.fold_in(rng, 6)
    for dim, shards_of in pieces:
        heights = jnp.exp(jax.random.uniform(jax.random.fold_in(own, dim), (shards_of,), jnp.float32, smallest / len(pieces), high / len(pieces)))
        factor_of = factor_of * jnp.repeat(heights, dims[dim] // shards_of).reshape([-1 if axis == dim else 1 for axis in range(len(dims))])
    return factor_of


def scatter_about(key, shape, width, bound, cuts=(), held_as=jnp.bfloat16):
    drawn = width * jax.random.normal(key, shape, jnp.float32)
    if cuts:
        drawn = drawn * block_scale(key, shape, cuts, -0.22, 0.18)
    return jnp.clip(drawn, -bound, bound).astype(held_as)


def setup_inputs(seed: int = 0) -> dict:
    streams_of = jax.random.split(jax.random.key(seed), 20)
    return {
        "pixels": scatter_about(streams_of[0], (DATES, ROWS, COLS, P_SIZE), 1.0, 6.0, ((1, 4), (2, 8))),
        "pad_mask": set_ends((jax.random.randint(streams_of[1], (DATES, ROWS, COLS), 0, 8) < 7).astype(jnp.int32), jax.random.fold_in(streams_of[1], 1), 0, 1),
        "timestamps": set_ends(jax.random.randint(streams_of[2], (SCENES, DATES), 0, 2000), jax.random.fold_in(streams_of[2], 1), 0, 1999).astype(jnp.int32),
        "scene_dates": draw_scene_dates(jax.random.fold_in(streams_of[19], 71), 0),
        "scene_map": draw_scene_map(jax.random.fold_in(streams_of[19], 71), 0),
        "blend_weight": set_ends(jax.random.randint(streams_of[5], (TILES_Y * EXT, TILES_X * EXT), 1, 4), jax.random.fold_in(streams_of[5], 1), 1, 3).astype(jnp.int32),
        "cotangent": scatter_about(streams_of[6], (DATES, ROWS, COLS, P_SIZE), 1.0, 6.0, ((1, 4), (2, 8))),
        "patch_w": scatter_about(streams_of[7], (P_SIZE, D), P_SIZE ** -0.5, 0.15625, ((0, 8),)),
        "norm1_gain": jnp.clip(1.0 + 0.18 * jax.random.normal(streams_of[8], (D,), jnp.float32), 0.099609375, 1.8984375).astype(jnp.bfloat16),
        "norm1_bias": scatter_about(streams_of[9], (D,), 0.3, 2.0, ((0, 8),)),
        "qkv_w": scatter_about(streams_of[10], (D, 3 * D), (D // 2) ** -0.5, 0.3125, ((0, 8),)),
        "proj_w": scatter_about(streams_of[11], (D, D), (D // 32) ** -0.5, 1.25, ((0, 8),)),
        "norm2_gain": jnp.clip(1.0 + 0.18 * jax.random.normal(streams_of[12], (D,), jnp.float32), 0.099609375, 1.8984375).astype(jnp.bfloat16),
        "norm2_bias": scatter_about(streams_of[13], (D,), 0.3, 2.0, ((0, 8),)),
        "fc1_w": scatter_about(streams_of[14], (D, FF), D ** -0.5, 0.21875, ((0, 8),)),
        "fc1_b": scatter_about(streams_of[15], (FF,), 0.5, 3.0, ((0, 8),)),
        "fc2_w": scatter_about(streams_of[16], (FF, D), FF ** -0.5, 0.109375, ((0, 8),)),
        "dec_w": scatter_about(streams_of[17], (D, DEC), D ** -0.5, 0.21875, ((0, 8),)),
        "head_w": scatter_about(streams_of[18], (DEC, P_SIZE), DEC ** -0.5, 0.25, ((0, 8),)),
    }


norm_eps = 1e-06
highest = lax.Precision.HIGHEST

@jax.custom_vjp
def low(v):
    return lax.optimization_barrier(v.astype(jnp.bfloat16)).astype(jnp.float32)

@jax.custom_vjp
def low_back(v):
    return v

def low_keep(v):
    return (low(v), None)

def low_pass(kept, grad):
    return (grad,)

def back_keep(v):
    return (v, None)

def back_low(kept, grad):
    return (low(grad),)
low.defvjp(low_keep, low_pass)
low_back.defvjp(back_keep, back_low)

def matmul(left, right):
    return jnp.dot(left, right, precision=highest, preferred_element_type=jnp.float32)

def layer_norm(hidden, gain_vec, shift_vec):
    center = lax.optimization_barrier(jnp.mean(hidden, axis=-1, keepdims=True))
    centered = hidden - center
    spread = lax.optimization_barrier(jnp.mean(centered * centered, axis=-1, keepdims=True))
    return centered * lax.rsqrt(spread + norm_eps) * gain_vec + shift_vec

def sincos(places, span_width):
    half_width = span_width // 2
    omega = 1.0 / 10000.0 ** (jnp.arange(half_width, dtype=jnp.float32) / half_width)
    angles = places[:, None] * omega[None, :]
    return jnp.concatenate([jnp.sin(angles), jnp.cos(angles)], axis=1)

def position_table(tile_row, tile_col, stamps, tile_side, model_width):
    side_width = model_width // 16 * 6
    time_width = model_width - 2 * side_width
    extent = tile_side + 2 * MARGIN
    num_dates = stamps.shape[0]
    offsets = jnp.arange(extent, dtype=jnp.int32) - MARGIN
    row_places = (tile_row * tile_side + offsets).astype(jnp.float32)
    col_places = (tile_col * tile_side + offsets).astype(jnp.float32)
    time_part = sincos(stamps.astype(jnp.float32), time_width)[:, None, None, :]
    row_part = sincos(row_places, side_width)[None, :, None, :]
    col_part = sincos(col_places, side_width)[None, None, :, :]
    full_shape = (num_dates, extent, extent)
    table = jnp.concatenate([jnp.broadcast_to(time_part, full_shape + (time_width,)), jnp.broadcast_to(row_part, full_shape + (side_width,)), jnp.broadcast_to(col_part, full_shape + (side_width,))], axis=-1)
    return table.reshape(num_dates * extent * extent, model_width)

def tile_forward(tile_item, weights):
    ext_tile, tile_row, tile_col, stamps, key_ok = tile_item
    patch_w, norm1_gain, norm1_bias, qkv_w, proj_w, norm2_gain, norm2_bias, fc1_w, fc1_b, fc2_w, dec_w, head_w = weights
    token_count = ext_tile.shape[0]
    model_width = patch_w.shape[1]
    head_dim = model_width // HEADS
    scale = float(head_dim) ** (-0.5)
    position = position_table(tile_row, tile_col, stamps, TILE, model_width)
    embedded = low_back(matmul(ext_tile, patch_w))
    trunk0 = embedded + position
    normed1 = low(layer_norm(trunk0, norm1_gain, norm1_bias))
    mixed = matmul(normed1, qkv_w)
    query = low(low_back(mixed[:, :model_width])).reshape(token_count, HEADS, head_dim)
    keys_all = low(low_back(mixed[:, model_width:2 * model_width])).reshape(token_count, HEADS, head_dim)
    values_all = low(low_back(mixed[:, 2 * model_width:])).reshape(token_count, HEADS, head_dim)
    scores = jnp.einsum('nhe,mhe->hnm', query, keys_all, precision=highest) * scale
    scores = low_back(jnp.where(key_ok[None, None, :], scores, -1000000000.0))
    probs = low(jax.nn.softmax(scores, axis=-1))
    attended = jnp.einsum('hnm,mhe->nhe', probs, values_all, precision=highest).reshape(token_count, model_width)
    attended = low(low_back(attended))
    trunk1 = trunk0 + low_back(matmul(attended, proj_w))
    normed2 = low(layer_norm(trunk1, norm2_gain, norm2_bias))
    hidden_pre = low_back(matmul(normed2, fc1_w) + fc1_b)
    hidden_act = low(jax.nn.gelu(hidden_pre, approximate=False))
    trunk2 = trunk1 + low_back(matmul(hidden_act, fc2_w))
    decoded = low(low_back(matmul(low(trunk2), dec_w)))
    return low_back(matmul(decoded, head_w))

def reference(pixels, pad_mask, timestamps, scene_dates, scene_map, blend_weight, cotangent, patch_w, norm1_gain, norm1_bias, qkv_w, proj_w, norm2_gain, norm2_bias, fc1_w, fc1_b, fc2_w, dec_w, head_w):
    tile_count = TILES_Y * TILES_X
    token_count = DATES * EXT * EXT
    row_index = np.arange(TILES_Y)[:, None] * TILE + np.arange(EXT)[None, :]
    col_index = np.arange(TILES_X)[:, None] * TILE + np.arange(EXT)[None, :]
    grid_rows = row_index[:, :, None, None]
    grid_cols = col_index[None, None, :, :]
    scene_patch = jnp.repeat(jnp.repeat(scene_map, TILE, axis=0), TILE, axis=1)
    scene_frame = jnp.pad(scene_patch, MARGIN, constant_values=-1)
    scene_ext = scene_frame[grid_rows, grid_cols].transpose(0, 2, 1, 3)
    same = scene_ext == scene_map[:, :, None, None]
    weight_tile = blend_weight.reshape(TILES_Y, EXT, TILES_X, EXT).transpose(0, 2, 1, 3).astype(jnp.float32) * same.astype(jnp.float32)
    denom_frame = jnp.zeros((ROWS + 2 * MARGIN, COLS + 2 * MARGIN), jnp.float32).at[grid_rows, grid_cols].add(weight_tile.transpose(0, 2, 1, 3))
    denom = denom_frame[MARGIN:-MARGIN, MARGIN:-MARGIN]
    tile_dates = scene_dates[scene_map]
    date_ok = jnp.arange(DATES, dtype=jnp.int32)[None, None, :] < tile_dates[:, :, None]
    key_ok = (date_ok[:, :, :, None, None] & same[:, :, None, :, :]).reshape(tile_count, token_count)
    tile_stamps = timestamps[scene_map].reshape(tile_count, DATES)
    tile_rows = jnp.repeat(jnp.arange(TILES_Y, dtype=jnp.int32), TILES_X)
    tile_cols = jnp.tile(jnp.arange(TILES_X, dtype=jnp.int32), TILES_Y)
    patch_dates = scene_dates[scene_patch]
    valid = pad_mask.astype(jnp.float32) * (jnp.arange(DATES, dtype=jnp.int32)[:, None, None] < patch_dates[None]).astype(jnp.float32)
    mask_pixels = pad_mask.astype(jnp.float32)[..., None]

    def forward(pixel_vals, *weights):
        masked = pixel_vals * mask_pixels
        framed = jnp.pad(masked, ((0, 0), (MARGIN, MARGIN), (MARGIN, MARGIN), (0, 0)))
        ext_all = framed[:, grid_rows, grid_cols]
        ext_all = ext_all.transpose(1, 3, 0, 2, 4, 5).reshape(tile_count, token_count, P_SIZE)

        def step(carry, tile_item):
            return (carry, jax.checkpoint(tile_forward)(tile_item, weights))
        _, preds = lax.scan(step, 0, (ext_all, tile_rows, tile_cols, tile_stamps, key_ok))
        weighted = preds.reshape(TILES_Y, TILES_X, DATES, EXT, EXT, P_SIZE) * weight_tile[:, :, None, :, :, None]
        numer_frame = jnp.zeros((DATES, ROWS + 2 * MARGIN, COLS + 2 * MARGIN, P_SIZE), jnp.float32).at[:, grid_rows, grid_cols].add(weighted.transpose(2, 0, 3, 1, 4, 5))
        numer = numer_frame[:, MARGIN:-MARGIN, MARGIN:-MARGIN]
        return valid[..., None] * numer / denom[None, :, :, None]
    weights32 = (patch_w.astype(jnp.float32), norm1_gain.astype(jnp.float32), norm1_bias.astype(jnp.float32), qkv_w.astype(jnp.float32), proj_w.astype(jnp.float32), norm2_gain.astype(jnp.float32), norm2_bias.astype(jnp.float32), fc1_w.astype(jnp.float32), fc1_b.astype(jnp.float32), fc2_w.astype(jnp.float32), dec_w.astype(jnp.float32), head_w.astype(jnp.float32))
    recon, pullback = jax.vjp(forward, pixels.astype(jnp.float32), *weights32)
    grads = pullback(cotangent.astype(jnp.float32))
    return (recon.astype(jnp.bfloat16), grads[0], grads[1], grads[2], grads[3], grads[4], grads[5], grads[6], grads[7], grads[8], grads[9], grads[10], grads[11], grads[12])
```

```python
import functools
import jax
import jax.numpy as jnp
import numpy as np
from jax import lax
from jax.experimental import pallas as pl
from jax.experimental.pallas import tpu as pltpu
from jax.sharding import PartitionSpec as P

HEADS = 12
MARGIN = 2
norm_eps = 1e-06
VMEM_BYTES = 56 * 1024 * 1024
f32, bf16 = jnp.float32, jnp.bfloat16


def params():
    return pltpu.CompilerParams(vmem_limit_bytes=VMEM_BYTES)


def cost(flops, nbytes):
    return pl.CostEstimate(flops=int(flops), bytes_accessed=int(nbytes), transcendentals=0)


def dot(a, b, ca=1, cb=0):
    return lax.dot_general(a, b, (((ca,), (cb,)), ((), ())), preferred_element_type=f32)


def whole(shape):
    return pl.BlockSpec(shape, lambda *_: (0,) * len(shape))


def rows(block, width):
    return pl.BlockSpec((block, width), lambda i: (i, 0))


def last_part(width):
    return pl.BlockSpec((1, width, width), lambda i: (3, 0, 0))


def norm_parts(hidden):
    center = jnp.mean(hidden, axis=-1, keepdims=True)
    centered = hidden - center
    spread = jnp.mean(centered * centered, axis=-1, keepdims=True)
    rstd = lax.rsqrt(spread + norm_eps)
    return centered * rstd, rstd


def token_block(tokens):
    for parts in (3, 2):
        if tokens % (16 * parts) == 0:
            return tokens // parts
    return tokens


def stacked(ref, depth):
    shares = ref.shape[0]
    return ref[:, : depth // shares, :].reshape(depth, ref.shape[2])


def embed_kernel(ext_ref, w_ref, pick_ref, table_ref, gain_ref, shift_ref, h0_ref, a_ref):
    hidden = dot(ext_ref[...], stacked(w_ref, ext_ref.shape[1])) + dot(pick_ref[...], table_ref[...])
    h0_ref[...] = hidden
    xhat, _ = norm_parts(hidden)
    a_ref[...] = (xhat * gain_ref[...] + shift_ref[...]).astype(bf16)


def embed(ext, patch_w, pick, table, gain, shift):
    tokens, depth = ext.shape
    width = patch_w.shape[2]
    tb = token_block(tokens)
    return pl.pallas_call(
        embed_kernel,
        grid=(tokens // tb,),
        in_specs=[rows(tb, depth), whole(patch_w.shape), rows(tb, pick.shape[1]),
                  whole(table.shape), whole(gain.shape), whole(shift.shape)],
        out_specs=[rows(tb, width), rows(tb, width)],
        out_shape=[jax.ShapeDtypeStruct((tokens, width), f32),
                   jax.ShapeDtypeStruct((tokens, width), bf16)],
        compiler_params=params(),
        cost_estimate=cost(2 * tokens * depth * width, tokens * depth * 2 + depth * width * 2 + tokens * width * 6),
        name="embed",
    )(ext, patch_w, pick, table, gain, shift)


def columns_kernel(a_ref, w_ref, o_ref):
    o_ref[...] = dot(a_ref[...], w_ref[0]).astype(o_ref.dtype)


def project(a, parts, count):
    tokens, width = a.shape
    half = width // 2
    return pl.pallas_call(
        columns_kernel,
        grid=(2 * count,),
        in_specs=[whole(a.shape), pl.BlockSpec((1, width, half), lambda i: (i // 2, 0, i % 2))],
        out_specs=pl.BlockSpec((tokens, half), lambda i: (0, i)),
        out_shape=jax.ShapeDtypeStruct((tokens, count * width), bf16),
        compiler_params=params(),
        cost_estimate=cost(2 * tokens * width * width * count, a.size * 2 + width * width * count * 2 + tokens * width * count * 2),
        name="project",
    )(a, parts)


def three_parts(value):
    first = value.astype(bf16)
    rest = value - first.astype(f32)
    second = rest.astype(bf16)
    third = (rest - second.astype(f32)).astype(bf16)
    return first, second, third


def in_lanes(parts, lane, tail):
    out = tail
    for spot, part in reversed(list(enumerate(parts))):
        out = jnp.where(lane == spot, part.astype(f32), out)
    return out.astype(bf16)


def attn_fwd_kernel(q_ref, k_ref, v_ref, kx_ref, o_ref, qx_ref, *, block, scale):
    tokens, pair = q_ref.shape
    half = pair // 2
    k_aug = jnp.concatenate([k_ref[...], kx_ref[...]], axis=1)
    v_aug = jnp.concatenate([v_ref[...], jnp.ones((tokens, pair), bf16)], axis=1)
    lane = lax.broadcasted_iota(jnp.int32, (block, pair), 1)
    for start in range(0, tokens, block):
        q_blk = q_ref[start : start + block, :].astype(f32) * scale
        outs = []
        for j in range(2):
            mine = (lane >= half) if j else (lane < half)
            q_aug = jnp.concatenate(
                [jnp.where(mine, q_blk, 0.0).astype(bf16),
                 jnp.where(lane == 3, 1.0, 0.0).astype(bf16)], axis=1)
            s = dot(q_aug, k_aug, 1, 1)
            top = jnp.max(s, axis=1, keepdims=True)
            p = jnp.exp(s - top).astype(bf16)
            mixed = dot(p, v_aug)
            total = mixed[:, pair:]
            outs.append(mixed[:, :pair] / total)
            lse = jnp.log(total) + top
            qx_ref[j, start : start + block, :] = in_lanes(
                three_parts(-lse), lane, jnp.where(lane == 3, 1.0, 0.0))
        o_ref[start : start + block, :] = jnp.where(lane < half, outs[0], outs[1]).astype(bf16)


def attn_fwd(qkv, kx, scale):
    tokens = qkv.shape[0]
    width = qkv.shape[1] // 3
    pairs = HEADS // 2
    pw = width // pairs
    spec = lambda part: pl.BlockSpec((tokens, pw), lambda h, part=part: (0, part * pairs + h))
    return pl.pallas_call(
        functools.partial(attn_fwd_kernel, block=token_block(tokens), scale=scale),
        grid=(pairs,),
        in_specs=[spec(0), spec(1), spec(2), whole(kx.shape)],
        out_specs=[pl.BlockSpec((tokens, pw), lambda h: (0, h)),
                   pl.BlockSpec((2, tokens, pw), lambda h: (h, 0, 0))],
        out_shape=[jax.ShapeDtypeStruct((tokens, width), bf16),
                   jax.ShapeDtypeStruct((HEADS, tokens, pw), bf16)],
        compiler_params=params(),
        cost_estimate=cost(2 * 4 * HEADS * tokens * tokens * 256, qkv.size * 2 + tokens * width * 2),
        name="attn_fwd",
    )(qkv, qkv, qkv, kx)


def attn_bwd_kernel(q_ref, k_ref, v_ref, do_ref, o_ref, qx_ref, kx_ref, d_ref, *, block, scale):
    tokens, pair = q_ref.shape
    half = pair // 2
    lane = lax.broadcasted_iota(jnp.int32, (tokens, pair), 1)
    q_all = q_ref[...].astype(f32) * scale
    do_all = do_ref[...].astype(f32)
    prod = do_all * o_ref[...].astype(f32)
    kx = kx_ref[...]
    dq = [None, None]
    dk = [None] * (tokens // block)
    dv = [None] * (tokens // block)
    for j in range(2):
        mine = (lane >= half) if j else (lane < half)
        q_j = jnp.where(mine, q_all, 0.0).astype(bf16)
        do_j = jnp.where(mine, do_all, 0.0).astype(bf16)
        delta = jnp.sum(jnp.where(mine, prod, 0.0), axis=1, keepdims=True)
        dox = in_lanes(three_parts(-delta), lane, jnp.zeros_like(prod))
        q_aug = jnp.concatenate([q_j, qx_ref[j]], axis=1)
        do_aug = jnp.concatenate([do_j, dox], axis=1)
        for b in range(tokens // block):
            at = slice(b * block, (b + 1) * block)
            k_blk = k_ref[at, :]
            sT = dot(jnp.concatenate([k_blk, kx[at]], axis=1), q_aug, 1, 1)
            pT = jnp.exp(sT)
            dpT = dot(jnp.concatenate([v_ref[at, :], kx[at]], axis=1), do_aug, 1, 1)
            dsT = (pT * dpT).astype(bf16)
            dv_b = dot(pT.astype(bf16), do_j)
            dk_b = dot(dsT, q_j)
            dq_b = dot(dsT, k_blk, 0, 0)
            dv[b] = dv_b if dv[b] is None else dv[b] + dv_b
            dk[b] = dk_b if dk[b] is None else dk[b] + dk_b
            dq[j] = dq_b if dq[j] is None else dq[j] + dq_b
    for b in range(tokens // block):
        at = slice(b * block, (b + 1) * block)
        d_ref[1, at, :] = dk[b].astype(bf16)
        d_ref[2, at, :] = dv[b].astype(bf16)
    d_ref[0] = (jnp.where(lane < half, dq[0], dq[1]) * scale).astype(bf16)


def attn_bwd(qkv, do, o, qx, kx, scale):
    tokens = qkv.shape[0]
    width = qkv.shape[1] // 3
    pairs = HEADS // 2
    pw = width // pairs
    spec = lambda part: pl.BlockSpec((tokens, pw), lambda h, part=part: (0, part * pairs + h))
    one = pl.BlockSpec((tokens, pw), lambda h: (0, h))
    return pl.pallas_call(
        functools.partial(attn_bwd_kernel, block=token_block(tokens), scale=scale),
        grid=(pairs,),
        in_specs=[spec(0), spec(1), spec(2), one, one,
                  pl.BlockSpec((2, tokens, pw), lambda h: (h, 0, 0)), whole(kx.shape)],
        out_specs=pl.BlockSpec((3, tokens, pw), lambda h: (0, 0, h)),
        out_shape=jax.ShapeDtypeStruct((3, tokens, width), bf16),
        compiler_params=params(),
        cost_estimate=cost(2 * 5 * HEADS * tokens * tokens * 256, qkv.size * 2 + tokens * width * 10),
        name="attn_bwd",
    )(qkv, qkv, qkv, do, o, qx, kx)


def proj_kernel(o_ref, w_ref, h0_ref, gain_ref, shift_ref, h1_ref, c_ref):
    hidden = h0_ref[...] + dot(o_ref[...], w_ref[0])
    h1_ref[...] = hidden
    xhat, _ = norm_parts(hidden)
    c_ref[...] = (xhat * gain_ref[...] + shift_ref[...]).astype(bf16)


def proj_norm(o, proj_w, h0, gain, shift):
    tokens, width = o.shape
    tb = token_block(tokens)
    return pl.pallas_call(
        proj_kernel,
        grid=(tokens // tb,),
        in_specs=[rows(tb, width), last_part(width), rows(tb, width), whole(gain.shape), whole(shift.shape)],
        out_specs=[rows(tb, width), rows(tb, width)],
        out_shape=[jax.ShapeDtypeStruct((tokens, width), f32),
                   jax.ShapeDtypeStruct((tokens, width), bf16)],
        compiler_params=params(),
        cost_estimate=cost(2 * tokens * width * width, tokens * width * 12 + width * width * 2),
        name="proj_norm",
    )(o, proj_w, h0, gain, shift)


def mlp_fwd_kernel(c_ref, fc1_ref, b_ref, fc2_ref, h1_ref, u_ref, g_ref, h2_ref, acc_ref):
    step = pl.program_id(0)
    pre = dot(c_ref[...], fc1_ref[0]) + b_ref[...]
    cdf = 0.5 * (1.0 + lax.erf(pre * np.float32(0.5 ** 0.5)))
    act = (pre * cdf).astype(bf16)
    u_ref[...] = act
    g_ref[...] = (cdf + pre * jnp.exp(-0.5 * pre * pre) * np.float32((2 * np.pi) ** -0.5)).astype(bf16)
    part = dot(act, fc2_ref[...])

    @pl.when(step == 0)
    def _():
        acc_ref[...] = h1_ref[...] + part

    @pl.when(step > 0)
    def _():
        acc_ref[...] += part

    @pl.when(step == pl.num_programs(0) - 1)
    def _():
        h2_ref[...] = acc_ref[...].astype(bf16)


def mlp_fwd(c, fc1, bias, fc2, h1):
    tokens, width = c.shape
    parts, _, block = fc1.shape
    ff = parts * block
    cols = lambda n: pl.BlockSpec((n, block), lambda i: (0, i))
    return pl.pallas_call(
        mlp_fwd_kernel,
        grid=(ff // block,),
        in_specs=[whole(c.shape), pl.BlockSpec((1, width, block), lambda i: (i, 0, 0)), cols(1),
                  pl.BlockSpec((block, width), lambda i: (i, 0)), whole(h1.shape)],
        out_specs=[cols(tokens), cols(tokens), whole(c.shape)],
        out_shape=[jax.ShapeDtypeStruct((tokens, ff), bf16), jax.ShapeDtypeStruct((tokens, ff), bf16),
                   jax.ShapeDtypeStruct((tokens, width), bf16)],
        scratch_shapes=[pltpu.VMEM((tokens, width), f32)],
        compiler_params=params(),
        cost_estimate=cost(4 * tokens * width * ff, tokens * ff * 4 + width * ff * 4 + tokens * width * 8),
        name="mlp_fwd",
    )(c, fc1, bias, fc2, h1)


def split_rows(value, core, keep_ref, send_ref, chips):
    width = value.shape[1]
    value = value.astype(bf16).reshape(chips, 2, value.shape[0] // chips // 2, width)
    even, odd = value[:, 0], value[:, 1]

    @pl.when(core == 0)
    def _():
        keep_ref[...] = even
        send_ref[...] = odd

    @pl.when(core == 1)
    def _():
        keep_ref[...] = odd
        send_ref[...] = even


def mlp_bwd_kernel(pos_ref, dm_ref, c_ref, u_ref, g_ref, fc1_ref, fc2_ref, dc_ref, gb_ref, k1_ref, s1_ref, k2_ref, s2_ref, *, chips):
    step = pl.program_id(0)
    core = pos_ref[2]
    dm = dm_ref[...]
    df32 = dot(dm, fc2_ref[...], 1, 1) * g_ref[...].astype(f32)
    df = df32.astype(bf16)
    gb_ref[...] = jnp.sum(df.astype(f32), axis=0, keepdims=True)
    parts, rows_each = k2_ref.shape[0], k2_ref.shape[2]
    width = dm.shape[1]
    grad2 = dot(u_ref[...], dm, 0, 0).astype(bf16).reshape(2, parts, rows_each, width)
    split_two(grad2, core, k2_ref, s2_ref)
    split_rows(dot(c_ref[...], df, 0, 0), core, k1_ref.at[0], s1_ref.at[0], chips)
    part = dot(df, fc1_ref[0], 1, 1)

    @pl.when(step == 0)
    def _():
        dc_ref[...] = part

    @pl.when(step > 0)
    def _():
        dc_ref[...] += part


def split_two(pair, core, keep_ref, send_ref):
    @pl.when(core == 0)
    def _():
        keep_ref[:, 0] = pair[0]
        send_ref[:, 0] = pair[1]

    @pl.when(core == 1)
    def _():
        keep_ref[:, 0] = pair[1]
        send_ref[:, 0] = pair[0]


def mlp_bwd(pos, dm, c, u, g, fc1, fc2, chips):
    tokens, width = c.shape
    parts, _, block = fc1.shape
    ff = parts * block
    rows1, rows2 = width // chips // 2, ff // chips // 2 // parts
    cols = lambda n: pl.BlockSpec((n, block), lambda i, _: (0, i))
    by_part = pl.BlockSpec((1, chips, rows1, block), lambda i, _: (i, 0, 0, 0))
    by_chip = pl.BlockSpec((parts, 1, rows2, width), lambda i, _: (0, i, 0, 0))
    grad1 = jax.ShapeDtypeStruct((parts, chips, rows1, block), bf16)
    grad2 = jax.ShapeDtypeStruct((parts, chips, rows2, width), bf16)
    return pl.pallas_call(
        functools.partial(mlp_bwd_kernel, chips=chips),
        grid_spec=pltpu.PrefetchScalarGridSpec(
            num_scalar_prefetch=1,
            grid=(parts,),
            in_specs=[whole(dm.shape), whole(c.shape), cols(tokens), cols(tokens),
                      pl.BlockSpec((1, width, block), lambda i, _: (i, 0, 0)),
                      pl.BlockSpec((block, width), lambda i, _: (i, 0))],
            out_specs=[whole(c.shape), cols(1), by_part, by_part, by_chip, by_chip],
        ),
        out_shape=[jax.ShapeDtypeStruct((tokens, width), f32), jax.ShapeDtypeStruct((1, ff), f32),
                   grad1, grad1, grad2, grad2],
        compiler_params=params(),
        cost_estimate=cost(8 * tokens * width * ff, tokens * ff * 4 + width * ff * 8 + tokens * width * 8),
        name="mlp_bwd",
    )(pos, dm, c, u, g, fc1, fc2)


def qkvo_grad_kernel(pos_ref, a_ref, d_ref, o_ref, dattn_ref, keep_ref, send_ref, *, chips):
    part = pl.program_id(0)
    core = pos_ref[2]

    @pl.when(part < 3)
    def _():
        split_rows(dot(a_ref[...], d_ref[0], 0, 0), core, keep_ref.at[0], send_ref.at[0], chips)

    @pl.when(part == 3)
    def _():
        split_rows(dot(o_ref[...], dattn_ref[...], 0, 0), core, keep_ref.at[0], send_ref.at[0], chips)


def qkvo_grad(pos, a, dqkv, o, dattn, chips):
    tokens, width = a.shape
    each = width // chips // 2
    out = pl.BlockSpec((1, chips, each, width), lambda i, _: (i, 0, 0, 0))
    shape = jax.ShapeDtypeStruct((4, chips, each, width), bf16)
    return pl.pallas_call(
        functools.partial(qkvo_grad_kernel, chips=chips),
        grid_spec=pltpu.PrefetchScalarGridSpec(
            num_scalar_prefetch=1,
            grid=(4,),
            in_specs=[whole(a.shape), pl.BlockSpec((1, tokens, width), lambda i, _: (jnp.minimum(i, 2), 0, 0)),
                      whole(a.shape), whole(a.shape)],
            out_specs=[out, out],
        ),
        out_shape=[shape, shape],
        compiler_params=params(),
        cost_estimate=cost(8 * tokens * width * width, tokens * width * 12 + width * width * 8),
        name="qkvo_grad",
    )(pos, a, dqkv, o, dattn)


def patch_grad_kernel(ext_ref, demb_ref, small_ref, out_ref):
    shares, spare, width = small_ref.shape
    grad = dot(ext_ref[...], demb_ref[...], 0, 0).astype(bf16)
    each = grad.shape[0] // shares
    out_ref[:, :each, :] = grad.reshape(shares, each, width)
    out_ref[:, each:, :] = small_ref[...]


def patch_grad(ext, demb, small):
    tokens, depth = ext.shape
    shares, spare, width = small.shape
    steps = 4
    per = shares // steps
    each = depth // shares
    return pl.pallas_call(
        patch_grad_kernel,
        grid=(steps,),
        in_specs=[pl.BlockSpec((tokens, depth // steps), lambda i: (0, i)), whole(demb.shape),
                  pl.BlockSpec((per, spare, width), lambda i: (i, 0, 0))],
        out_specs=pl.BlockSpec((per, each + spare, width), lambda i: (i, 0, 0)),
        out_shape=jax.ShapeDtypeStruct((shares, each + spare, width), bf16),
        compiler_params=params(),
        cost_estimate=cost(2 * tokens * depth * width, ext.size * 2 + demb.size * 2 + depth * width * 2),
        name="patch_grad",
    )(ext, demb, small)


def pixel_grad_kernel(d_ref, w_ref, shown_ref, out_ref):
    out_ref[...] = dot(d_ref[...], stacked(w_ref, out_ref.shape[1]), 1, 1) * shown_ref[...]


def pixel_back(dmasked, patch, shown, depth):
    own, width = dmasked.shape
    tb = token_block(own)
    return pl.pallas_call(
        pixel_grad_kernel,
        grid=(own // tb,),
        in_specs=[rows(tb, width), whole(patch.shape), rows(tb, 1)],
        out_specs=rows(tb, depth),
        out_shape=jax.ShapeDtypeStruct((own, depth), f32),
        compiler_params=params(),
        cost_estimate=cost(2 * own * depth * width, own * depth * 4 + depth * width * 2),
        name="pixel_back",
    )(dmasked, patch, shown)


def place_kernel(pos_ref, *refs, kinds, groups):
    count = len(kinds)
    per = count + 3 * len(groups)
    outs = refs[2 * per :]
    z, g, core = pos_ref[0], pos_ref[1], pos_ref[2]

    def put(m, share, part, row, value):
        if kinds[m] == "wide":
            each = outs[m].shape[1] // 8
            outs[m][part, pl.ds(pl.multiple_of(share * each + row, 16), value.shape[0]), :] = value
        else:
            each = outs[m].shape[0] // 32
            start = (share * 4 + part) * each + row
            outs[m][pl.ds(pl.multiple_of(start, 16), value.shape[0]), :] = value

    for rel in range(2):
        cc = core ^ rel
        mine = refs[rel * per : (rel + 1) * per]
        for m in range(count):
            each = mine[m].shape[0] if kinds[m] == "wide" else mine[m].shape[0] // 4
            width = outs[m].shape[-1]
            for part in range(4):
                value = mine[m][:, part * width : (part + 1) * width] if kinds[m] == "wide" else mine[m][part * each : (part + 1) * each, :]
                put(m, z * 2 + cc, part, 0, value)
        for i, (m, row, height, first) in enumerate(groups):
            got, near, far = mine[count + 3 * i : count + 3 * i + 3]
            for k in range(3):
                share = ((z - k - 1) & 3) * 2 + cc
                for ref, base, turn in ((got, 0, 0), (near, 0, first), (far, 0, 3 ^ first), (far, 3, 3)):
                    put(m, share, g ^ turn, row, ref[base + k])


def place(pos, pieces, others, kinds, groups, shapes):
    args = (*pieces, *others)
    return pl.pallas_call(
        functools.partial(place_kernel, kinds=kinds, groups=groups),
        grid_spec=pltpu.PrefetchScalarGridSpec(
            num_scalar_prefetch=1,
            grid=(1,),
            in_specs=[whole(p.shape) for p in args],
            out_specs=[whole(s) for s in shapes],
        ),
        out_shape=[jax.ShapeDtypeStruct(s, bf16) for s in shapes],
        compiler_params=params(),
        cost_estimate=cost(0, 4 * sum(np.prod(s) for s in shapes)),
        name="place",
    )(pos, *args)


def norm_back(dnormed, hidden, gain):
    xhat, rstd = norm_parts(hidden)
    dxhat = dnormed * gain
    mean_d = jnp.mean(dxhat, axis=-1, keepdims=True)
    mean_dx = jnp.mean(dxhat * xhat, axis=-1, keepdims=True)
    grad = rstd * (dxhat - mean_d - xhat * mean_dx)
    return grad, jnp.sum(dnormed * xhat, axis=0, keepdims=True), jnp.sum(dnormed, axis=0, keepdims=True)


def sum_rows(step, ref, part):
    @pl.when(step == 0)
    def _():
        ref[...] = part

    @pl.when(step > 0)
    def _():
        ref[...] += part


def norm2_back_kernel(dc_ref, h1_ref, dh2_ref, gain_ref, w_ref, dh1_ref, da_ref, do_ref, gg_ref, gs_ref):
    step = pl.program_id(0)
    grad, ggain, gshift = norm_back(dc_ref[...], h1_ref[...], gain_ref[...])
    dh1 = dh2_ref[...] + grad
    dh1_ref[...] = dh1
    dattn = dh1.astype(bf16)
    da_ref[...] = dattn
    do_ref[...] = dot(dattn, w_ref[0], 1, 1).astype(bf16)
    sum_rows(step, gg_ref, ggain)
    sum_rows(step, gs_ref, gshift)


def norm2_back(dc, h1, dh2, gain, proj_w):
    tokens, width = dc.shape
    tb = token_block(tokens)
    blk = rows(tb, width)
    vec = whole((1, width))
    return pl.pallas_call(
        norm2_back_kernel,
        grid=(tokens // tb,),
        in_specs=[blk, blk, blk, vec, last_part(width)],
        out_specs=[blk, blk, blk, vec, vec],
        out_shape=[jax.ShapeDtypeStruct((tokens, width), f32), jax.ShapeDtypeStruct((tokens, width), bf16),
                   jax.ShapeDtypeStruct((tokens, width), bf16),
                   jax.ShapeDtypeStruct((1, width), f32), jax.ShapeDtypeStruct((1, width), f32)],
        compiler_params=params(),
        cost_estimate=cost(2 * tokens * width * width, tokens * width * 20 + width * width * 2),
        name="norm2_back",
    )(dc, h1, dh2, gain, proj_w)


def norm1_back_kernel(d_ref, w_ref, h0_ref, dh1_ref, gain_ref, de_ref, gg_ref, gs_ref):
    step = pl.program_id(0)
    da = dot(d_ref[0], w_ref[0], 1, 1) + dot(d_ref[1], w_ref[1], 1, 1) + dot(d_ref[2], w_ref[2], 1, 1)
    grad, ggain, gshift = norm_back(da, h0_ref[...], gain_ref[...])
    de_ref[...] = (dh1_ref[...] + grad).astype(bf16)
    sum_rows(step, gg_ref, ggain)
    sum_rows(step, gs_ref, gshift)


def norm1_back(dqkv, qkv_w, h0, dh1, gain):
    _, tokens, width = dqkv.shape
    tb = token_block(tokens)
    blk = rows(tb, width)
    vec = whole((1, width))
    return pl.pallas_call(
        norm1_back_kernel,
        grid=(tokens // tb,),
        in_specs=[pl.BlockSpec((3, tb, width), lambda i: (0, i, 0)), whole((3, width, width)), blk, blk, vec],
        out_specs=[blk, vec, vec],
        out_shape=[jax.ShapeDtypeStruct((tokens, width), bf16),
                   jax.ShapeDtypeStruct((1, width), f32), jax.ShapeDtypeStruct((1, width), f32)],
        compiler_params=params(),
        cost_estimate=cost(6 * tokens * width * width, tokens * width * 16 + width * width * 6),
        name="norm1_back",
    )(dqkv, qkv_w, h0, dh1, gain)


def part_slices(side):
    low, own, high = slice(0, MARGIN), slice(MARGIN, MARGIN + side), slice(MARGIN + side, 2 * MARGIN + side)
    return [(own, own), (own, low), (own, high), (low, own), (high, own),
            (low, low), (low, high), (high, low), (high, high)]


@functools.lru_cache(None)
def token_places(dates, side):
    extent = side + 2 * MARGIN
    grid = np.stack(np.meshgrid(np.arange(dates), np.arange(extent), np.arange(extent), indexing="ij"), -1)
    return np.concatenate([grid[:, r, c].reshape(-1, 3) for r, c in part_slices(side)])


@functools.lru_cache(None)
def halo_tables(dates, side):
    places = token_places(dates, side)
    extent = side + 2 * MARGIN
    own = dates * side * side
    edge = dates * side * MARGIN
    index = {tuple(p): i for i, p in enumerate(places)}

    def table(wanted, count):
        out = np.zeros((len(wanted), count), np.float32)
        out[np.arange(len(wanted)), [index[w] for w in wanted]] = 1
        return out

    def shifted(part, dr, dc):
        r, c = part_slices(side)[part]
        grid = np.stack(np.meshgrid(np.arange(dates), np.arange(extent)[r], np.arange(extent)[c], indexing="ij"), -1)
        return [(d, y + dr, x + dc) for d, y, x in grid.reshape(-1, 3)]

    first = table(shifted(1, 0, side) + shifted(2, 0, -side), own)
    north = shifted(3, side, 0) + shifted(5, side, 0) + shifted(6, side, 0)
    south = shifted(4, -side, 0) + shifted(7, -side, 0) + shifted(8, -side, 0)
    second = table(north + south, own + 2 * edge)
    return first, second


def chain(axis, step):
    count = lax.axis_size(axis)
    return [(i, i + step) for i in range(count) if 0 <= i + step < count]


def pick(table, values):
    return lax.dot(jnp.asarray(table, bf16), values, preferred_element_type=f32)


def give_margin(own, dates, side):
    first, second = halo_tables(dates, side)
    edge = dates * side * MARGIN
    corner = dates * MARGIN * MARGIN
    sent = pick(first, own).astype(bf16)
    left = lax.ppermute(sent[:edge], "gx", chain("gx", 1))
    right = lax.ppermute(sent[edge:], "gx", chain("gx", -1))
    middle = jnp.concatenate([own, left, right])
    sent = pick(second, middle).astype(bf16)
    upper = lax.ppermute(sent[: edge + 2 * corner], "gy", chain("gy", 1))
    lower = lax.ppermute(sent[edge + 2 * corner :], "gy", chain("gy", -1))
    return jnp.concatenate([middle, upper[:edge], lower[:edge], upper[edge:], lower[edge:]])


def take_margin(every, dates, side):
    first, second = halo_tables(dates, side)
    own = dates * side * side
    edge = dates * side * MARGIN
    corner = dates * MARGIN * MARGIN
    after = own + 2 * edge
    upper = jnp.concatenate([every[after : after + edge], every[after + 2 * edge : after + 2 * edge + 2 * corner]])
    lower = jnp.concatenate([every[after + edge : after + 2 * edge], every[after + 2 * edge + 2 * corner :]])
    below = lax.ppermute(upper, "gy", chain("gy", -1))
    above = lax.ppermute(lower, "gy", chain("gy", 1))
    middle = every[:after].astype(f32) + pick(second.T, jnp.concatenate([below, above]))
    sides = middle[own:].astype(bf16)
    east = lax.ppermute(sides[:edge], "gx", chain("gx", -1))
    west = lax.ppermute(sides[edge:], "gx", chain("gx", 1))
    return middle[:own] + pick(first.T, jnp.concatenate([east, west]))


def sincos(places, span_width):
    half_width = span_width // 2
    omega = 1.0 / 10000.0 ** (jnp.arange(half_width, dtype=f32) / half_width)
    angles = places[:, None] * omega[None, :]
    return jnp.concatenate([jnp.sin(angles), jnp.cos(angles)], axis=1)


def position_parts(tile_row, tile_col, stamps, side, width):
    side_width = width // 16 * 6
    time_width = width - 2 * side_width
    extent = side + 2 * MARGIN
    dates = stamps.shape[0]
    offsets = jnp.arange(extent, dtype=jnp.int32) - MARGIN
    table = jnp.concatenate([
        jnp.pad(sincos(stamps.astype(f32), time_width), ((0, 0), (0, 2 * side_width))),
        jnp.pad(sincos((tile_row * side + offsets).astype(f32), side_width), ((0, 0), (time_width, side_width))),
        jnp.pad(sincos((tile_col * side + offsets).astype(f32), side_width), ((0, 0), (time_width + side_width, 0))),
    ])
    places = token_places(dates, side)
    hot = np.zeros((len(places), dates + 2 * extent), np.float32)
    spots = np.arange(len(places))
    hot[spots, places[:, 0]] = 1
    hot[spots, dates + places[:, 1]] = 1
    hot[spots, dates + extent + places[:, 2]] = 1
    hot = np.concatenate([hot] * 3, axis=1)
    spare = -hot.shape[1] % 128
    hot = np.pad(hot, ((0, 0), (0, spare)))
    parts = jnp.concatenate(three_parts(table))
    return jnp.asarray(hot, bf16), jnp.pad(parts, ((0, spare), (0, 0)))


def dense(left, right, ca=1, cb=0):
    return lax.dot_general(left, right, (((ca,), (cb,)), ((), ())), preferred_element_type=f32)


def gather(shard):
    return lax.all_gather(shard, "gx", axis=0, tiled=True)


def swap(value, axis, bit):
    return lax.ppermute(value, axis, [(i, i ^ bit) for i in range(lax.axis_size(axis))])


def turn(value, step):
    count = lax.axis_size("gx")
    return lax.ppermute(value, "gx", [(i, (i + 2 * step) % count) for i in range(count)])


def after(value, *earlier):
    return lax.optimization_barrier((value, *earlier))[0]


def along_z(mine):
    return jnp.stack([turn(mine, k) for k in (1, 2, 3)])


def along_gy(got, first):
    near = swap(got, "gy", first)
    far = swap(jnp.concatenate([got, near]), "gy", 3 ^ first)
    return got, near, far


def core_swap(pieces):
    return tuple(swap(p, "gx", 1) for p in pieces)


def added(*values):
    return sum(v.astype(f32) for v in values).astype(bf16)


def at(value, index, axis=0):
    return lax.dynamic_index_in_dim(value, index, axis, keepdims=False)


def folded_gy(value):
    return value.reshape(2, 2, *value.shape[1:])


def near_sum(keep, got, first, g):
    keep, got = folded_gy(keep), folded_gy(got)
    dim, b = (1, g & 1) if first == 1 else (0, g >> 1)
    return added(at(keep, 1 - b, dim), at(got, 1 - b, dim)), added(at(keep, b, dim), at(got, b, dim))


def far_sum(keep, got, first, g):
    b = (g >> 1) if first == 1 else (g & 1)
    return added(at(keep, 1 - b), at(got, 1 - b)), (at(keep, b), at(got, b))


def along_z_sum(mine, z):
    came = [turn(at(mine, (z + k) % 4), k) for k in (1, 2, 3)]
    return at(mine, z), came


def four_parts(mine, first, g):
    pair = jnp.stack([mine, swap(mine, "gy", first)])
    every = jnp.concatenate([pair, swap(pair, "gy", 3 ^ first)])
    place_of = lambda rel: rel if first == 1 else (rel >> 1) | ((rel & 1) << 1)
    return [at(every, place_of(p ^ g)).astype(f32) for p in range(4)]


def gather_last(dec_w, head_w):
    rows_each, width = head_w.shape
    slabs = head_w.reshape(rows_each, -1, dec_w.shape[1]).transpose(1, 0, 2).reshape(-1, dec_w.shape[1])
    return lax.all_gather(jnp.concatenate([dec_w, slabs]), "gx", axis=0, tiled=False)


def gather_pieces(qkv_w, proj_w, fc1_w, fc2_w, ready):
    each, width = proj_w.shape
    half = each // 2
    row = lax.axis_index("gy")
    share_a = jnp.concatenate([qkv_w, proj_w], axis=1)
    got_a = along_z(lax.dynamic_slice_in_dim(share_a, row * width, width, axis=1))
    pieces_a = (share_a, *along_gy(got_a[:, :half], 1), *along_gy(got_a[:, half:], 2))
    mine_b = jnp.concatenate([lax.dynamic_slice_in_dim(fc1_w, row * width, width, axis=1),
                              lax.dynamic_slice_in_dim(fc2_w, row * each, each, axis=0)])
    got_b = along_z(after(mine_b, got_a, ready))
    pieces_b = (fc1_w, fc2_w, *along_gy(got_b[:, :each], 1), *along_gy(got_b[:, each:], 2))
    return (pieces_a, core_swap(pieces_a)), (pieces_b, core_swap(pieces_b))


def place_a(pos, pieces, others, ready):
    each = pieces[0].shape[0]
    half, width = each // 2, pieces[1].shape[-1]
    others = lax.optimization_barrier((*others, ready))[:-1]
    return place(pos, pieces, others, ("wide",), ((0, 0, half, 1), (0, half, half, 2)), [(4, width, width)])[0]


def place_b(pos, pieces, others, ready):
    each, width = pieces[0].shape[0], pieces[2].shape[-1]
    others = lax.optimization_barrier((*others, ready))[:-1]
    return place(pos, pieces, others, ("wide", "tall"), ((0, 0, each, 1), (1, 0, each, 2)),
                 [(4, width, width), (4 * width, width)])


def collect_all(keep, send, tall):
    both = jnp.stack([keep, send], axis=2)
    parts, chips, _, rows_each, width = both.shape
    if tall:
        grad = both.transpose(1, 2, 0, 3, 4).reshape(-1, width)
    else:
        grad = both.transpose(1, 2, 3, 0, 4).reshape(-1, parts * width)
    grad = lax.psum(scatter(grad), "gy").astype(f32)
    return jnp.split(grad, parts, axis=0 if tall else 1)


def over_gy(part):
    if lax.axis_size("gy") != 4:
        return lax.psum(part, "gy")
    part = added(part, swap(part, "gy", 1))
    return added(part, swap(part, "gy", 2))


def scatter(grad):
    return lax.psum_scatter(grad.astype(bf16), "gx", scatter_dimension=0, tiled=True)


def on_device(pixels, pad_mask, timestamps, scene_dates, scene_map, blend_weight, cotangent, patch_w, norm1_gain,
              norm1_bias, qkv_w, proj_w, norm2_gain, norm2_bias, fc1_w, fc1_b, fc2_w, dec_w, head_w):
    dates, side, _, pixel_width = pixels.shape
    own = dates * side * side
    extent = side + 2 * MARGIN
    places = token_places(dates, side)
    tokens = len(places)
    model_width = patch_w.shape[1]
    scale = float(model_width // HEADS) ** (-0.5)
    tile_row = lax.axis_index("gy")
    tile_col = lax.axis_index("gx")
    split = lax.axis_size("gx") == 8 and lax.axis_size("gy") == 4
    chip, core = (tile_col >> 1, tile_col & 1) if split else (0, 0)
    pos = jnp.stack([jnp.int32(chip), tile_row, jnp.int32(core)]).astype(jnp.int32)

    vectors = jnp.concatenate([norm1_gain, norm1_bias, norm2_gain, norm2_bias, fc1_b])
    each, spare = norm1_gain.shape[0], model_width - vectors.shape[0]
    vectors = jnp.broadcast_to(jnp.pad(vectors, (0, spare))[None, :], (8, model_width))
    masked = (pixels * pad_mask.astype(bf16)[..., None]).reshape(own, pixel_width)
    ext = give_margin(masked, dates, side)

    nearby = lax.dynamic_slice(jnp.pad(scene_map, 1, constant_values=-1), (tile_row, tile_col), (3, 3))
    own_scene = nearby[1, 1]
    bands = np.array([0] * MARGIN + [1] * side + [2] * MARGIN)
    same = (nearby == own_scene)[bands][:, bands].astype(f32)
    weight = blend_weight.astype(f32) * same
    own_dates = scene_dates[own_scene]
    stamps = timestamps[own_scene]
    date_ok = jnp.arange(dates, dtype=jnp.int32) < own_dates
    spot_hot = np.zeros((tokens, extent * extent), np.float32)
    spot_hot[np.arange(tokens), places[:, 1] * extent + places[:, 2]] = 1
    per_token = pick(spot_hot, jnp.stack([weight.reshape(-1), same.reshape(-1)], axis=1).astype(bf16))
    weight_tok = per_token[:, :1]
    seen = per_token[:, 1:] * (jnp.asarray(places[:, :1], jnp.int32) < own_dates).astype(f32)
    lane = np.arange(128)[None, :]
    kx = jnp.where(lane < 3, 1.0, jnp.where(lane == 3, (1.0 - seen) * -1e9, 0.0)).astype(bf16)
    shown = pad_mask.reshape(own, 1).astype(f32)
    valid = (pad_mask.astype(f32) * date_ok.astype(f32)[:, None, None]).reshape(own, 1)

    full_patch = lax.all_gather(jnp.concatenate([patch_w, vectors]), "gx", axis=0, tiled=False)
    if split:
        pieces_a, pieces_b = gather_pieces(qkv_w, proj_w, fc1_w, fc2_w, ext)
    else:
        parts_of = lambda m: m.reshape(model_width, 4, model_width).transpose(1, 0, 2)
        full_a = parts_of(jnp.concatenate([gather(qkv_w), gather(proj_w)], axis=1))
        full_fc1, full_fc2 = parts_of(gather(fc1_w)), gather(fc2_w)
    dec_rows, dec_width = dec_w.shape
    head_rows, slabs = head_w.shape[0], pixel_width // dec_width
    tops = gather_last(dec_w, after(head_w, full_patch))
    full_dec = tops[:, :dec_rows].reshape(-1, dec_width)
    full_head = tops[:, dec_rows:].reshape(-1, slabs, head_rows, dec_width).transpose(0, 2, 1, 3).reshape(-1, pixel_width)

    hot, table = position_parts(tile_row, tile_col, stamps, side, model_width)
    small = full_patch[:, patch_w.shape[0], :].astype(f32)
    gain1, shift1, gain2, shift2 = (small[:, i * each : (i + 1) * each].reshape(1, -1) for i in range(4))
    full_b = small[:, 4 * each : 4 * each + fc1_b.shape[0]].reshape(1, -1)

    h0, a = embed(ext, full_patch, hot, table, gain1, shift1)
    if split:
        full_a = place_a(pos, *pieces_a, a)
    qkv = project(a, full_a, 3)
    weight_tok = after(weight_tok, qkv)
    denom = take_margin(weight_tok.astype(bf16), dates, side)
    ratio = valid / denom
    gr = (cotangent.reshape(own, pixel_width).astype(f32) * ratio).astype(bf16)
    o, qx = attn_fwd(qkv, kx, scale)
    h1, c = proj_norm(o, full_a, h0, gain2, shift2)
    if split:
        full_fc1, full_fc2 = place_b(pos, *pieces_b, c)
    gz = dense(after(gr, c), full_head, 1, 1).astype(bf16)
    dz_every = give_margin(gz, dates, side)
    u, slope, h2r = mlp_fwd(c, full_fc1, full_b, full_fc2, h1)
    z = dense(h2r, full_dec).astype(bf16)
    folded = take_margin((z.astype(f32) * weight_tok).astype(bf16), dates, side).astype(bf16)
    recon = (dense(folded, full_head) * ratio).astype(bf16)

    grad_head = dense(folded, gr, 0, 0)
    dz = (dz_every.astype(f32) * weight_tok).astype(bf16)
    grad_dec = dense(h2r, dz, 0, 0)
    dh2 = dense(dz, full_dec, 1, 1)
    dm = dh2.astype(bf16)
    dc, grad_fc1_b, keep1, send1, keep2, send2 = mlp_bwd(pos, dm, c, u, slope, full_fc1, full_fc2, 4)
    g = tile_row
    if split:
        got1, got2 = swap(send1, "gx", 1), swap(send2, "gx", 1)
    dh1, dattn, do, grad_gain2, grad_shift2 = norm2_back(dc, h1, dh2, gain2, full_a)
    if split:
        got1, got2 = after(got1, do), after(got2, do)
        out1, keep1 = near_sum(keep1, got1, 1, g)
        out2, keep2 = near_sum(keep2, got2, 2, g)
        do, out1, out2 = lax.optimization_barrier((do, out1, out2))
        got1, got2 = swap(out1, "gy", 1), swap(out2, "gy", 2)
    dqkv = attn_bwd(qkv, do, o, qx, kx, scale)
    if split:
        got1, got2 = after(got1, dqkv), after(got2, dqkv)
        out1, keep1 = far_sum(keep1, got1, 1, g)
        out2, keep2 = far_sum(keep2, got2, 2, g)
        dqkv, out1, out2 = lax.optimization_barrier((dqkv, out1, out2))
        got1, got2 = swap(out1, "gy", 2), swap(out2, "gy", 1)
    keep3, send3 = qkvo_grad(pos, a, dqkv, o, dattn, 4)
    if split:
        got3 = swap(send3, "gx", 1)
        got1, got2 = after(got1, keep3), after(got2, keep3)
        mine1, came1 = along_z_sum(added(*keep1, got1), chip)
        mine2, came2 = along_z_sum(added(*keep2, got2), chip)
        got3 = after(got3, mine1, mine2)
        half = keep3.shape[2] // 2
        out3, keep3a = near_sum(keep3[:, :, :half], got3[:, :, :half], 1, g)
        out4, keep3b = near_sum(keep3[:, :, half:], got3[:, :, half:], 2, g)
        dqkv, out3, out4 = lax.optimization_barrier((dqkv, out3, out4))
        got3, got4 = swap(out3, "gy", 1), swap(out4, "gy", 2)
    demb, grad_gain1, grad_shift1 = norm1_back(dqkv, full_a, h0, dh1, gain1)
    if split:
        got3, got4 = after(got3, demb), after(got4, demb)
        out3, keep3a = far_sum(keep3a, got3, 1, g)
        out4, keep3b = far_sum(keep3b, got4, 2, g)
        demb, out3, out4 = lax.optimization_barrier((demb, out3, out4))
        got3, got4 = swap(out3, "gy", 2), swap(out4, "gy", 1)
    shares = lax.axis_size("gx")
    small = jnp.concatenate([v.reshape(shares, -1) for v in (grad_gain1, grad_shift1, grad_gain2, grad_shift2, grad_fc1_b)],
                            axis=1).astype(bf16)
    small = jnp.pad(small, ((0, 0), (0, spare)))
    grad_patch = patch_grad(ext, demb, jnp.broadcast_to(small[:, None, :], (shares, 8, model_width)))
    part_patch = lax.psum_scatter(grad_patch, "gx", scatter_dimension=0, tiled=False)
    if split:
        got3, got4 = after(got3, grad_patch), after(got4, grad_patch)
        mine3, came3 = along_z_sum(jnp.concatenate([added(*keep3a, got3), added(*keep3b, got4)], axis=1), chip)
        demb = after(demb, mine3)
        came1, came2 = [after(v, mine3) for v in came1], [after(v, mine3) for v in came2]
        sum1 = four_parts(added(mine1, *came1), 1, g)
        sum2 = four_parts(added(mine2, *came2), 2, g)
    dmasked = take_margin(demb, dates, side).astype(bf16)
    pixel_grad = pixel_back(dmasked, full_patch, shown, pixel_width)
    grad_head, grad_dec = scatter(grad_head), scatter(grad_dec)
    ends = over_gy(jnp.concatenate([grad_dec, grad_head.reshape(-1, dec_width)]))
    if split:
        came3 = [after(v, pixel_grad) for v in came3]
        sum3 = four_parts(added(mine3, *came3), 1, g)
    else:
        sum1, sum2, sum3 = collect_all(keep1, send1, False), collect_all(keep2, send2, True), collect_all(keep3, send3, False)
    last = over_gy(part_patch).astype(f32)
    small = last[patch_w.shape[0]]
    return (
        recon.reshape(pixels.shape),
        pixel_grad.reshape(pixels.shape),
        last[: patch_w.shape[0]],
        small[:each],
        small[each : 2 * each],
        jnp.concatenate(sum3[:3], axis=1),
        sum3[3],
        small[2 * each : 3 * each],
        small[3 * each : 4 * each],
        jnp.concatenate(sum1, axis=1),
        small[4 * each : 4 * each + fc1_b.shape[0]],
        jnp.concatenate(sum2, axis=0),
        ends[:dec_rows].astype(f32),
        ends[dec_rows:].reshape(head_rows, pixel_width).astype(f32),
    )


def solution(mesh):
    in_specs = (
        P(None, "gy", "gx", None),
        P(None, "gy", "gx"),
        P(),
        P(),
        P(),
        P("gy", "gx"),
        P(None, "gy", "gx", None),
        P("gx", None),
        P("gx"),
        P("gx"),
        P("gx", None),
        P("gx", None),
        P("gx"),
        P("gx"),
        P("gx", None),
        P("gx"),
        P("gx", None),
        P("gx", None),
        P("gx", None),
    )
    out_specs = (
        P(None, "gy", "gx", None),
        P(None, "gy", "gx", None),
        P("gx", None),
        P("gx"),
        P("gx"),
        P("gx", None),
        P("gx", None),
        P("gx"),
        P("gx"),
        P("gx", None),
        P("gx"),
        P("gx", None),
        P("gx", None),
        P("gx", None),
    )
    return jax.shard_map(
        on_device, mesh=mesh, in_specs=in_specs, out_specs=out_specs, check_vma=False
    )
```

```python
import functools
import jax
import jax.numpy as jnp
import numpy as np
from jax import lax
from jax.experimental import pallas as pl
from jax.experimental.pallas import tpu as pltpu
from jax.sharding import PartitionSpec as P

HEADS = 12
MARGIN = 2
norm_eps = 1e-06
VMEM_BYTES = 56 * 1024 * 1024
f32, bf16 = jnp.float32, jnp.bfloat16


def params():
    return pltpu.CompilerParams(vmem_limit_bytes=VMEM_BYTES)


def cost(flops, nbytes):
    return pl.CostEstimate(flops=int(flops), bytes_accessed=int(nbytes), transcendentals=0)


def dot(a, b, ca=1, cb=0):
    return lax.dot_general(a, b, (((ca,), (cb,)), ((), ())), preferred_element_type=f32)


def whole(shape):
    return pl.BlockSpec(shape, lambda *_: (0,) * len(shape))


def rows(block, width):
    return pl.BlockSpec((block, width), lambda i: (i, 0))


def columns_part(gathered, width, index):
    shares, each, _ = gathered.shape
    return pl.BlockSpec((shares, each, width), lambda i: (0, 0, index(i)))


def last_part(gathered, width):
    return columns_part(gathered, width, lambda i: 3)


def patch_part(gathered, depth):
    shares, _, width = gathered.shape
    return pl.BlockSpec((shares, depth // shares, width), lambda i: (0, 0, 0))


def square(ref):
    return ref[...].reshape(-1, ref.shape[-1])


def norm_parts(hidden):
    center = jnp.mean(hidden, axis=-1, keepdims=True)
    centered = hidden - center
    spread = jnp.mean(centered * centered, axis=-1, keepdims=True)
    rstd = lax.rsqrt(spread + norm_eps)
    return centered * rstd, rstd


def token_block(tokens):
    for parts in (3, 2):
        if tokens % (16 * parts) == 0:
            return tokens // parts
    return tokens


def embed_kernel(own_ref, left_ref, right_ref, upper_ref, lower_ref, w_ref, pick_ref, table_ref, vec_ref, ext_ref, h0_ref, a_ref, *, pieces):
    refs = (own_ref, left_ref, right_ref, upper_ref, lower_ref)
    for step, held in enumerate(pieces):
        @pl.when(pl.program_id(0) == step)
        def _(held=held):
            spot = 0
            for i, start, count in held:
                ext_ref[spot : spot + count, :] = refs[i][start : start + count, :]
                spot += count
    hidden = dot(ext_ref[...], square(w_ref)) + dot(pick_ref[...], table_ref[...])
    h0_ref[...] = hidden
    xhat, _ = norm_parts(hidden)
    a_ref[...] = (xhat * vec_ref[0:1, :] + vec_ref[1:2, :]).astype(bf16)


def embed(strips, gathered, pick, table, vec):
    tokens = pick.shape[0]
    depth = strips[0].shape[1]
    width = gathered.shape[2]
    tb = token_block(tokens)
    sizes = [strips[0].shape[0]] + [s.shape[0] - 16 for s in strips[1:]]
    pieces, room = [[]], tb
    for i, size in enumerate(sizes):
        start = 0
        while start < size:
            if room == 0:
                pieces.append([])
                room = tb
            count = min(size - start, room)
            pieces[-1].append((i, start, count))
            start, room = start + count, room - count
    return pl.pallas_call(
        functools.partial(embed_kernel, pieces=pieces),
        grid=(tokens // tb,),
        in_specs=[whole(s.shape) for s in strips] + [patch_part(gathered, depth), rows(tb, pick.shape[1]),
                  whole(table.shape), whole(vec.shape)],
        out_specs=[rows(tb, depth), rows(tb, width), rows(tb, width)],
        out_shape=[jax.ShapeDtypeStruct((tokens, depth), bf16), jax.ShapeDtypeStruct((tokens, width), f32),
                   jax.ShapeDtypeStruct((tokens, width), bf16)],
        compiler_params=params(),
        cost_estimate=cost(2 * tokens * depth * width, tokens * depth * 4 + depth * width * 2 + tokens * width * 6),
        name="embed",
    )(*strips, gathered, pick, table, vec)


def columns_kernel(a_ref, w_ref, o_ref):
    o_ref[...] = dot(a_ref[...], square(w_ref)).astype(o_ref.dtype)


def project(a, gathered, count):
    tokens, width = a.shape
    half = width // 2
    return pl.pallas_call(
        columns_kernel,
        grid=(2 * count,),
        in_specs=[whole(a.shape), columns_part(gathered, half, lambda i: i)],
        out_specs=pl.BlockSpec((tokens, half), lambda i: (0, i)),
        out_shape=jax.ShapeDtypeStruct((tokens, count * width), bf16),
        compiler_params=params(),
        cost_estimate=cost(2 * tokens * width * width * count, a.size * 2 + width * width * count * 2 + tokens * width * count * 2),
        name="project",
    )(a, gathered)


def three_parts(value):
    first = value.astype(bf16)
    rest = value - first.astype(f32)
    second = rest.astype(bf16)
    third = (rest - second.astype(f32)).astype(bf16)
    return first, second, third


def in_lanes(parts, lane, tail):
    out = tail
    for spot, part in reversed(list(enumerate(parts))):
        out = jnp.where(lane == spot, part.astype(f32), out)
    return out.astype(bf16)


def attn_fwd_kernel(q_ref, k_ref, v_ref, kx_ref, o_ref, qx_ref, *, block, scale):
    tokens, pair = q_ref.shape
    half = pair // 2
    k_aug = jnp.concatenate([k_ref[...], kx_ref[...]], axis=1)
    v_aug = jnp.concatenate([v_ref[...], jnp.ones((tokens, pair), bf16)], axis=1)
    lane = lax.broadcasted_iota(jnp.int32, (block, pair), 1)
    for start in range(0, tokens, block):
        q_blk = q_ref[start : start + block, :].astype(f32) * scale
        outs = []
        for j in range(2):
            mine = (lane >= half) if j else (lane < half)
            q_aug = jnp.concatenate(
                [jnp.where(mine, q_blk, 0.0).astype(bf16),
                 jnp.where(lane == 3, 1.0, 0.0).astype(bf16)], axis=1)
            s = dot(q_aug, k_aug, 1, 1)
            top = jnp.max(s, axis=1, keepdims=True)
            p = jnp.exp(s - top).astype(bf16)
            mixed = dot(p, v_aug)
            total = mixed[:, pair:]
            outs.append(mixed[:, :pair] / total)
            lse = jnp.log(total) + top
            qx_ref[j, start : start + block, :] = in_lanes(
                three_parts(-lse), lane, jnp.where(lane == 3, 1.0, 0.0))
        o_ref[start : start + block, :] = jnp.where(lane < half, outs[0], outs[1]).astype(bf16)


def attn_fwd(qkv, kx, scale):
    tokens = qkv.shape[0]
    width = qkv.shape[1] // 3
    pairs = HEADS // 2
    pw = width // pairs
    spec = lambda part: pl.BlockSpec((tokens, pw), lambda h, part=part: (0, part * pairs + h))
    return pl.pallas_call(
        functools.partial(attn_fwd_kernel, block=token_block(tokens), scale=scale),
        grid=(pairs,),
        in_specs=[spec(0), spec(1), spec(2), whole(kx.shape)],
        out_specs=[pl.BlockSpec((tokens, pw), lambda h: (0, h)),
                   pl.BlockSpec((2, tokens, pw), lambda h: (h, 0, 0))],
        out_shape=[jax.ShapeDtypeStruct((tokens, width), bf16),
                   jax.ShapeDtypeStruct((HEADS, tokens, pw), bf16)],
        compiler_params=params(),
        cost_estimate=cost(2 * 4 * HEADS * tokens * tokens * 256, qkv.size * 2 + tokens * width * 2),
        name="attn_fwd",
    )(qkv, qkv, qkv, kx)


def attn_bwd_kernel(q_ref, k_ref, v_ref, do_ref, o_ref, qx_ref, kx_ref, d_ref, *, block, scale):
    tokens, pair = q_ref.shape
    half = pair // 2
    lane = lax.broadcasted_iota(jnp.int32, (tokens, pair), 1)
    q_all = q_ref[...].astype(f32) * scale
    do_all = do_ref[...].astype(f32)
    prod = do_all * o_ref[...].astype(f32)
    kx = kx_ref[...]
    dq = [None, None]
    dk = [None] * (tokens // block)
    dv = [None] * (tokens // block)
    for j in range(2):
        mine = (lane >= half) if j else (lane < half)
        q_j = jnp.where(mine, q_all, 0.0).astype(bf16)
        do_j = jnp.where(mine, do_all, 0.0).astype(bf16)
        delta = jnp.sum(jnp.where(mine, prod, 0.0), axis=1, keepdims=True)
        dox = in_lanes(three_parts(-delta), lane, jnp.zeros_like(prod))
        q_aug = jnp.concatenate([q_j, qx_ref[j]], axis=1)
        do_aug = jnp.concatenate([do_j, dox], axis=1)
        for b in range(tokens // block):
            at = slice(b * block, (b + 1) * block)
            k_blk = k_ref[at, :]
            sT = dot(jnp.concatenate([k_blk, kx[at]], axis=1), q_aug, 1, 1)
            pT = jnp.exp(sT)
            dpT = dot(jnp.concatenate([v_ref[at, :], kx[at]], axis=1), do_aug, 1, 1)
            dsT = (pT * dpT).astype(bf16)
            dv_b = dot(pT.astype(bf16), do_j)
            dk_b = dot(dsT, q_j)
            dq_b = dot(dsT, k_blk, 0, 0)
            dv[b] = dv_b if dv[b] is None else dv[b] + dv_b
            dk[b] = dk_b if dk[b] is None else dk[b] + dk_b
            dq[j] = dq_b if dq[j] is None else dq[j] + dq_b
    for b in range(tokens // block):
        at = slice(b * block, (b + 1) * block)
        d_ref[1, at, :] = dk[b].astype(bf16)
        d_ref[2, at, :] = dv[b].astype(bf16)
    d_ref[0] = (jnp.where(lane < half, dq[0], dq[1]) * scale).astype(bf16)


def attn_bwd(qkv, do, o, qx, kx, scale):
    tokens = qkv.shape[0]
    width = qkv.shape[1] // 3
    pairs = HEADS // 2
    pw = width // pairs
    spec = lambda part: pl.BlockSpec((tokens, pw), lambda h, part=part: (0, part * pairs + h))
    one = pl.BlockSpec((tokens, pw), lambda h: (0, h))
    return pl.pallas_call(
        functools.partial(attn_bwd_kernel, block=token_block(tokens), scale=scale),
        grid=(pairs,),
        in_specs=[spec(0), spec(1), spec(2), one, one,
                  pl.BlockSpec((2, tokens, pw), lambda h: (h, 0, 0)), whole(kx.shape)],
        out_specs=pl.BlockSpec((3, tokens, pw), lambda h: (0, 0, h)),
        out_shape=jax.ShapeDtypeStruct((3, tokens, width), bf16),
        compiler_params=params(),
        cost_estimate=cost(2 * 5 * HEADS * tokens * tokens * 256, qkv.size * 2 + tokens * width * 10),
        name="attn_bwd",
    )(qkv, qkv, qkv, do, o, qx, kx)


def proj_kernel(o_ref, w_ref, h0_ref, vec_ref, h1_ref, c_ref):
    hidden = h0_ref[...] + dot(o_ref[...], square(w_ref))
    h1_ref[...] = hidden
    xhat, _ = norm_parts(hidden)
    c_ref[...] = (xhat * vec_ref[2:3, :] + vec_ref[3:4, :]).astype(bf16)


def proj_norm(o, proj_w, h0, vec):
    tokens, width = o.shape
    tb = token_block(tokens)
    return pl.pallas_call(
        proj_kernel,
        grid=(tokens // tb,),
        in_specs=[rows(tb, width), last_part(proj_w, width), rows(tb, width), whole(vec.shape)],
        out_specs=[rows(tb, width), rows(tb, width)],
        out_shape=[jax.ShapeDtypeStruct((tokens, width), f32),
                   jax.ShapeDtypeStruct((tokens, width), bf16)],
        compiler_params=params(),
        cost_estimate=cost(2 * tokens * width * width, tokens * width * 12 + width * width * 2),
        name="proj_norm",
    )(o, proj_w, h0, vec)


def mlp_weight_specs(gathered, width):
    shares, parts, _, _ = gathered.shape
    each = width // shares
    return [pl.BlockSpec((shares, 1, each, width), lambda i, *_: (0, i, 0, 0)),
            pl.BlockSpec((shares // parts, parts, each, width), lambda i, *_: (i, 0, 1, 0))]


def mlp_fwd_kernel(c_ref, fc1_ref, b_ref, fc2_ref, h1_ref, u_ref, g_ref, h2_ref, acc_ref):
    step = pl.program_id(0)
    pre = dot(c_ref[...], square(fc1_ref)) + b_ref[...]
    cdf = 0.5 * (1.0 + lax.erf(pre * np.float32(0.5 ** 0.5)))
    act = (pre * cdf).astype(bf16)
    u_ref[...] = act
    g_ref[...] = (cdf + pre * jnp.exp(-0.5 * pre * pre) * np.float32((2 * np.pi) ** -0.5)).astype(bf16)
    part = dot(act, square(fc2_ref))

    @pl.when(step == 0)
    def _():
        acc_ref[...] = h1_ref[...] + part

    @pl.when(step > 0)
    def _():
        acc_ref[...] += part

    @pl.when(step == pl.num_programs(0) - 1)
    def _():
        h2_ref[...] = acc_ref[...].astype(bf16)


def mlp_fwd(c, gathered, bias, h1):
    tokens, width = c.shape
    parts, block = gathered.shape[1], width
    ff = parts * block
    fc1_spec, fc2_spec = mlp_weight_specs(gathered, width)
    cols = lambda n: pl.BlockSpec((n, block), lambda i: (0, i))
    return pl.pallas_call(
        mlp_fwd_kernel,
        grid=(ff // block,),
        in_specs=[whole(c.shape), fc1_spec, cols(1), fc2_spec, whole(h1.shape)],
        out_specs=[cols(tokens), cols(tokens), whole(c.shape)],
        out_shape=[jax.ShapeDtypeStruct((tokens, ff), bf16), jax.ShapeDtypeStruct((tokens, ff), bf16),
                   jax.ShapeDtypeStruct((tokens, width), bf16)],
        scratch_shapes=[pltpu.VMEM((tokens, width), f32)],
        compiler_params=params(),
        cost_estimate=cost(4 * tokens * width * ff, tokens * ff * 4 + width * ff * 4 + tokens * width * 8),
        name="mlp_fwd",
    )(c, gathered, bias, gathered, h1)


def split_rows(value, core, keep_ref, send_ref, chips):
    width = value.shape[1]
    value = value.astype(bf16).reshape(chips, 2, value.shape[0] // chips // 2, width)
    even, odd = value[:, 0], value[:, 1]

    @pl.when(core == 0)
    def _():
        keep_ref[...] = even
        send_ref[...] = odd

    @pl.when(core == 1)
    def _():
        keep_ref[...] = odd
        send_ref[...] = even


def mlp_bwd_kernel(pos_ref, dm_ref, c_ref, u_ref, g_ref, fc1_ref, fc2_ref, dc_ref, gb_ref, k1_ref, s1_ref, k2_ref, s2_ref, *, chips):
    step = pl.program_id(0)
    core = pos_ref[2]
    dm = dm_ref[...]
    df32 = dot(dm, square(fc2_ref), 1, 1) * g_ref[...].astype(f32)
    df = df32.astype(bf16)
    gb_ref[...] = jnp.sum(df.astype(f32), axis=0, keepdims=True)
    parts, rows_each = k2_ref.shape[0], k2_ref.shape[2]
    width = dm.shape[1]
    grad2 = dot(u_ref[...], dm, 0, 0).astype(bf16).reshape(2, parts, rows_each, width)
    split_two(grad2, core, k2_ref, s2_ref)
    split_rows(dot(c_ref[...], df, 0, 0), core, k1_ref.at[0], s1_ref.at[0], chips)
    part = dot(df, square(fc1_ref), 1, 1)

    @pl.when(step == 0)
    def _():
        dc_ref[...] = part

    @pl.when(step > 0)
    def _():
        dc_ref[...] += part


def split_two(pair, core, keep_ref, send_ref):
    @pl.when(core == 0)
    def _():
        keep_ref[:, 0] = pair[0]
        send_ref[:, 0] = pair[1]

    @pl.when(core == 1)
    def _():
        keep_ref[:, 0] = pair[1]
        send_ref[:, 0] = pair[0]


def mlp_bwd(pos, dm, c, u, g, gathered, chips):
    tokens, width = c.shape
    parts, block = gathered.shape[1], width
    ff = parts * block
    rows1, rows2 = width // chips // 2, ff // chips // 2 // parts
    cols = lambda n: pl.BlockSpec((n, block), lambda i, _: (0, i))
    by_part = pl.BlockSpec((1, chips, rows1, block), lambda i, _: (i, 0, 0, 0))
    by_chip = pl.BlockSpec((parts, 1, rows2, width), lambda i, _: (0, i, 0, 0))
    grad1 = jax.ShapeDtypeStruct((parts, chips, rows1, block), bf16)
    grad2 = jax.ShapeDtypeStruct((parts, chips, rows2, width), bf16)
    return pl.pallas_call(
        functools.partial(mlp_bwd_kernel, chips=chips),
        grid_spec=pltpu.PrefetchScalarGridSpec(
            num_scalar_prefetch=1,
            grid=(parts,),
            in_specs=[whole(dm.shape), whole(c.shape), cols(tokens), cols(tokens), *mlp_weight_specs(gathered, width)],
            out_specs=[whole(c.shape), cols(1), by_part, by_part, by_chip, by_chip],
        ),
        out_shape=[jax.ShapeDtypeStruct((tokens, width), f32), jax.ShapeDtypeStruct((1, ff), f32),
                   grad1, grad1, grad2, grad2],
        compiler_params=params(),
        cost_estimate=cost(8 * tokens * width * ff, tokens * ff * 4 + width * ff * 8 + tokens * width * 8),
        name="mlp_bwd",
    )(pos, dm, c, u, g, gathered, gathered)


def qkvo_grad_kernel(pos_ref, a_ref, d_ref, o_ref, dattn_ref, keep_ref, send_ref, *, chips):
    part = pl.program_id(0)
    core = pos_ref[2]

    @pl.when(part < 3)
    def _():
        split_rows(dot(a_ref[...], d_ref[0], 0, 0), core, keep_ref.at[0], send_ref.at[0], chips)

    @pl.when(part == 3)
    def _():
        split_rows(dot(o_ref[...], dattn_ref[...], 0, 0), core, keep_ref.at[0], send_ref.at[0], chips)


def qkvo_grad(pos, a, dqkv, o, dattn, chips):
    tokens, width = a.shape
    each = width // chips // 2
    out = pl.BlockSpec((1, chips, each, width), lambda i, _: (i, 0, 0, 0))
    shape = jax.ShapeDtypeStruct((4, chips, each, width), bf16)
    return pl.pallas_call(
        functools.partial(qkvo_grad_kernel, chips=chips),
        grid_spec=pltpu.PrefetchScalarGridSpec(
            num_scalar_prefetch=1,
            grid=(4,),
            in_specs=[whole(a.shape), pl.BlockSpec((1, tokens, width), lambda i, _: (jnp.minimum(i, 2), 0, 0)),
                      whole(a.shape), whole(a.shape)],
            out_specs=[out, out],
        ),
        out_shape=[shape, shape],
        compiler_params=params(),
        cost_estimate=cost(8 * tokens * width * width, tokens * width * 12 + width * width * 8),
        name="qkvo_grad",
    )(pos, a, dqkv, o, dattn)


def patch_grad_kernel(pos_ref, ext_ref, demb_ref, bias_ref, *refs):
    core = pos_ref[2]
    *vector_refs, keep_ref, send_ref = refs
    parts, _, each, width = keep_ref.shape
    grad = dot(ext_ref[...], demb_ref[...], 0, 0).astype(bf16)
    depth = grad.shape[0] // 2 // parts
    spare = each - depth
    grad = grad.reshape(2, parts, depth, width)
    small = [ref[...] for ref in vector_refs]
    small += [bias_ref[:, i * width : (i + 1) * width] for i in range(bias_ref.shape[1] // width)]
    row = lax.broadcasted_iota(jnp.int32, (spare, width), 0)
    block = jnp.zeros((spare, width), f32)
    for i, value in enumerate(small):
        block = jnp.where(row == i, value, block)
    block = block.astype(bf16)

    def put(ref, value):
        ref[:, 0, :depth, :] = value
        for part in range(parts):
            ref[part, 0, depth:, :] = block

    @pl.when(core == 0)
    def _():
        put(keep_ref, grad[0])
        put(send_ref, grad[1])

    @pl.when(core == 1)
    def _():
        put(keep_ref, grad[1])
        put(send_ref, grad[0])


def patch_grad(pos, ext, demb, bias, vectors, parts, chips):
    tokens, depth = ext.shape
    width = demb.shape[1]
    each = depth // (2 * chips) // parts + 16
    out = pl.BlockSpec((parts, 1, each, width), lambda i, _: (0, i, 0, 0))
    shape = jax.ShapeDtypeStruct((parts, chips, each, width), bf16)
    return pl.pallas_call(
        patch_grad_kernel,
        grid_spec=pltpu.PrefetchScalarGridSpec(
            num_scalar_prefetch=1,
            grid=(chips,),
            in_specs=[pl.BlockSpec((tokens, depth // chips), lambda i, _: (0, i)), whole(demb.shape), whole(bias.shape)]
            + [whole(v.shape) for v in vectors],
            out_specs=[out, out],
        ),
        out_shape=[shape, shape],
        compiler_params=params(),
        cost_estimate=cost(2 * tokens * depth * width, ext.size * 2 + demb.size * 2 + depth * width * 2),
        name="patch_grad",
    )(pos, ext, demb, bias, *vectors)


def pixel_grad_kernel(d_ref, w_ref, shown_ref, out_ref):
    out_ref[...] = dot(d_ref[...], square(w_ref), 1, 1) * shown_ref[...]


def pixel_back(dmasked, patch, shown, depth):
    own, width = dmasked.shape
    tb = token_block(own)
    return pl.pallas_call(
        pixel_grad_kernel,
        grid=(own // tb,),
        in_specs=[rows(tb, width), patch_part(patch, depth), rows(tb, 1)],
        out_specs=rows(tb, depth),
        out_shape=jax.ShapeDtypeStruct((own, depth), f32),
        compiler_params=params(),
        cost_estimate=cost(2 * own * depth * width, own * depth * 4 + depth * width * 2),
        name="pixel_back",
    )(dmasked, patch, shown)


def place_kernel(pos_ref, *refs):
    out_ref = refs[-1]
    z, g, core = pos_ref[0], pos_ref[1], pos_ref[2]
    width = out_ref.shape[3]
    for rel in range(2):
        cc = core ^ rel
        fc1_ref, fc2_ref, *moved = refs[rel * 6 : (rel + 1) * 6]
        each = fc1_ref.shape[0]
        for part in range(4):
            out_ref[z * 2 + cc, part, :each, :] = fc1_ref[:, part * width : (part + 1) * width]
            out_ref[z * 2 + cc, part, each:, :] = fc2_ref[part * each : (part + 1) * each, :]
        for turn in range(4):
            for k in range(3):
                out_ref[((z - k - 1) & 3) * 2 + cc, g ^ turn] = moved[turn][k]


def place(pos, pieces, others):
    args = (*pieces, *others)
    each, width = pieces[0].shape[0], pieces[1].shape[1]
    shape = (8, 4, 2 * each, width)
    return pl.pallas_call(
        place_kernel,
        grid_spec=pltpu.PrefetchScalarGridSpec(
            num_scalar_prefetch=1,
            grid=(1,),
            in_specs=[whole(p.shape) for p in args],
            out_specs=whole(shape),
        ),
        out_shape=jax.ShapeDtypeStruct(shape, bf16),
        compiler_params=params(),
        cost_estimate=cost(0, 4 * np.prod(shape)),
        name="place",
    )(pos, *args)


def norm_back(dnormed, hidden, gain):
    xhat, rstd = norm_parts(hidden)
    dxhat = dnormed * gain
    mean_d = jnp.mean(dxhat, axis=-1, keepdims=True)
    mean_dx = jnp.mean(dxhat * xhat, axis=-1, keepdims=True)
    grad = rstd * (dxhat - mean_d - xhat * mean_dx)
    return grad, jnp.sum(dnormed * xhat, axis=0, keepdims=True), jnp.sum(dnormed, axis=0, keepdims=True)


def sum_rows(step, ref, part):
    @pl.when(step == 0)
    def _():
        ref[...] = part

    @pl.when(step > 0)
    def _():
        ref[...] += part


def norm2_back_kernel(dc_ref, h1_ref, dh2_ref, gain_ref, w_ref, dh1_ref, da_ref, do_ref, gg_ref, gs_ref):
    step = pl.program_id(0)
    grad, ggain, gshift = norm_back(dc_ref[...], h1_ref[...], gain_ref[2:3, :])
    dh1 = dh2_ref[...] + grad
    dh1_ref[...] = dh1
    dattn = dh1.astype(bf16)
    da_ref[...] = dattn
    do_ref[...] = dot(dattn, square(w_ref), 1, 1).astype(bf16)
    sum_rows(step, gg_ref, ggain)
    sum_rows(step, gs_ref, gshift)


def norm2_back(dc, h1, dh2, gain, proj_w):
    tokens, width = dc.shape
    tb = token_block(tokens)
    blk = rows(tb, width)
    vec = whole((1, width))
    return pl.pallas_call(
        norm2_back_kernel,
        grid=(tokens // tb,),
        in_specs=[blk, blk, blk, whole(gain.shape), last_part(proj_w, width)],
        out_specs=[blk, blk, blk, vec, vec],
        out_shape=[jax.ShapeDtypeStruct((tokens, width), f32), jax.ShapeDtypeStruct((tokens, width), bf16),
                   jax.ShapeDtypeStruct((tokens, width), bf16),
                   jax.ShapeDtypeStruct((1, width), f32), jax.ShapeDtypeStruct((1, width), f32)],
        compiler_params=params(),
        cost_estimate=cost(2 * tokens * width * width, tokens * width * 20 + width * width * 2),
        name="norm2_back",
    )(dc, h1, dh2, gain, proj_w)


def norm1_back_kernel(d_ref, w_ref, h0_ref, dh1_ref, gain_ref, de_ref, gg_ref, gs_ref):
    step = pl.program_id(0)
    width = h0_ref.shape[1]
    da = sum(dot(d_ref[p], w_ref[:, :, p * width : (p + 1) * width].reshape(width, width), 1, 1) for p in range(3))
    grad, ggain, gshift = norm_back(da, h0_ref[...], gain_ref[0:1, :])
    de_ref[...] = (dh1_ref[...] + grad).astype(bf16)
    sum_rows(step, gg_ref, ggain)
    sum_rows(step, gs_ref, gshift)


def norm1_back(dqkv, qkv_w, h0, dh1, gain):
    tokens, width = h0.shape
    tb = token_block(tokens)
    blk = rows(tb, width)
    vec = whole((1, width))
    return pl.pallas_call(
        norm1_back_kernel,
        grid=(tokens // tb,),
        in_specs=[pl.BlockSpec((3, tb, width), lambda i: (0, i, 0)), columns_part(qkv_w, 3 * width, lambda i: 0), blk, blk, whole(gain.shape)],
        out_specs=[blk, vec, vec],
        out_shape=[jax.ShapeDtypeStruct((tokens, width), bf16),
                   jax.ShapeDtypeStruct((1, width), f32), jax.ShapeDtypeStruct((1, width), f32)],
        compiler_params=params(),
        cost_estimate=cost(6 * tokens * width * width, tokens * width * 16 + width * width * 6),
        name="norm1_back",
    )(dqkv, qkv_w, h0, dh1, gain)


def part_slices(side):
    low, own, high = slice(0, MARGIN), slice(MARGIN, MARGIN + side), slice(MARGIN + side, 2 * MARGIN + side)
    return [(own, own), (own, low), (own, high), (low, own), (low, low), (low, high),
            (high, own), (high, low), (high, high)]


@functools.lru_cache(None)
def token_places(dates, side):
    extent = side + 2 * MARGIN
    grid = np.stack(np.meshgrid(np.arange(dates), np.arange(extent), np.arange(extent), indexing="ij"), -1)
    return np.concatenate([grid[:, r, c].reshape(-1, 3) for r, c in part_slices(side)])


@functools.lru_cache(None)
def halo_tables(dates, side):
    places = token_places(dates, side)
    extent = side + 2 * MARGIN
    own = dates * side * side
    edge = dates * side * MARGIN
    index = {tuple(p): i for i, p in enumerate(places)}

    def table(wanted, count):
        out = np.zeros((len(wanted), count), np.float32)
        out[np.arange(len(wanted)), [index[w] for w in wanted]] = 1
        return out

    def shifted(part, dr, dc):
        r, c = part_slices(side)[part]
        grid = np.stack(np.meshgrid(np.arange(dates), np.arange(extent)[r], np.arange(extent)[c], indexing="ij"), -1)
        return [(d, y + dr, x + dc) for d, y, x in grid.reshape(-1, 3)]

    first = table(shifted(1, 0, side) + shifted(2, 0, -side), own)
    north = shifted(3, side, 0) + shifted(4, side, 0) + shifted(5, side, 0)
    south = shifted(6, -side, 0) + shifted(7, -side, 0) + shifted(8, -side, 0)
    second = table(north + south, own + 2 * edge)
    return first, second


def chain(axis, step):
    count = lax.axis_size(axis)
    return [(i, i + step) for i in range(count) if 0 <= i + step < count]


def pick(table, values):
    return lax.dot(jnp.asarray(table, bf16), values, preferred_element_type=f32)


def to_neighbours(low, high, axis):
    return lax.ppermute(low, axis, chain(axis, -1)), lax.ppermute(high, axis, chain(axis, 1))


def margin_first(own, dates, side):
    first, _ = halo_tables(dates, side)
    edge = dates * side * MARGIN
    sent = pick(first, own).astype(bf16)
    return sent[edge:], sent[:edge]


def margin_second(own, right, left, dates, side):
    _, second = halo_tables(dates, side)
    both = dates * side * MARGIN + 2 * dates * MARGIN * MARGIN
    middle = jnp.concatenate([own, left, right])
    sent = pick(second, middle).astype(bf16)
    return middle, sent[both:], sent[:both]


def give_margin_and_sum(own, dates, side, weight, *ready):
    first, second = halo_tables(dates, side)
    edge = dates * side * MARGIN
    corner = dates * MARGIN * MARGIN
    width = own.shape[1]

    def with_rows(strip, values):
        values = values.reshape(1, -1).astype(bf16)
        return jnp.concatenate([strip, jnp.pad(values, ((0, 15), (0, width - values.shape[1])))])

    def values_of(strip, *shape):
        return strip[-16, : np.prod(shape)].reshape(shape).astype(f32)

    sent = pick(first, own).astype(bf16)
    right, left = to_neighbours(with_rows(sent[edge:], weight[:, :MARGIN]), with_rows(sent[:edge], weight[:, -MARGIN:]), "gx")
    right, left, *_ = tied(right, left, *ready)
    extent = side + 2 * MARGIN
    total = weight[:, MARGIN:-MARGIN]
    total = total + jnp.pad(values_of(left, extent, MARGIN), ((0, 0), (0, side - MARGIN)))
    total = total + jnp.pad(values_of(right, extent, MARGIN), ((0, 0), (side - MARGIN, 0)))
    middle = jnp.concatenate([own, left[:edge], right[:edge]])
    sent = pick(second, middle).astype(bf16)
    lower, upper = to_neighbours(with_rows(sent[edge + 2 * corner :], total[:MARGIN]),
                                 with_rows(sent[: edge + 2 * corner], total[-MARGIN:]), "gy")
    total = total[MARGIN:-MARGIN]
    total = total + jnp.pad(values_of(upper, MARGIN, side), ((0, side - MARGIN), (0, 0)))
    total = total + jnp.pad(values_of(lower, MARGIN, side), ((side - MARGIN, 0), (0, 0)))
    return (own, left, right, upper, lower), total


def fold_first(every, dates, side):
    edge = dates * side * MARGIN
    middle = dates * side * side + 2 * edge
    both = edge + 2 * dates * MARGIN * MARGIN
    return every[middle : middle + both], every[middle + both :]


def fold_second(every, below, above, dates, side):
    _, second = halo_tables(dates, side)
    own = dates * side * side
    edge = dates * side * MARGIN
    middle = every[: own + 2 * edge].astype(f32) + pick(second.T, jnp.concatenate([below, above]))
    sides = middle[own:].astype(bf16)
    return middle[:own], sides[:edge], sides[edge:]


def fold_third(part, east, west, dates, side):
    first, _ = halo_tables(dates, side)
    return (part + pick(first.T, jnp.concatenate([east, west]))).astype(bf16)


def sincos(places, span_width):
    half_width = span_width // 2
    omega = 1.0 / 10000.0 ** (jnp.arange(half_width, dtype=f32) / half_width)
    angles = places[:, None] * omega[None, :]
    return jnp.concatenate([jnp.sin(angles), jnp.cos(angles)], axis=1)


def position_parts(tile_row, tile_col, stamps, side, width):
    side_width = width // 16 * 6
    time_width = width - 2 * side_width
    extent = side + 2 * MARGIN
    dates = stamps.shape[0]
    offsets = jnp.arange(extent, dtype=jnp.int32) - MARGIN
    table = jnp.concatenate([
        jnp.pad(sincos(stamps.astype(f32), time_width), ((0, 0), (0, 2 * side_width))),
        jnp.pad(sincos((tile_row * side + offsets).astype(f32), side_width), ((0, 0), (time_width, side_width))),
        jnp.pad(sincos((tile_col * side + offsets).astype(f32), side_width), ((0, 0), (time_width + side_width, 0))),
    ])
    places = token_places(dates, side)
    hot = np.zeros((len(places), dates + 2 * extent), np.float32)
    spots = np.arange(len(places))
    hot[spots, places[:, 0]] = 1
    hot[spots, dates + places[:, 1]] = 1
    hot[spots, dates + extent + places[:, 2]] = 1
    hot = np.concatenate([hot] * 3, axis=1)
    spare = -hot.shape[1] % 128
    hot = np.pad(hot, ((0, 0), (0, spare)))
    parts = jnp.concatenate(three_parts(table))
    return jnp.asarray(hot, bf16), jnp.pad(parts, ((0, spare), (0, 0)))


def dense(left, right, ca=1, cb=0):
    return lax.dot_general(left, right, (((ca,), (cb,)), ((), ())), preferred_element_type=f32)


def gather(shard):
    return lax.all_gather(shard, "gx", axis=0, tiled=True)


def swap(value, axis, bit):
    return lax.ppermute(value, axis, [(i, i ^ bit) for i in range(lax.axis_size(axis))])


def turn(value, step):
    count = lax.axis_size("gx")
    return lax.ppermute(value, "gx", [(i, (i + 2 * step) % count) for i in range(count)])


def after(value, *earlier):
    return lax.optimization_barrier((value, *earlier))[0]


def along_z(mine):
    return jnp.stack([turn(mine, k) for k in (1, 2, 3)])


def tied(*values):
    return lax.optimization_barrier(values)


def along_gy(got):
    return got, swap(got, "gy", 1), swap(got, "gy", 2), swap(got, "gy", 3)


def core_swap(pieces):
    return tuple(swap(p, "gx", 1) for p in pieces)


def added(*values):
    return sum(v.astype(f32) for v in values).astype(bf16)


def at(value, index, axis=0):
    return lax.dynamic_index_in_dim(value, index, axis, keepdims=False)


def folded_gy(value):
    return value.reshape(2, 2, *value.shape[1:])


def near_sum(keep, got, first, g):
    keep, got = folded_gy(keep), folded_gy(got)
    dim, b = (1, g & 1) if first == 1 else (0, g >> 1)
    return added(at(keep, 1 - b, dim), at(got, 1 - b, dim)), added(at(keep, b, dim), at(got, b, dim))


def far_sum(keep, got, first, g):
    b = (g >> 1) if first == 1 else (g & 1)
    return added(at(keep, 1 - b), at(got, 1 - b)), (at(keep, b), at(got, b))


def to_each(keep, got, g):
    return [added(at(keep, g ^ m), at(got, g ^ m)) for m in (1, 2, 3)], (at(keep, g), at(got, g))


def swap_each(values):
    return [swap(v, "gy", m) for v, m in zip(values, (1, 2, 3))]


def along_z_sum(mine, z):
    came = [turn(at(mine, (z + k) % 4), k) for k in (1, 2, 3)]
    return at(mine, z), came


def side_by_side(value):
    half = value.shape[1] // 2
    return jnp.concatenate([value[:, :half], value[:, half:]], axis=2)


def stacked_again(value):
    half = value.shape[1] // 2
    return jnp.concatenate([value[:, :half], value[:, half:]])


def to_all_gy(mine):
    return [mine] + [swap(mine, "gy", m) for m in (1, 2, 3)]


def in_order(every, g):
    every = jnp.stack(every)
    return [at(every, p ^ g) for p in range(4)]


def gather_apart(shard):
    return lax.all_gather(shard, "gx", axis=0, tiled=False)


def collect_all(keep, send, tall):
    both = jnp.stack([keep, send], axis=2)
    parts, chips, _, rows_each, width = both.shape
    if tall:
        grad = both.transpose(1, 2, 0, 3, 4).reshape(-1, width)
    else:
        grad = both.transpose(1, 2, 3, 0, 4).reshape(-1, parts * width)
    grad = lax.psum(scatter(grad), "gy").astype(f32)
    return jnp.split(grad, parts, axis=0 if tall else 1)


def scatter(grad):
    return lax.psum_scatter(grad.astype(bf16), "gx", scatter_dimension=0, tiled=True)


def on_device(pixels, pad_mask, timestamps, scene_dates, scene_map, blend_weight, cotangent, patch_w, norm1_gain,
              norm1_bias, qkv_w, proj_w, norm2_gain, norm2_bias, fc1_w, fc1_b, fc2_w, dec_w, head_w):
    dates, side, _, pixel_width = pixels.shape
    own = dates * side * side
    extent = side + 2 * MARGIN
    places = token_places(dates, side)
    tokens = len(places)
    model_width = patch_w.shape[1]
    scale = float(model_width // HEADS) ** (-0.5)
    tile_row = lax.axis_index("gy")
    tile_col = lax.axis_index("gx")
    split = lax.axis_size("gx") == 8 and lax.axis_size("gy") == 4
    chip, core = (tile_col >> 1, tile_col & 1) if split else (0, 0)
    pos = jnp.stack([jnp.int32(chip), tile_row, jnp.int32(core)]).astype(jnp.int32)

    nearby = lax.dynamic_slice(jnp.pad(scene_map, 1, constant_values=-1), (tile_row, tile_col), (3, 3))
    own_scene = nearby[1, 1]
    bands = np.array([0] * MARGIN + [1] * side + [2] * MARGIN)
    same = (nearby == own_scene)[bands][:, bands].astype(f32)
    weight = blend_weight.astype(f32) * same
    masked = (pixels * pad_mask.astype(bf16)[..., None]).reshape(own, pixel_width)
    each = norm1_gain.shape[0]
    vectors = jnp.concatenate([jnp.stack([norm1_gain, norm1_bias, norm2_gain, norm2_bias]), fc1_b.reshape(-1, each)])
    vectors = jnp.pad(vectors, ((0, 16 - vectors.shape[0]), (0, model_width - each)))
    dec_rows, dec_width = dec_w.shape
    head_rows, slabs = head_w.shape[0], pixel_width // dec_width
    share_p = jnp.concatenate([patch_w, vectors])
    share_a = jnp.concatenate([qkv_w, proj_w], axis=1)
    slabs_of = head_w.reshape(head_rows, slabs, dec_width).transpose(1, 0, 2).reshape(-1, dec_width)
    share_d = jnp.concatenate([dec_w, slabs_of])
    front_p = gather_apart(share_p)
    masked, share_a = tied(masked, share_a)
    front_a = gather_apart(share_a)
    quarter = patch_w.shape[0] // 4
    if split:
        row = tile_row
        mine_b = jnp.concatenate([lax.dynamic_slice_in_dim(fc1_w, row * model_width, model_width, axis=1),
                                  lax.dynamic_slice_in_dim(fc2_w, row * each, each, axis=0)])
        got_b = along_z(mine_b)
        strips, denom = give_margin_and_sum(masked, dates, side, weight, got_b)
    else:
        strips, denom = give_margin_and_sum(masked, dates, side, weight)
    tops = gather_apart(after(share_d, *strips[1:], front_p))
    full_dec = tops[:, :dec_rows].reshape(-1, dec_width)
    full_head = tops[:, dec_rows:].reshape(-1, slabs, head_rows, dec_width).transpose(0, 2, 1, 3).reshape(-1, pixel_width)
    small = front_p[:, patch_w.shape[0] :]
    if split:
        got_b = after(got_b, *strips[1:])
        pieces_b = (fc1_w, fc2_w, *along_gy(got_b))
        strips = tied(*strips, got_b)[:-1]
    else:
        parts_of = lambda m: m.reshape(8, model_width // 8, 4, model_width).transpose(0, 2, 1, 3)
        quarters_of = lambda m: m.reshape(8, 4, -1, model_width)
        full_mlp = jnp.concatenate([parts_of(gather(fc1_w)), quarters_of(gather(fc2_w))], axis=2)
    own_dates = scene_dates[own_scene]
    stamps = timestamps[own_scene]
    date_ok = jnp.arange(dates, dtype=jnp.int32) < own_dates
    spot_hot = np.zeros((tokens, extent * extent), np.float32)
    spot_hot[np.arange(tokens), places[:, 1] * extent + places[:, 2]] = 1
    per_token = pick(spot_hot, jnp.stack([weight.reshape(-1), same.reshape(-1)], axis=1).astype(bf16))
    weight_tok = per_token[:, :1]
    seen = per_token[:, 1:] * (jnp.asarray(places[:, :1], jnp.int32) < own_dates).astype(f32)
    lane = np.arange(128)[None, :]
    kx = jnp.where(lane < 3, 1.0, jnp.where(lane == 3, (1.0 - seen) * -1e9, 0.0)).astype(bf16)
    denom = jnp.broadcast_to(denom[None], (dates, side, side)).reshape(own, 1)

    hot, table = position_parts(tile_row, tile_col, stamps, side, model_width)
    small = small[:, :8, :each].astype(f32)
    vec = small[:, :4].transpose(1, 0, 2).reshape(4, -1)
    full_b = small[:, 4:].reshape(1, -1)

    shown = pad_mask.reshape(own, 1).astype(f32)
    valid = (pad_mask.astype(f32) * date_ok.astype(f32)[:, None, None]).reshape(own, 1)
    ratio = valid / denom
    gr = (cotangent.reshape(own, pixel_width).astype(f32) * ratio).astype(bf16)
    ext, h0, a = embed(strips, front_p, hot, table, vec)
    qkv = project(a, front_a, 3)
    if split:
        qkv, *pieces_b = tied(qkv, *pieces_b)
        others_b = core_swap(pieces_b)
    o, qx = attn_fwd(qkv, kx, scale)
    if split:
        o, *others_b = tied(o, *others_b)
    h1, c = proj_norm(o, front_a, h0, vec)
    gz = dense(after(gr, c), full_head, 1, 1).astype(bf16)
    west, east = margin_first(gz, dates, side)
    c, west, east = tied(c, west, east)
    right, left = to_neighbours(west, east, "gx")
    if split:
        full_mlp = place(pos, pieces_b, (*others_b[:-1], after(others_b[-1], c)))
        full_mlp, right, left = tied(full_mlp, right, left)
    middle, north, south = margin_second(gz, right, left, dates, side)
    full_mlp, north, south = tied(full_mlp, north, south)
    lower, upper = to_neighbours(north, south, "gy")
    u, slope, h2r = mlp_fwd(c, full_mlp, full_b, h1)
    z = dense(h2r, full_dec).astype(bf16)
    every = (z.astype(f32) * weight_tok).astype(bf16)
    north, south = fold_first(every, dates, side)
    below, above = to_neighbours(north, south, "gy")

    lower, upper, north, south = tied(lower, upper, north, south)
    dz_every = jnp.concatenate([middle, upper, lower])
    dz = (dz_every.astype(f32) * weight_tok).astype(bf16)
    dh2 = dense(dz, full_dec, 1, 1)
    dm, north, south = tied(dh2.astype(bf16), north, south)
    dc, grad_fc1_b, keep1, send1, keep2, send2 = mlp_bwd(pos, dm, c, u, slope, full_mlp, 4)
    g = tile_row
    if split:
        got1, got2 = swap(send1, "gx", 1), swap(send2, "gx", 1)
    below, above, dc = tied(below, above, dc)
    folded, west, east = fold_second(every, below, above, dates, side)
    grad_dec = dense(h2r, dz, 0, 0)
    dc, west, east, grad_dec = tied(dc, west, east, grad_dec)
    right, left = to_neighbours(west, east, "gx")
    dh1, dattn, do, grad_gain2, grad_shift2 = norm2_back(dc, h1, dh2, vec, front_a)
    if split:
        got1, got2 = after(got1, do), after(got2, do)
        out1, keep1 = near_sum(keep1, got1, 1, g)
        out2, keep2 = near_sum(keep2, got2, 2, g)
        do, out1, out2 = tied(do, out1, out2)
        got1, got2 = swap(out1, "gy", 1), swap(out2, "gy", 2)
    right, left, do = tied(right, left, do)
    folded = fold_third(folded, right, left, dates, side)
    grad_head = dense(folded, gr, 0, 0)
    do, grad_head, grad_dec = tied(do, grad_head.astype(bf16), grad_dec)
    grad_head, grad_dec = scatter(grad_head), scatter(grad_dec)
    dqkv = attn_bwd(qkv, do, o, qx, kx, scale)
    if split:
        got1, got2 = after(got1, dqkv), after(got2, dqkv)
        out1, keep1 = far_sum(keep1, got1, 1, g)
        out2, keep2 = far_sum(keep2, got2, 2, g)
        dqkv, out1, out2 = tied(dqkv, out1, out2)
        got1, got2 = swap(out1, "gy", 2), swap(out2, "gy", 1)
    keep3, send3 = qkvo_grad(pos, a, dqkv, o, dattn, 4)
    ends = jnp.concatenate([after(grad_dec, keep3), after(grad_head, keep3).reshape(-1, dec_width)])
    if split:
        got3 = swap(send3, "gx", 1)
        got1, got2 = after(got1, keep3), after(got2, keep3)
        mine1, came1 = along_z_sum(jnp.concatenate([added(*keep1, got1), added(*keep2, got2)], axis=1), chip)
        dqkv, mine1, ends = tied(dqkv, mine1, ends)
        ends_near = swap(ends, "gy", 1)
    demb, grad_gain1, grad_shift1 = norm1_back(dqkv, front_a, h0, dh1, vec)
    vectors = (grad_gain1, grad_shift1, grad_gain2, grad_shift2)
    north, south = fold_first(demb, dates, side)
    if split:
        got3, ends_near = after(got3, demb), after(ends_near, demb)
        outs3, keep3 = to_each(keep3, got3, g)
        ends = added(ends, ends_near)
        demb, north, south, ends, *outs3 = tied(demb, north, south, ends, *outs3)
    below, above = to_neighbours(north, south, "gy")
    if split:
        got3 = swap_each(outs3)
        keep4, send4 = patch_grad(pos, ext, demb, grad_fc1_b, vectors, 4, 4)
        got4 = swap(send4, "gx", 1)
        below, above = after(below, keep4), after(above, keep4)
    part, west, east = fold_second(demb, below, above, dates, side)
    right, left = to_neighbours(west, east, "gx")
    if split:
        got4 = after(got4, west, east)
        outs4, keep4 = to_each(keep4, got4, g)
        came1 = [after(v, *outs4) for v in came1]
        done1 = added(mine1, *came1)
        right, left, done1, *outs4 = tied(right, left, done1, *outs4)
        got4 = swap_each(outs4)
        dmasked = fold_third(part, right, left, dates, side)
        pixel_grad = pixel_back(dmasked, front_p, shown, pixel_width)
        every1 = to_all_gy(after(done1, dmasked))
        got3 = [after(v, pixel_grad) for v in got3]
        mine3 = added(*keep3, *got3)
        got4 = [after(v, mine3) for v in got4]
        mine4, came4 = along_z_sum(jnp.concatenate([mine3, added(*keep4, *got4)], axis=1), chip)
        folded, mine4, ends = tied(folded, mine4, ends)
        ends_far = swap(ends, "gy", 2)
        recon = (dense(folded, full_head) * ratio).astype(bf16)
        came4 = [after(v, recon) for v in came4]
        done4 = added(mine4, *came4)
        every1 = tied(*every1, done4)[:-1]
        every4 = to_all_gy(done4)
        every1 = in_order(every1, g)
        sum1 = jnp.concatenate([v[:each] for v in every1], axis=1).astype(f32)
        sum2 = jnp.concatenate([v[each:] for v in every1], axis=0).astype(f32)
        ends = ends.astype(f32) + ends_far.astype(f32)
        every4 = tied(*every4, sum1, sum2, ends)[:-3]
        every4 = in_order(every4, g)
        sum1, sum2 = jnp.split(sum1, 4, axis=1), jnp.split(sum2, 4, axis=0)
        sum3 = [v[:each] for v in every4]
        grad_patch = jnp.concatenate([v[each : each + quarter] for v in every4])
        small = every4[0][each + quarter :]
    else:
        recon = (dense(folded, full_head) * ratio).astype(bf16)
        dmasked = fold_third(part, right, left, dates, side)
        sum1, sum2 = collect_all(keep1, send1, False), collect_all(keep2, send2, True)
        sum3 = collect_all(keep3, send3, False)
        pixel_grad = pixel_back(dmasked, front_p, shown, pixel_width)
        grad_patch = lax.psum(scatter(dense(ext, demb, 0, 0)), "gy")
        small = lax.psum(jnp.concatenate([*vectors, grad_fc1_b.reshape(-1, model_width)]), ("gy", "gx"))
        ends = lax.psum(ends, "gy")
    small = small.astype(f32)
    mine_of = lambda value, count: lax.dynamic_slice_in_dim(value.reshape(-1), tile_col * count, count)
    grad_bias = mine_of(small[4 : 4 + full_b.shape[1] // model_width], fc1_b.shape[0])
    return (
        recon.reshape(pixels.shape),
        pixel_grad.reshape(pixels.shape),
        grad_patch.astype(f32),
        mine_of(small[0], each),
        mine_of(small[1], each),
        jnp.concatenate(sum3[:3], axis=1).astype(f32),
        sum3[3].astype(f32),
        mine_of(small[2], each),
        mine_of(small[3], each),
        jnp.concatenate(sum1, axis=1).astype(f32),
        grad_bias,
        jnp.concatenate(sum2, axis=0).astype(f32),
        ends[:dec_rows].astype(f32),
        ends[dec_rows:].reshape(head_rows, pixel_width).astype(f32),
    )


def solution(mesh):
    in_specs = (
        P(None, "gy", "gx", None),
        P(None, "gy", "gx"),
        P(),
        P(),
        P(),
        P("gy", "gx"),
        P(None, "gy", "gx", None),
        P("gx", None),
        P("gx"),
        P("gx"),
        P("gx", None),
        P("gx", None),
        P("gx"),
        P("gx"),
        P("gx", None),
        P("gx"),
        P("gx", None),
        P("gx", None),
        P("gx", None),
    )
    out_specs = (
        P(None, "gy", "gx", None),
        P(None, "gy", "gx", None),
        P("gx", None),
        P("gx"),
        P("gx"),
        P("gx", None),
        P("gx", None),
        P("gx"),
        P("gx"),
        P("gx", None),
        P("gx"),
        P("gx", None),
        P("gx", None),
        P("gx", None),
    )
    return jax.shard_map(
        on_device, mesh=mesh, in_specs=in_specs, out_specs=out_specs, check_vma=False
    )
```

```python
import functools
import jax
import jax.numpy as jnp
import numpy as np
from jax import lax
from jax.experimental import pallas as pl
from jax.experimental.pallas import tpu as pltpu
from jax.sharding import PartitionSpec as P

HEADS = 12
MARGIN = 2
norm_eps = 1e-06
VMEM_BYTES = 56 * 1024 * 1024
f32, bf16 = jnp.float32, jnp.bfloat16


def params():
    return pltpu.CompilerParams(vmem_limit_bytes=VMEM_BYTES)


def cost(flops, nbytes):
    return pl.CostEstimate(flops=int(flops), bytes_accessed=int(nbytes), transcendentals=0)


def dot(a, b, ca=1, cb=0):
    return lax.dot_general(a, b, (((ca,), (cb,)), ((), ())), preferred_element_type=f32)


def whole(shape):
    return pl.BlockSpec(shape, lambda *_: (0,) * len(shape))


def rows(block, width):
    return pl.BlockSpec((block, width), lambda i: (i, 0))


def last_part(gathered, width):
    shares = gathered.shape[0]
    return pl.BlockSpec((shares, 1, width // shares, width), lambda i: (0, 3, 0, 0))


def patch_part(gathered, depth):
    shares, _, width = gathered.shape
    return pl.BlockSpec((shares, depth // shares, width), lambda i: (0, 0, 0))


def square(ref):
    return ref[...].reshape(-1, ref.shape[-1])


def norm_parts(hidden):
    center = jnp.mean(hidden, axis=-1, keepdims=True)
    centered = hidden - center
    spread = jnp.mean(centered * centered, axis=-1, keepdims=True)
    rstd = lax.rsqrt(spread + norm_eps)
    return centered * rstd, rstd


def token_block(tokens):
    for parts in (3, 2):
        if tokens % (16 * parts) == 0:
            return tokens // parts
    return tokens


def embed_kernel(own_ref, left_ref, right_ref, upper_ref, lower_ref, w_ref, pick_ref, table_ref, vec_ref, ext_ref, h0_ref, a_ref, *, pieces):
    refs = (own_ref, left_ref, right_ref, upper_ref, lower_ref)
    for step, held in enumerate(pieces):
        @pl.when(pl.program_id(0) == step)
        def _(held=held):
            spot = 0
            for i, start, count in held:
                ext_ref[spot : spot + count, :] = refs[i][start : start + count, :]
                spot += count
    hidden = dot(ext_ref[...], square(w_ref)) + dot(pick_ref[...], table_ref[...])
    h0_ref[...] = hidden
    xhat, _ = norm_parts(hidden)
    a_ref[...] = (xhat * vec_ref[0:1, :] + vec_ref[1:2, :]).astype(bf16)


def embed(strips, gathered, pick, table, vec):
    tokens = pick.shape[0]
    depth = strips[0].shape[1]
    width = gathered.shape[2]
    tb = token_block(tokens)
    sizes = [strips[0].shape[0]] + [s.shape[0] - 16 for s in strips[1:]]
    pieces, room = [[]], tb
    for i, size in enumerate(sizes):
        start = 0
        while start < size:
            if room == 0:
                pieces.append([])
                room = tb
            count = min(size - start, room)
            pieces[-1].append((i, start, count))
            start, room = start + count, room - count
    return pl.pallas_call(
        functools.partial(embed_kernel, pieces=pieces),
        grid=(tokens // tb,),
        in_specs=[whole(s.shape) for s in strips] + [patch_part(gathered, depth), rows(tb, pick.shape[1]),
                  whole(table.shape), whole(vec.shape)],
        out_specs=[rows(tb, depth), rows(tb, width), rows(tb, width)],
        out_shape=[jax.ShapeDtypeStruct((tokens, depth), bf16), jax.ShapeDtypeStruct((tokens, width), f32),
                   jax.ShapeDtypeStruct((tokens, width), bf16)],
        compiler_params=params(),
        cost_estimate=cost(2 * tokens * depth * width, tokens * depth * 4 + depth * width * 2 + tokens * width * 6),
        name="embed",
    )(*strips, gathered, pick, table, vec)


def columns_kernel(a_ref, w_ref, o_ref):
    o_ref[...] = dot(a_ref[...], square(w_ref)).astype(o_ref.dtype)


def project(a, gathered, count):
    tokens, width = a.shape
    half = width // 2
    return pl.pallas_call(
        columns_kernel,
        grid=(2 * count,),
        in_specs=[whole(a.shape), pl.BlockSpec((gathered.shape[0], 1, width // gathered.shape[0], half), lambda i: (0, i // 2, 0, i % 2))],
        out_specs=pl.BlockSpec((tokens, half), lambda i: (0, i)),
        out_shape=jax.ShapeDtypeStruct((tokens, count * width), bf16),
        compiler_params=params(),
        cost_estimate=cost(2 * tokens * width * width * count, a.size * 2 + width * width * count * 2 + tokens * width * count * 2),
        name="project",
    )(a, gathered)


def three_parts(value):
    first = value.astype(bf16)
    rest = value - first.astype(f32)
    second = rest.astype(bf16)
    third = (rest - second.astype(f32)).astype(bf16)
    return first, second, third


def in_lanes(parts, lane, tail):
    out = tail
    for spot, part in reversed(list(enumerate(parts))):
        out = jnp.where(lane == spot, part.astype(f32), out)
    return out.astype(bf16)


def attn_fwd_kernel(q_ref, k_ref, v_ref, kx_ref, o_ref, qx_ref, *, block, scale):
    tokens, pair = q_ref.shape
    half = pair // 2
    k_aug = jnp.concatenate([k_ref[...], kx_ref[...]], axis=1)
    v_aug = jnp.concatenate([v_ref[...], jnp.ones((tokens, pair), bf16)], axis=1)
    lane = lax.broadcasted_iota(jnp.int32, (block, pair), 1)
    for start in range(0, tokens, block):
        q_blk = q_ref[start : start + block, :].astype(f32) * scale
        outs = []
        for j in range(2):
            mine = (lane >= half) if j else (lane < half)
            q_aug = jnp.concatenate(
                [jnp.where(mine, q_blk, 0.0).astype(bf16),
                 jnp.where(lane == 3, 1.0, 0.0).astype(bf16)], axis=1)
            s = dot(q_aug, k_aug, 1, 1)
            top = jnp.max(s, axis=1, keepdims=True)
            p = jnp.exp(s - top).astype(bf16)
            mixed = dot(p, v_aug)
            total = mixed[:, pair:]
            outs.append(mixed[:, :pair] / total)
            lse = jnp.log(total) + top
            qx_ref[j, start : start + block, :] = in_lanes(
                three_parts(-lse), lane, jnp.where(lane == 3, 1.0, 0.0))
        o_ref[start : start + block, :] = jnp.where(lane < half, outs[0], outs[1]).astype(bf16)


def attn_fwd(qkv, kx, scale):
    tokens = qkv.shape[0]
    width = qkv.shape[1] // 3
    pairs = HEADS // 2
    pw = width // pairs
    spec = lambda part: pl.BlockSpec((tokens, pw), lambda h, part=part: (0, part * pairs + h))
    return pl.pallas_call(
        functools.partial(attn_fwd_kernel, block=token_block(tokens), scale=scale),
        grid=(pairs,),
        in_specs=[spec(0), spec(1), spec(2), whole(kx.shape)],
        out_specs=[pl.BlockSpec((tokens, pw), lambda h: (0, h)),
                   pl.BlockSpec((2, tokens, pw), lambda h: (h, 0, 0))],
        out_shape=[jax.ShapeDtypeStruct((tokens, width), bf16),
                   jax.ShapeDtypeStruct((HEADS, tokens, pw), bf16)],
        compiler_params=params(),
        cost_estimate=cost(2 * 4 * HEADS * tokens * tokens * 256, qkv.size * 2 + tokens * width * 2),
        name="attn_fwd",
    )(qkv, qkv, qkv, kx)


def attn_bwd_kernel(q_ref, k_ref, v_ref, do_ref, o_ref, qx_ref, kx_ref, d_ref, *, block, scale):
    tokens, pair = q_ref.shape
    half = pair // 2
    lane = lax.broadcasted_iota(jnp.int32, (tokens, pair), 1)
    q_all = q_ref[...].astype(f32) * scale
    do_all = do_ref[...].astype(f32)
    prod = do_all * o_ref[...].astype(f32)
    kx = kx_ref[...]
    dq = [None, None]
    dk = [None] * (tokens // block)
    dv = [None] * (tokens // block)
    for j in range(2):
        mine = (lane >= half) if j else (lane < half)
        q_j = jnp.where(mine, q_all, 0.0).astype(bf16)
        do_j = jnp.where(mine, do_all, 0.0).astype(bf16)
        delta = jnp.sum(jnp.where(mine, prod, 0.0), axis=1, keepdims=True)
        dox = in_lanes(three_parts(-delta), lane, jnp.zeros_like(prod))
        q_aug = jnp.concatenate([q_j, qx_ref[j]], axis=1)
        do_aug = jnp.concatenate([do_j, dox], axis=1)
        for b in range(tokens // block):
            at = slice(b * block, (b + 1) * block)
            k_blk = k_ref[at, :]
            sT = dot(jnp.concatenate([k_blk, kx[at]], axis=1), q_aug, 1, 1)
            pT = jnp.exp(sT)
            dpT = dot(jnp.concatenate([v_ref[at, :], kx[at]], axis=1), do_aug, 1, 1)
            dsT = (pT * dpT).astype(bf16)
            dv_b = dot(pT.astype(bf16), do_j)
            dk_b = dot(dsT, q_j)
            dq_b = dot(dsT, k_blk, 0, 0)
            dv[b] = dv_b if dv[b] is None else dv[b] + dv_b
            dk[b] = dk_b if dk[b] is None else dk[b] + dk_b
            dq[j] = dq_b if dq[j] is None else dq[j] + dq_b
    for b in range(tokens // block):
        at = slice(b * block, (b + 1) * block)
        d_ref[1, at, :] = dk[b].astype(bf16)
        d_ref[2, at, :] = dv[b].astype(bf16)
    d_ref[0] = (jnp.where(lane < half, dq[0], dq[1]) * scale).astype(bf16)


def attn_bwd(qkv, do, o, qx, kx, scale):
    tokens = qkv.shape[0]
    width = qkv.shape[1] // 3
    pairs = HEADS // 2
    pw = width // pairs
    spec = lambda part: pl.BlockSpec((tokens, pw), lambda h, part=part: (0, part * pairs + h))
    one = pl.BlockSpec((tokens, pw), lambda h: (0, h))
    return pl.pallas_call(
        functools.partial(attn_bwd_kernel, block=token_block(tokens), scale=scale),
        grid=(pairs,),
        in_specs=[spec(0), spec(1), spec(2), one, one,
                  pl.BlockSpec((2, tokens, pw), lambda h: (h, 0, 0)), whole(kx.shape)],
        out_specs=pl.BlockSpec((3, tokens, pw), lambda h: (0, 0, h)),
        out_shape=jax.ShapeDtypeStruct((3, tokens, width), bf16),
        compiler_params=params(),
        cost_estimate=cost(2 * 5 * HEADS * tokens * tokens * 256, qkv.size * 2 + tokens * width * 10),
        name="attn_bwd",
    )(qkv, qkv, qkv, do, o, qx, kx)


def proj_kernel(o_ref, w_ref, h0_ref, vec_ref, h1_ref, c_ref):
    hidden = h0_ref[...] + dot(o_ref[...], square(w_ref))
    h1_ref[...] = hidden
    xhat, _ = norm_parts(hidden)
    c_ref[...] = (xhat * vec_ref[2:3, :] + vec_ref[3:4, :]).astype(bf16)


def proj_norm(o, proj_w, h0, vec):
    tokens, width = o.shape
    tb = token_block(tokens)
    return pl.pallas_call(
        proj_kernel,
        grid=(tokens // tb,),
        in_specs=[rows(tb, width), last_part(proj_w, width), rows(tb, width), whole(vec.shape)],
        out_specs=[rows(tb, width), rows(tb, width)],
        out_shape=[jax.ShapeDtypeStruct((tokens, width), f32),
                   jax.ShapeDtypeStruct((tokens, width), bf16)],
        compiler_params=params(),
        cost_estimate=cost(2 * tokens * width * width, tokens * width * 12 + width * width * 2),
        name="proj_norm",
    )(o, proj_w, h0, vec)


def mlp_weight_specs(gathered, width):
    shares, parts, _, _ = gathered.shape
    each = width // shares
    return [pl.BlockSpec((shares, 1, each, width), lambda i, *_: (0, i, 0, 0)),
            pl.BlockSpec((shares // parts, parts, each, width), lambda i, *_: (i, 0, 1, 0))]


def mlp_fwd_kernel(c_ref, fc1_ref, b_ref, fc2_ref, h1_ref, u_ref, g_ref, h2_ref, acc_ref):
    step = pl.program_id(0)
    pre = dot(c_ref[...], square(fc1_ref)) + b_ref[...]
    cdf = 0.5 * (1.0 + lax.erf(pre * np.float32(0.5 ** 0.5)))
    act = (pre * cdf).astype(bf16)
    u_ref[...] = act
    g_ref[...] = (cdf + pre * jnp.exp(-0.5 * pre * pre) * np.float32((2 * np.pi) ** -0.5)).astype(bf16)
    part = dot(act, square(fc2_ref))

    @pl.when(step == 0)
    def _():
        acc_ref[...] = h1_ref[...] + part

    @pl.when(step > 0)
    def _():
        acc_ref[...] += part

    @pl.when(step == pl.num_programs(0) - 1)
    def _():
        h2_ref[...] = acc_ref[...].astype(bf16)


def mlp_fwd(c, gathered, bias, h1):
    tokens, width = c.shape
    parts, block = gathered.shape[1], width
    ff = parts * block
    fc1_spec, fc2_spec = mlp_weight_specs(gathered, width)
    cols = lambda n: pl.BlockSpec((n, block), lambda i: (0, i))
    return pl.pallas_call(
        mlp_fwd_kernel,
        grid=(ff // block,),
        in_specs=[whole(c.shape), fc1_spec, cols(1), fc2_spec, whole(h1.shape)],
        out_specs=[cols(tokens), cols(tokens), whole(c.shape)],
        out_shape=[jax.ShapeDtypeStruct((tokens, ff), bf16), jax.ShapeDtypeStruct((tokens, ff), bf16),
                   jax.ShapeDtypeStruct((tokens, width), bf16)],
        scratch_shapes=[pltpu.VMEM((tokens, width), f32)],
        compiler_params=params(),
        cost_estimate=cost(4 * tokens * width * ff, tokens * ff * 4 + width * ff * 4 + tokens * width * 8),
        name="mlp_fwd",
    )(c, gathered, bias, gathered, h1)


def split_rows(value, core, keep_ref, send_ref, chips):
    width = value.shape[1]
    value = value.astype(bf16).reshape(chips, 2, value.shape[0] // chips // 2, width)
    even, odd = value[:, 0], value[:, 1]

    @pl.when(core == 0)
    def _():
        keep_ref[...] = even
        send_ref[...] = odd

    @pl.when(core == 1)
    def _():
        keep_ref[...] = odd
        send_ref[...] = even


def mlp_bwd_kernel(pos_ref, dm_ref, c_ref, u_ref, g_ref, fc1_ref, fc2_ref, dc_ref, gb_ref, k1_ref, s1_ref, k2_ref, s2_ref, *, chips):
    step = pl.program_id(0)
    core = pos_ref[2]
    dm = dm_ref[...]
    df32 = dot(dm, square(fc2_ref), 1, 1) * g_ref[...].astype(f32)
    df = df32.astype(bf16)
    gb_ref[...] = jnp.sum(df.astype(f32), axis=0, keepdims=True)
    parts, rows_each = k2_ref.shape[0], k2_ref.shape[2]
    width = dm.shape[1]
    grad2 = dot(u_ref[...], dm, 0, 0).astype(bf16).reshape(2, parts, rows_each, width)
    split_two(grad2, core, k2_ref, s2_ref)
    split_rows(dot(c_ref[...], df, 0, 0), core, k1_ref.at[0], s1_ref.at[0], chips)
    part = dot(df, square(fc1_ref), 1, 1)

    @pl.when(step == 0)
    def _():
        dc_ref[...] = part

    @pl.when(step > 0)
    def _():
        dc_ref[...] += part


def split_two(pair, core, keep_ref, send_ref):
    @pl.when(core == 0)
    def _():
        keep_ref[:, 0] = pair[0]
        send_ref[:, 0] = pair[1]

    @pl.when(core == 1)
    def _():
        keep_ref[:, 0] = pair[1]
        send_ref[:, 0] = pair[0]


def mlp_bwd(pos, dm, c, u, g, gathered, chips):
    tokens, width = c.shape
    parts, block = gathered.shape[1], width
    ff = parts * block
    rows1, rows2 = width // chips // 2, ff // chips // 2 // parts
    cols = lambda n: pl.BlockSpec((n, block), lambda i, _: (0, i))
    by_part = pl.BlockSpec((1, chips, rows1, block), lambda i, _: (i, 0, 0, 0))
    by_chip = pl.BlockSpec((parts, 1, rows2, width), lambda i, _: (0, i, 0, 0))
    grad1 = jax.ShapeDtypeStruct((parts, chips, rows1, block), bf16)
    grad2 = jax.ShapeDtypeStruct((parts, chips, rows2, width), bf16)
    return pl.pallas_call(
        functools.partial(mlp_bwd_kernel, chips=chips),
        grid_spec=pltpu.PrefetchScalarGridSpec(
            num_scalar_prefetch=1,
            grid=(parts,),
            in_specs=[whole(dm.shape), whole(c.shape), cols(tokens), cols(tokens), *mlp_weight_specs(gathered, width)],
            out_specs=[whole(c.shape), cols(1), by_part, by_part, by_chip, by_chip],
        ),
        out_shape=[jax.ShapeDtypeStruct((tokens, width), f32), jax.ShapeDtypeStruct((1, ff), f32),
                   grad1, grad1, grad2, grad2],
        compiler_params=params(),
        cost_estimate=cost(8 * tokens * width * ff, tokens * ff * 4 + width * ff * 8 + tokens * width * 8),
        name="mlp_bwd",
    )(pos, dm, c, u, g, gathered, gathered)


def qkvo_grad_kernel(pos_ref, a_ref, d_ref, o_ref, dattn_ref, keep_ref, send_ref, *, chips):
    part = pl.program_id(0)
    core = pos_ref[2]

    @pl.when(part < 3)
    def _():
        split_rows(dot(a_ref[...], d_ref[0], 0, 0), core, keep_ref.at[0], send_ref.at[0], chips)

    @pl.when(part == 3)
    def _():
        split_rows(dot(o_ref[...], dattn_ref[...], 0, 0), core, keep_ref.at[0], send_ref.at[0], chips)


def qkvo_grad(pos, a, dqkv, o, dattn, chips):
    tokens, width = a.shape
    each = width // chips // 2
    out = pl.BlockSpec((1, chips, each, width), lambda i, _: (i, 0, 0, 0))
    shape = jax.ShapeDtypeStruct((4, chips, each, width), bf16)
    return pl.pallas_call(
        functools.partial(qkvo_grad_kernel, chips=chips),
        grid_spec=pltpu.PrefetchScalarGridSpec(
            num_scalar_prefetch=1,
            grid=(4,),
            in_specs=[whole(a.shape), pl.BlockSpec((1, tokens, width), lambda i, _: (jnp.minimum(i, 2), 0, 0)),
                      whole(a.shape), whole(a.shape)],
            out_specs=[out, out],
        ),
        out_shape=[shape, shape],
        compiler_params=params(),
        cost_estimate=cost(8 * tokens * width * width, tokens * width * 12 + width * width * 8),
        name="qkvo_grad",
    )(pos, a, dqkv, o, dattn)


def patch_grad_kernel(pos_ref, ext_ref, demb_ref, bias_ref, *refs):
    core = pos_ref[2]
    *vector_refs, keep_ref, send_ref = refs
    parts, _, each, width = keep_ref.shape
    grad = dot(ext_ref[...], demb_ref[...], 0, 0).astype(bf16)
    depth = grad.shape[0] // 2 // parts
    spare = each - depth
    grad = grad.reshape(2, parts, depth, width)
    small = [ref[...] for ref in vector_refs]
    small += [bias_ref[:, i * width : (i + 1) * width] for i in range(bias_ref.shape[1] // width)]
    row = lax.broadcasted_iota(jnp.int32, (spare, width), 0)
    block = jnp.zeros((spare, width), f32)
    for i, value in enumerate(small):
        block = jnp.where(row == i, value, block)
    block = block.astype(bf16)

    def put(ref, value):
        ref[:, 0, :depth, :] = value
        for part in range(parts):
            ref[part, 0, depth:, :] = block

    @pl.when(core == 0)
    def _():
        put(keep_ref, grad[0])
        put(send_ref, grad[1])

    @pl.when(core == 1)
    def _():
        put(keep_ref, grad[1])
        put(send_ref, grad[0])


def patch_grad(pos, ext, demb, bias, vectors, parts, chips):
    tokens, depth = ext.shape
    width = demb.shape[1]
    each = depth // (2 * chips) // parts + 16
    out = pl.BlockSpec((parts, 1, each, width), lambda i, _: (0, i, 0, 0))
    shape = jax.ShapeDtypeStruct((parts, chips, each, width), bf16)
    return pl.pallas_call(
        patch_grad_kernel,
        grid_spec=pltpu.PrefetchScalarGridSpec(
            num_scalar_prefetch=1,
            grid=(chips,),
            in_specs=[pl.BlockSpec((tokens, depth // chips), lambda i, _: (0, i)), whole(demb.shape), whole(bias.shape)]
            + [whole(v.shape) for v in vectors],
            out_specs=[out, out],
        ),
        out_shape=[shape, shape],
        compiler_params=params(),
        cost_estimate=cost(2 * tokens * depth * width, ext.size * 2 + demb.size * 2 + depth * width * 2),
        name="patch_grad",
    )(pos, ext, demb, bias, *vectors)


def pixel_grad_kernel(d_ref, w_ref, shown_ref, out_ref):
    out_ref[...] = dot(d_ref[...], square(w_ref), 1, 1) * shown_ref[...]


def pixel_back(dmasked, patch, shown, depth):
    own, width = dmasked.shape
    tb = token_block(own)
    return pl.pallas_call(
        pixel_grad_kernel,
        grid=(own // tb,),
        in_specs=[rows(tb, width), patch_part(patch, depth), rows(tb, 1)],
        out_specs=rows(tb, depth),
        out_shape=jax.ShapeDtypeStruct((own, depth), f32),
        compiler_params=params(),
        cost_estimate=cost(2 * own * depth * width, own * depth * 4 + depth * width * 2),
        name="pixel_back",
    )(dmasked, patch, shown)


def place_kernel(pos_ref, *refs, kinds):
    out_ref = refs[-1]
    z, g, core = pos_ref[0], pos_ref[1], pos_ref[2]
    width = out_ref.shape[3]
    count = len(kinds)
    each = out_ref.shape[2] // count
    for rel in range(2):
        cc = core ^ rel
        mine = refs[rel * (count + 4) : (rel + 1) * (count + 4)]
        for m, kind in enumerate(kinds):
            for part in range(4):
                if kind == "wide":
                    value = mine[m][:, part * width : (part + 1) * width]
                else:
                    value = mine[m][part * each : (part + 1) * each, :]
                out_ref[z * 2 + cc, part, m * each : (m + 1) * each, :] = value
        for turn in range(4):
            for k in range(3):
                out_ref[((z - k - 1) & 3) * 2 + cc, g ^ turn] = mine[count + turn][k]


def place(pos, pieces, others, kinds):
    args = (*pieces, *others)
    shape = (8, 4, pieces[-1].shape[1], pieces[-1].shape[2])
    return pl.pallas_call(
        functools.partial(place_kernel, kinds=kinds),
        grid_spec=pltpu.PrefetchScalarGridSpec(
            num_scalar_prefetch=1,
            grid=(1,),
            in_specs=[whole(p.shape) for p in args],
            out_specs=whole(shape),
        ),
        out_shape=jax.ShapeDtypeStruct(shape, bf16),
        compiler_params=params(),
        cost_estimate=cost(0, 4 * np.prod(shape)),
        name="place",
    )(pos, *args)


def norm_back(dnormed, hidden, gain):
    xhat, rstd = norm_parts(hidden)
    dxhat = dnormed * gain
    mean_d = jnp.mean(dxhat, axis=-1, keepdims=True)
    mean_dx = jnp.mean(dxhat * xhat, axis=-1, keepdims=True)
    grad = rstd * (dxhat - mean_d - xhat * mean_dx)
    return grad, jnp.sum(dnormed * xhat, axis=0, keepdims=True), jnp.sum(dnormed, axis=0, keepdims=True)


def sum_rows(step, ref, part):
    @pl.when(step == 0)
    def _():
        ref[...] = part

    @pl.when(step > 0)
    def _():
        ref[...] += part


def norm2_back_kernel(dc_ref, h1_ref, dh2_ref, gain_ref, w_ref, dh1_ref, da_ref, do_ref, gg_ref, gs_ref):
    step = pl.program_id(0)
    grad, ggain, gshift = norm_back(dc_ref[...], h1_ref[...], gain_ref[2:3, :])
    dh1 = dh2_ref[...] + grad
    dh1_ref[...] = dh1
    dattn = dh1.astype(bf16)
    da_ref[...] = dattn
    do_ref[...] = dot(dattn, square(w_ref), 1, 1).astype(bf16)
    sum_rows(step, gg_ref, ggain)
    sum_rows(step, gs_ref, gshift)


def norm2_back(dc, h1, dh2, gain, proj_w):
    tokens, width = dc.shape
    tb = token_block(tokens)
    blk = rows(tb, width)
    vec = whole((1, width))
    return pl.pallas_call(
        norm2_back_kernel,
        grid=(tokens // tb,),
        in_specs=[blk, blk, blk, whole(gain.shape), last_part(proj_w, width)],
        out_specs=[blk, blk, blk, vec, vec],
        out_shape=[jax.ShapeDtypeStruct((tokens, width), f32), jax.ShapeDtypeStruct((tokens, width), bf16),
                   jax.ShapeDtypeStruct((tokens, width), bf16),
                   jax.ShapeDtypeStruct((1, width), f32), jax.ShapeDtypeStruct((1, width), f32)],
        compiler_params=params(),
        cost_estimate=cost(2 * tokens * width * width, tokens * width * 20 + width * width * 2),
        name="norm2_back",
    )(dc, h1, dh2, gain, proj_w)


def norm1_back_kernel(d_ref, w_ref, h0_ref, dh1_ref, gain_ref, de_ref, gg_ref, gs_ref):
    step = pl.program_id(0)
    width = h0_ref.shape[1]
    da = sum(dot(d_ref[p], w_ref[:, p].reshape(width, width), 1, 1) for p in range(3))
    grad, ggain, gshift = norm_back(da, h0_ref[...], gain_ref[0:1, :])
    de_ref[...] = (dh1_ref[...] + grad).astype(bf16)
    sum_rows(step, gg_ref, ggain)
    sum_rows(step, gs_ref, gshift)


def norm1_back(dqkv, qkv_w, h0, dh1, gain):
    tokens, width = h0.shape
    tb = token_block(tokens)
    blk = rows(tb, width)
    vec = whole((1, width))
    return pl.pallas_call(
        norm1_back_kernel,
        grid=(tokens // tb,),
        in_specs=[pl.BlockSpec((3, tb, width), lambda i: (0, i, 0)), pl.BlockSpec((qkv_w.shape[0], 3, width // qkv_w.shape[0], width), lambda i: (0, 0, 0, 0)), blk, blk, whole(gain.shape)],
        out_specs=[blk, vec, vec],
        out_shape=[jax.ShapeDtypeStruct((tokens, width), bf16),
                   jax.ShapeDtypeStruct((1, width), f32), jax.ShapeDtypeStruct((1, width), f32)],
        compiler_params=params(),
        cost_estimate=cost(6 * tokens * width * width, tokens * width * 16 + width * width * 6),
        name="norm1_back",
    )(dqkv, qkv_w, h0, dh1, gain)


def part_slices(side):
    low, own, high = slice(0, MARGIN), slice(MARGIN, MARGIN + side), slice(MARGIN + side, 2 * MARGIN + side)
    return [(own, own), (own, low), (own, high), (low, own), (low, low), (low, high),
            (high, own), (high, low), (high, high)]


@functools.lru_cache(None)
def token_places(dates, side):
    extent = side + 2 * MARGIN
    grid = np.stack(np.meshgrid(np.arange(dates), np.arange(extent), np.arange(extent), indexing="ij"), -1)
    return np.concatenate([grid[:, r, c].reshape(-1, 3) for r, c in part_slices(side)])


@functools.lru_cache(None)
def halo_tables(dates, side):
    places = token_places(dates, side)
    extent = side + 2 * MARGIN
    own = dates * side * side
    edge = dates * side * MARGIN
    index = {tuple(p): i for i, p in enumerate(places)}

    def table(wanted, count):
        out = np.zeros((len(wanted), count), np.float32)
        out[np.arange(len(wanted)), [index[w] for w in wanted]] = 1
        return out

    def shifted(part, dr, dc):
        r, c = part_slices(side)[part]
        grid = np.stack(np.meshgrid(np.arange(dates), np.arange(extent)[r], np.arange(extent)[c], indexing="ij"), -1)
        return [(d, y + dr, x + dc) for d, y, x in grid.reshape(-1, 3)]

    first = table(shifted(1, 0, side) + shifted(2, 0, -side), own)
    north = shifted(3, side, 0) + shifted(4, side, 0) + shifted(5, side, 0)
    south = shifted(6, -side, 0) + shifted(7, -side, 0) + shifted(8, -side, 0)
    second = table(north + south, own + 2 * edge)
    return first, second


def chain(axis, step):
    count = lax.axis_size(axis)
    return [(i, i + step) for i in range(count) if 0 <= i + step < count]


def pick(table, values):
    return lax.dot(jnp.asarray(table, bf16), values, preferred_element_type=f32)


def to_neighbours(low, high, axis):
    return lax.ppermute(low, axis, chain(axis, -1)), lax.ppermute(high, axis, chain(axis, 1))


def margin_first(own, dates, side):
    first, _ = halo_tables(dates, side)
    edge = dates * side * MARGIN
    sent = pick(first, own).astype(bf16)
    return sent[edge:], sent[:edge]


def margin_second(own, right, left, dates, side):
    _, second = halo_tables(dates, side)
    both = dates * side * MARGIN + 2 * dates * MARGIN * MARGIN
    middle = jnp.concatenate([own, left, right])
    sent = pick(second, middle).astype(bf16)
    return middle, sent[both:], sent[:both]


def give_margin_and_sum(own, dates, side, weight, *ready):
    first, second = halo_tables(dates, side)
    edge = dates * side * MARGIN
    corner = dates * MARGIN * MARGIN
    width = own.shape[1]

    def with_rows(strip, values):
        values = values.reshape(1, -1).astype(bf16)
        return jnp.concatenate([strip, jnp.pad(values, ((0, 15), (0, width - values.shape[1])))])

    def values_of(strip, *shape):
        return strip[-16, : np.prod(shape)].reshape(shape).astype(f32)

    sent = pick(first, own).astype(bf16)
    right, left = to_neighbours(with_rows(sent[edge:], weight[:, :MARGIN]), with_rows(sent[:edge], weight[:, -MARGIN:]), "gx")
    right, left, *_ = tied(right, left, *ready)
    extent = side + 2 * MARGIN
    total = weight[:, MARGIN:-MARGIN]
    total = total + jnp.pad(values_of(left, extent, MARGIN), ((0, 0), (0, side - MARGIN)))
    total = total + jnp.pad(values_of(right, extent, MARGIN), ((0, 0), (side - MARGIN, 0)))
    middle = jnp.concatenate([own, left[:edge], right[:edge]])
    sent = pick(second, middle).astype(bf16)
    lower, upper = to_neighbours(with_rows(sent[edge + 2 * corner :], total[:MARGIN]),
                                 with_rows(sent[: edge + 2 * corner], total[-MARGIN:]), "gy")
    total = total[MARGIN:-MARGIN]
    total = total + jnp.pad(values_of(upper, MARGIN, side), ((0, side - MARGIN), (0, 0)))
    total = total + jnp.pad(values_of(lower, MARGIN, side), ((side - MARGIN, 0), (0, 0)))
    return (own, left, right, upper, lower), total


def fold_first(every, dates, side):
    edge = dates * side * MARGIN
    middle = dates * side * side + 2 * edge
    both = edge + 2 * dates * MARGIN * MARGIN
    return every[middle : middle + both], every[middle + both :]


def fold_second(every, below, above, dates, side):
    _, second = halo_tables(dates, side)
    own = dates * side * side
    edge = dates * side * MARGIN
    middle = every[: own + 2 * edge].astype(f32) + pick(second.T, jnp.concatenate([below, above]))
    sides = middle[own:].astype(bf16)
    return middle[:own], sides[:edge], sides[edge:]


def fold_third(part, east, west, dates, side):
    first, _ = halo_tables(dates, side)
    return (part + pick(first.T, jnp.concatenate([east, west]))).astype(bf16)


def sincos(places, span_width):
    half_width = span_width // 2
    omega = 1.0 / 10000.0 ** (jnp.arange(half_width, dtype=f32) / half_width)
    angles = places[:, None] * omega[None, :]
    return jnp.concatenate([jnp.sin(angles), jnp.cos(angles)], axis=1)


def position_parts(tile_row, tile_col, stamps, side, width):
    side_width = width // 16 * 6
    time_width = width - 2 * side_width
    extent = side + 2 * MARGIN
    dates = stamps.shape[0]
    offsets = jnp.arange(extent, dtype=jnp.int32) - MARGIN
    table = jnp.concatenate([
        jnp.pad(sincos(stamps.astype(f32), time_width), ((0, 0), (0, 2 * side_width))),
        jnp.pad(sincos((tile_row * side + offsets).astype(f32), side_width), ((0, 0), (time_width, side_width))),
        jnp.pad(sincos((tile_col * side + offsets).astype(f32), side_width), ((0, 0), (time_width + side_width, 0))),
    ])
    places = token_places(dates, side)
    hot = np.zeros((len(places), dates + 2 * extent), np.float32)
    spots = np.arange(len(places))
    hot[spots, places[:, 0]] = 1
    hot[spots, dates + places[:, 1]] = 1
    hot[spots, dates + extent + places[:, 2]] = 1
    hot = np.concatenate([hot] * 3, axis=1)
    spare = -hot.shape[1] % 128
    hot = np.pad(hot, ((0, 0), (0, spare)))
    parts = jnp.concatenate(three_parts(table))
    return jnp.asarray(hot, bf16), jnp.pad(parts, ((0, spare), (0, 0)))


def dense(left, right, ca=1, cb=0):
    return lax.dot_general(left, right, (((ca,), (cb,)), ((), ())), preferred_element_type=f32)


def gather(shard):
    return lax.all_gather(shard, "gx", axis=0, tiled=True)


def swap(value, axis, bit):
    return lax.ppermute(value, axis, [(i, i ^ bit) for i in range(lax.axis_size(axis))])


def turn(value, step):
    count = lax.axis_size("gx")
    return lax.ppermute(value, "gx", [(i, (i + 2 * step) % count) for i in range(count)])


def after(value, *earlier):
    return lax.optimization_barrier((value, *earlier))[0]


def along_z(mine):
    return jnp.stack([turn(mine, k) for k in (1, 2, 3)])


def tied(*values):
    return lax.optimization_barrier(values)


def along_gy(got):
    return got, swap(got, "gy", 1), swap(got, "gy", 2), swap(got, "gy", 3)


def core_swap(pieces):
    return tuple(swap(p, "gx", 1) for p in pieces)


def added(*values):
    return sum(v.astype(f32) for v in values).astype(bf16)


def at(value, index, axis=0):
    return lax.dynamic_index_in_dim(value, index, axis, keepdims=False)


def folded_gy(value):
    return value.reshape(2, 2, *value.shape[1:])


def near_sum(keep, got, first, g):
    keep, got = folded_gy(keep), folded_gy(got)
    dim, b = (1, g & 1) if first == 1 else (0, g >> 1)
    return added(at(keep, 1 - b, dim), at(got, 1 - b, dim)), added(at(keep, b, dim), at(got, b, dim))


def far_sum(keep, got, first, g):
    b = (g >> 1) if first == 1 else (g & 1)
    return added(at(keep, 1 - b), at(got, 1 - b)), (at(keep, b), at(got, b))


def to_each(keep, got, g):
    return [added(at(keep, g ^ m), at(got, g ^ m)) for m in (1, 2, 3)], (at(keep, g), at(got, g))


def swap_each(values):
    return [swap(v, "gy", m) for v, m in zip(values, (1, 2, 3))]


def scatter_z(mine):
    count = lax.axis_size("gx")
    groups = [list(range(core, count, 2)) for core in range(2)]
    return lax.psum_scatter(mine, "gx", scatter_dimension=0, axis_index_groups=groups, tiled=False)


def along_z_sum(mine, z):
    came = [turn(at(mine, (z + k) % 4), k) for k in (1, 2, 3)]
    return at(mine, z), came


def side_by_side(value):
    half = value.shape[1] // 2
    return jnp.concatenate([value[:, :half], value[:, half:]], axis=2)


def stacked_again(value):
    half = value.shape[1] // 2
    return jnp.concatenate([value[:, :half], value[:, half:]])


def to_all_gy(mine):
    return [mine] + [swap(mine, "gy", m) for m in (1, 2, 3)]


def in_order(every, g):
    every = jnp.stack(every)
    return [at(every, p ^ g) for p in range(4)]


def gather_apart(shard):
    return lax.all_gather(shard, "gx", axis=0, tiled=False)


def collect_all(keep, send, tall):
    both = jnp.stack([keep, send], axis=2)
    parts, chips, _, rows_each, width = both.shape
    if tall:
        grad = both.transpose(1, 2, 0, 3, 4).reshape(-1, width)
    else:
        grad = both.transpose(1, 2, 3, 0, 4).reshape(-1, parts * width)
    grad = lax.psum(scatter(grad), "gy").astype(f32)
    return jnp.split(grad, parts, axis=0 if tall else 1)


def scatter(grad):
    return lax.psum_scatter(grad.astype(bf16), "gx", scatter_dimension=0, tiled=True)


def on_device(pixels, pad_mask, timestamps, scene_dates, scene_map, blend_weight, cotangent, patch_w, norm1_gain,
              norm1_bias, qkv_w, proj_w, norm2_gain, norm2_bias, fc1_w, fc1_b, fc2_w, dec_w, head_w):
    dates, side, _, pixel_width = pixels.shape
    own = dates * side * side
    extent = side + 2 * MARGIN
    places = token_places(dates, side)
    tokens = len(places)
    model_width = patch_w.shape[1]
    scale = float(model_width // HEADS) ** (-0.5)
    tile_row = lax.axis_index("gy")
    tile_col = lax.axis_index("gx")
    split = lax.axis_size("gx") == 8 and lax.axis_size("gy") == 4
    chip, core = (tile_col >> 1, tile_col & 1) if split else (0, 0)
    pos = jnp.stack([jnp.int32(chip), tile_row, jnp.int32(core)]).astype(jnp.int32)

    nearby = lax.dynamic_slice(jnp.pad(scene_map, 1, constant_values=-1), (tile_row, tile_col), (3, 3))
    own_scene = nearby[1, 1]
    bands = np.array([0] * MARGIN + [1] * side + [2] * MARGIN)
    same = (nearby == own_scene)[bands][:, bands].astype(f32)
    weight = blend_weight.astype(f32) * same
    masked = (pixels * pad_mask.astype(bf16)[..., None]).reshape(own, pixel_width)
    each = norm1_gain.shape[0]
    vectors = jnp.concatenate([jnp.stack([norm1_gain, norm1_bias, norm2_gain, norm2_bias]), fc1_b.reshape(-1, each)])
    vectors = jnp.pad(vectors, ((0, 16 - vectors.shape[0]), (0, model_width - each)))
    dec_rows, dec_width = dec_w.shape
    head_rows, slabs = head_w.shape[0], pixel_width // dec_width
    share_p = jnp.concatenate([patch_w, vectors])
    share_a = jnp.concatenate([qkv_w, proj_w], axis=1)
    slabs_of = head_w.reshape(head_rows, slabs, dec_width).transpose(1, 0, 2).reshape(-1, dec_width)
    share_d = jnp.concatenate([dec_w, slabs_of])
    front_p = gather_apart(share_p)
    quarter = patch_w.shape[0] // 4
    parts_of = lambda m: m.reshape(8, model_width // 8, 4, model_width).transpose(0, 2, 1, 3)
    if split:
        row = tile_row
        got_a = along_z(lax.dynamic_slice_in_dim(share_a, row * model_width, model_width, axis=1))
        mine_b = jnp.concatenate([lax.dynamic_slice_in_dim(fc1_w, row * model_width, model_width, axis=1),
                                  lax.dynamic_slice_in_dim(fc2_w, row * each, each, axis=0)])
        strips, denom = give_margin_and_sum(masked, dates, side, weight, got_a)
        got_b = along_z(after(mine_b, front_p, *strips[1:]))
        pieces_a = (share_a, *along_gy(got_a))
        others_a = core_swap(pieces_a)
        share_d = after(share_d, got_b, *pieces_a)
    else:
        strips, denom = give_margin_and_sum(masked, dates, side, weight)
        front_a = parts_of(jnp.concatenate([gather(qkv_w), gather(proj_w)], axis=1))
        quarters_of = lambda m: m.reshape(8, 4, -1, model_width)
        full_mlp = jnp.concatenate([parts_of(gather(fc1_w)), quarters_of(gather(fc2_w))], axis=2)
    tops = gather_apart(share_d)
    full_dec = tops[:, :dec_rows].reshape(-1, dec_width)
    full_head = tops[:, dec_rows:].reshape(-1, slabs, head_rows, dec_width).transpose(0, 2, 1, 3).reshape(-1, pixel_width)
    small = front_p[:, patch_w.shape[0] :]
    own_dates = scene_dates[own_scene]
    stamps = timestamps[own_scene]
    date_ok = jnp.arange(dates, dtype=jnp.int32) < own_dates
    spot_hot = np.zeros((tokens, extent * extent), np.float32)
    spot_hot[np.arange(tokens), places[:, 1] * extent + places[:, 2]] = 1
    per_token = pick(spot_hot, jnp.stack([weight.reshape(-1), same.reshape(-1)], axis=1).astype(bf16))
    weight_tok = per_token[:, :1]
    seen = per_token[:, 1:] * (jnp.asarray(places[:, :1], jnp.int32) < own_dates).astype(f32)
    lane = np.arange(128)[None, :]
    kx = jnp.where(lane < 3, 1.0, jnp.where(lane == 3, (1.0 - seen) * -1e9, 0.0)).astype(bf16)
    denom = jnp.broadcast_to(denom[None], (dates, side, side)).reshape(own, 1)

    hot, table = position_parts(tile_row, tile_col, stamps, side, model_width)
    small = small[:, :8, :each].astype(f32)
    vec = small[:, :4].transpose(1, 0, 2).reshape(4, -1)
    full_b = small[:, 4:].reshape(1, -1)

    shown = pad_mask.reshape(own, 1).astype(f32)
    valid = (pad_mask.astype(f32) * date_ok.astype(f32)[:, None, None]).reshape(own, 1)
    ratio = valid / denom
    gr = (cotangent.reshape(own, pixel_width).astype(f32) * ratio).astype(bf16)
    ext, h0, a = embed(strips, front_p, hot, table, vec)
    if split:
        front_a = place(pos, pieces_a, (*others_a[:-1], after(others_a[-1], a)), ("wide",))
        a, got_b = tied(a, got_b)
        pieces_b = (fc1_w, fc2_w, *along_gy(got_b))
    qkv = project(a, front_a, 3)
    o, qx = attn_fwd(qkv, kx, scale)
    if split:
        o, *pieces_b = tied(o, *pieces_b)
        others_b = core_swap(pieces_b)
    h1, c = proj_norm(o, front_a, h0, vec)
    gz = dense(after(gr, c), full_head, 1, 1).astype(bf16)
    west, east = margin_first(gz, dates, side)
    c, west, east = tied(c, west, east)
    right, left = to_neighbours(west, east, "gx")
    if split:
        full_mlp = place(pos, pieces_b, (*others_b[:-1], after(others_b[-1], c)), ("wide", "tall"))
        full_mlp, right, left = tied(full_mlp, right, left)
    middle, north, south = margin_second(gz, right, left, dates, side)
    full_mlp, north, south = tied(full_mlp, north, south)
    lower, upper = to_neighbours(north, south, "gy")
    u, slope, h2r = mlp_fwd(c, full_mlp, full_b, h1)
    z = dense(h2r, full_dec).astype(bf16)
    every = (z.astype(f32) * weight_tok).astype(bf16)
    north, south = fold_first(every, dates, side)
    below, above = to_neighbours(north, south, "gy")

    lower, upper, north, south = tied(lower, upper, north, south)
    dz_every = jnp.concatenate([middle, upper, lower])
    dz = (dz_every.astype(f32) * weight_tok).astype(bf16)
    dh2 = dense(dz, full_dec, 1, 1)
    dm, north, south = tied(dh2.astype(bf16), north, south)
    dc, grad_fc1_b, keep1, send1, keep2, send2 = mlp_bwd(pos, dm, c, u, slope, full_mlp, 4)
    g = tile_row
    if split:
        got1, got2 = swap(send1, "gx", 1), swap(send2, "gx", 1)
    grad_dec = dense(h2r, dz, 0, 0)
    dc, grad_dec = tied(dc, grad_dec.astype(bf16))
    grad_dec = scatter(grad_dec)
    dh1, dattn, do, grad_gain2, grad_shift2 = norm2_back(dc, h1, dh2, vec, front_a)
    below, above, do = tied(below, above, do)
    folded, west, east = fold_second(every, below, above, dates, side)
    do, west, east = tied(do, west, east)
    right, left = to_neighbours(west, east, "gx")
    if split:
        got1, got2 = after(got1, do), after(got2, do)
        out1, keep1 = near_sum(keep1, got1, 1, g)
        out2, keep2 = near_sum(keep2, got2, 2, g)
        do, out1, out2 = tied(do, out1, out2)
        got1, got2 = swap(out1, "gy", 1), swap(out2, "gy", 2)
    dqkv = attn_bwd(qkv, do, o, qx, kx, scale)
    right, left = after(right, dqkv), after(left, dqkv)
    folded = fold_third(folded, right, left, dates, side)
    grad_head = dense(folded, gr, 0, 0)
    dqkv, grad_head = tied(dqkv, grad_head.astype(bf16))
    grad_head = scatter(grad_head)
    if split:
        got1, got2 = after(got1, dqkv), after(got2, dqkv)
        out1, keep1 = far_sum(keep1, got1, 1, g)
        out2, keep2 = far_sum(keep2, got2, 2, g)
        dqkv, out1, out2 = tied(dqkv, out1, out2)
        got1, got2 = swap(out1, "gy", 2), swap(out2, "gy", 1)
    keep3, send3 = qkvo_grad(pos, a, dqkv, o, dattn, 4)
    if split:
        got3 = swap(send3, "gx", 1)
    demb, grad_gain1, grad_shift1 = norm1_back(dqkv, front_a, h0, dh1, vec)
    vectors = (grad_gain1, grad_shift1, grad_gain2, grad_shift2)
    north, south = fold_first(demb, dates, side)
    ends = jnp.concatenate([after(grad_dec, demb), after(grad_head, demb).reshape(-1, dec_width)])
    if split:
        got3, got1, got2 = after(got3, demb), after(got1, demb), after(got2, demb)
        outs3, keep3 = to_each(keep3, got3, g)
        mine1 = jnp.concatenate([added(*keep1, got1), added(*keep2, got2)], axis=1)
        demb, mine1 = tied(demb, mine1)
        done1 = scatter_z(mine1)
        demb, north, south, *outs3 = tied(demb, north, south, *outs3)
    below, above = to_neighbours(north, south, "gy")
    if split:
        got3 = swap_each(outs3)
        keep4, send4 = patch_grad(pos, ext, demb, grad_fc1_b, vectors, 4, 4)
        got4 = swap(send4, "gx", 1)
        got3 = [after(v, keep4) for v in got3]
        mine3 = added(*keep3, *got3)
        below, above, got4 = after(below, mine3), after(above, mine3), after(got4, mine3)
    part, west, east = fold_second(demb, below, above, dates, side)
    right, left = to_neighbours(west, east, "gx")
    if split:
        outs4, keep4 = to_each(keep4, got4, g)
        right, left, *outs4 = tied(right, left, *outs4)
        got4 = swap_each(outs4)
        dmasked = fold_third(part, right, left, dates, side)
        dmasked, done1 = tied(dmasked, done1)
        every1 = to_all_gy(jnp.concatenate([done1, ends.reshape(-1, model_width)]))
        pixel_grad = pixel_back(dmasked, front_p, shown, pixel_width)
        got4 = [after(v, pixel_grad) for v in got4]
        mine4, came4 = along_z_sum(jnp.concatenate([mine3, added(*keep4, *got4)], axis=1), chip)
        folded, mine4 = tied(folded, mine4)
        recon = (dense(folded, full_head) * ratio).astype(bf16)
        came4 = [after(v, recon) for v in came4]
        done4 = added(mine4, *came4)
        every1 = tied(*every1, done4)[:-1]
        every4 = to_all_gy(done4)
        ends = added(*[v[2 * each :] for v in every1]).astype(f32).reshape(-1, dec_width)
        every1 = in_order([v[: 2 * each] for v in every1], g)
        sum1 = jnp.concatenate([v[:each] for v in every1], axis=1).astype(f32)
        sum2 = jnp.concatenate([v[each:] for v in every1], axis=0).astype(f32)
        every4 = tied(*every4, sum1, sum2, ends)[:-3]
        every4 = in_order(every4, g)
        sum1, sum2 = jnp.split(sum1, 4, axis=1), jnp.split(sum2, 4, axis=0)
        sum3 = [v[:each] for v in every4]
        grad_patch = jnp.concatenate([v[each : each + quarter] for v in every4])
        small = every4[0][each + quarter :]
    else:
        recon = (dense(folded, full_head) * ratio).astype(bf16)
        dmasked = fold_third(part, right, left, dates, side)
        sum1, sum2 = collect_all(keep1, send1, False), collect_all(keep2, send2, True)
        sum3 = collect_all(keep3, send3, False)
        pixel_grad = pixel_back(dmasked, front_p, shown, pixel_width)
        grad_patch = lax.psum(scatter(dense(ext, demb, 0, 0)), "gy")
        small = lax.psum(jnp.concatenate([*vectors, grad_fc1_b.reshape(-1, model_width)]), ("gy", "gx"))
        ends = lax.psum(ends, "gy")
    small = small.astype(f32)
    mine_of = lambda value, count: lax.dynamic_slice_in_dim(value.reshape(-1), tile_col * count, count)
    grad_bias = mine_of(small[4 : 4 + full_b.shape[1] // model_width], fc1_b.shape[0])
    return (
        recon.reshape(pixels.shape),
        pixel_grad.reshape(pixels.shape),
        grad_patch.astype(f32),
        mine_of(small[0], each),
        mine_of(small[1], each),
        jnp.concatenate(sum3[:3], axis=1).astype(f32),
        sum3[3].astype(f32),
        mine_of(small[2], each),
        mine_of(small[3], each),
        jnp.concatenate(sum1, axis=1).astype(f32),
        grad_bias,
        jnp.concatenate(sum2, axis=0).astype(f32),
        ends[:dec_rows].astype(f32),
        ends[dec_rows:].reshape(head_rows, pixel_width).astype(f32),
    )


def solution(mesh):
    in_specs = (
        P(None, "gy", "gx", None),
        P(None, "gy", "gx"),
        P(),
        P(),
        P(),
        P("gy", "gx"),
        P(None, "gy", "gx", None),
        P("gx", None),
        P("gx"),
        P("gx"),
        P("gx", None),
        P("gx", None),
        P("gx"),
        P("gx"),
        P("gx", None),
        P("gx"),
        P("gx", None),
        P("gx", None),
        P("gx", None),
    )
    out_specs = (
        P(None, "gy", "gx", None),
        P(None, "gy", "gx", None),
        P("gx", None),
        P("gx"),
        P("gx"),
        P("gx", None),
        P("gx", None),
        P("gx"),
        P("gx"),
        P("gx", None),
        P("gx"),
        P("gx", None),
        P("gx", None),
        P("gx", None),
    )
    return jax.shard_map(
        on_device, mesh=mesh, in_specs=in_specs, out_specs=out_specs, check_vma=False
    )
```

```python
import functools
import jax
import jax.numpy as jnp
import numpy as np
from jax import lax
from jax.experimental import pallas as pl
from jax.experimental.pallas import tpu as pltpu
from jax.sharding import PartitionSpec as P

HEADS = 12
MARGIN = 2
norm_eps = 1e-06
VMEM_BYTES = 56 * 1024 * 1024
f32, bf16 = jnp.float32, jnp.bfloat16


def params():
    return pltpu.CompilerParams(vmem_limit_bytes=VMEM_BYTES)


def cost(flops, nbytes):
    return pl.CostEstimate(flops=int(flops), bytes_accessed=int(nbytes), transcendentals=0)


def dot(a, b, ca=1, cb=0):
    return lax.dot_general(a, b, (((ca,), (cb,)), ((), ())), preferred_element_type=f32)


def whole(shape):
    return pl.BlockSpec(shape, lambda *_: (0,) * len(shape))


def rows(block, width):
    return pl.BlockSpec((block, width), lambda i: (i, 0))


def last_part(gathered, width):
    shares = gathered.shape[0]
    return pl.BlockSpec((shares, 1, width // shares, width), lambda i: (0, 3, 0, 0))


def patch_part(gathered, depth):
    shares, _, width = gathered.shape
    return pl.BlockSpec((shares, depth // shares, width), lambda i: (0, 0, 0))


def square(ref):
    return ref[...].reshape(-1, ref.shape[-1])


def norm_parts(hidden):
    center = jnp.mean(hidden, axis=-1, keepdims=True)
    centered = hidden - center
    spread = jnp.mean(centered * centered, axis=-1, keepdims=True)
    rstd = lax.rsqrt(spread + norm_eps)
    return centered * rstd, rstd


def token_block(tokens):
    for parts in (3, 2):
        if tokens % (16 * parts) == 0:
            return tokens // parts
    return tokens


def embed_kernel(own_ref, left_ref, right_ref, upper_ref, lower_ref, w_ref, pick_ref, table_ref, vec_ref, ext_ref, h0_ref, a_ref, *, pieces):
    refs = (own_ref, left_ref, right_ref, upper_ref, lower_ref)
    for step, held in enumerate(pieces):
        @pl.when(pl.program_id(0) == step)
        def _(held=held):
            spot = 0
            for i, start, count in held:
                ext_ref[spot : spot + count, :] = refs[i][start : start + count, :]
                spot += count
    hidden = dot(ext_ref[...], square(w_ref)) + dot(pick_ref[...], table_ref[...])
    h0_ref[...] = hidden
    xhat, _ = norm_parts(hidden)
    a_ref[...] = (xhat * vec_ref[0:1, :] + vec_ref[1:2, :]).astype(bf16)


def embed(strips, gathered, pick, table, vec):
    tokens = pick.shape[0]
    depth = strips[0].shape[1]
    width = gathered.shape[2]
    tb = token_block(tokens)
    sizes = [strips[0].shape[0]] + [s.shape[0] - 16 for s in strips[1:]]
    pieces, room = [[]], tb
    for i, size in enumerate(sizes):
        start = 0
        while start < size:
            if room == 0:
                pieces.append([])
                room = tb
            count = min(size - start, room)
            pieces[-1].append((i, start, count))
            start, room = start + count, room - count
    return pl.pallas_call(
        functools.partial(embed_kernel, pieces=pieces),
        grid=(tokens // tb,),
        in_specs=[whole(s.shape) for s in strips] + [patch_part(gathered, depth), rows(tb, pick.shape[1]),
                  whole(table.shape), whole(vec.shape)],
        out_specs=[rows(tb, depth), rows(tb, width), rows(tb, width)],
        out_shape=[jax.ShapeDtypeStruct((tokens, depth), bf16), jax.ShapeDtypeStruct((tokens, width), f32),
                   jax.ShapeDtypeStruct((tokens, width), bf16)],
        compiler_params=params(),
        cost_estimate=cost(2 * tokens * depth * width, tokens * depth * 4 + depth * width * 2 + tokens * width * 6),
        name="embed",
    )(*strips, gathered, pick, table, vec)


def columns_kernel(a_ref, w_ref, o_ref):
    o_ref[...] = dot(a_ref[...], square(w_ref)).astype(o_ref.dtype)


def project(a, gathered, count):
    tokens, width = a.shape
    half = width // 2
    return pl.pallas_call(
        columns_kernel,
        grid=(2 * count,),
        in_specs=[whole(a.shape), pl.BlockSpec((gathered.shape[0], 1, width // gathered.shape[0], half), lambda i: (0, i // 2, 0, i % 2))],
        out_specs=pl.BlockSpec((tokens, half), lambda i: (0, i)),
        out_shape=jax.ShapeDtypeStruct((tokens, count * width), bf16),
        compiler_params=params(),
        cost_estimate=cost(2 * tokens * width * width * count, a.size * 2 + width * width * count * 2 + tokens * width * count * 2),
        name="project",
    )(a, gathered)


def three_parts(value):
    first = value.astype(bf16)
    rest = value - first.astype(f32)
    second = rest.astype(bf16)
    third = (rest - second.astype(f32)).astype(bf16)
    return first, second, third


def in_lanes(parts, lane, tail):
    out = tail
    for spot, part in reversed(list(enumerate(parts))):
        out = jnp.where(lane == spot, part.astype(f32), out)
    return out.astype(bf16)


def attn_fwd_kernel(q_ref, k_ref, v_ref, kx_ref, o_ref, qx_ref, *, block, scale):
    tokens, pair = q_ref.shape
    half = pair // 2
    k_aug = jnp.concatenate([k_ref[...], kx_ref[...]], axis=1)
    v_aug = jnp.concatenate([v_ref[...], jnp.ones((tokens, pair), bf16)], axis=1)
    lane = lax.broadcasted_iota(jnp.int32, (block, pair), 1)
    for start in range(0, tokens, block):
        q_blk = q_ref[start : start + block, :].astype(f32) * scale
        outs = []
        for j in range(2):
            mine = (lane >= half) if j else (lane < half)
            q_aug = jnp.concatenate(
                [jnp.where(mine, q_blk, 0.0).astype(bf16),
                 jnp.where(lane == 3, 1.0, 0.0).astype(bf16)], axis=1)
            s = dot(q_aug, k_aug, 1, 1)
            top = jnp.max(s, axis=1, keepdims=True)
            p = jnp.exp(s - top).astype(bf16)
            mixed = dot(p, v_aug)
            total = mixed[:, pair:]
            outs.append(mixed[:, :pair] / total)
            lse = jnp.log(total) + top
            qx_ref[j, start : start + block, :] = in_lanes(
                three_parts(-lse), lane, jnp.where(lane == 3, 1.0, 0.0))
        o_ref[start : start + block, :] = jnp.where(lane < half, outs[0], outs[1]).astype(bf16)


def attn_fwd(qkv, kx, scale):
    tokens = qkv.shape[0]
    width = qkv.shape[1] // 3
    pairs = HEADS // 2
    pw = width // pairs
    spec = lambda part: pl.BlockSpec((tokens, pw), lambda h, part=part: (0, part * pairs + h))
    return pl.pallas_call(
        functools.partial(attn_fwd_kernel, block=token_block(tokens), scale=scale),
        grid=(pairs,),
        in_specs=[spec(0), spec(1), spec(2), whole(kx.shape)],
        out_specs=[pl.BlockSpec((tokens, pw), lambda h: (0, h)),
                   pl.BlockSpec((2, tokens, pw), lambda h: (h, 0, 0))],
        out_shape=[jax.ShapeDtypeStruct((tokens, width), bf16),
                   jax.ShapeDtypeStruct((HEADS, tokens, pw), bf16)],
        compiler_params=params(),
        cost_estimate=cost(2 * 4 * HEADS * tokens * tokens * 256, qkv.size * 2 + tokens * width * 2),
        name="attn_fwd",
    )(qkv, qkv, qkv, kx)


def attn_bwd_kernel(q_ref, k_ref, v_ref, do_ref, o_ref, qx_ref, kx_ref, d_ref, *, block, scale):
    tokens, pair = q_ref.shape
    half = pair // 2
    lane = lax.broadcasted_iota(jnp.int32, (tokens, pair), 1)
    q_all = q_ref[...].astype(f32) * scale
    do_all = do_ref[...].astype(f32)
    prod = do_all * o_ref[...].astype(f32)
    kx = kx_ref[...]
    dq = [None, None]
    dk = [None] * (tokens // block)
    dv = [None] * (tokens // block)
    for j in range(2):
        mine = (lane >= half) if j else (lane < half)
        q_j = jnp.where(mine, q_all, 0.0).astype(bf16)
        do_j = jnp.where(mine, do_all, 0.0).astype(bf16)
        delta = jnp.sum(jnp.where(mine, prod, 0.0), axis=1, keepdims=True)
        dox = in_lanes(three_parts(-delta), lane, jnp.zeros_like(prod))
        q_aug = jnp.concatenate([q_j, qx_ref[j]], axis=1)
        do_aug = jnp.concatenate([do_j, dox], axis=1)
        for b in range(tokens // block):
            at = slice(b * block, (b + 1) * block)
            k_blk = k_ref[at, :]
            sT = dot(jnp.concatenate([k_blk, kx[at]], axis=1), q_aug, 1, 1)
            pT = jnp.exp(sT)
            dpT = dot(jnp.concatenate([v_ref[at, :], kx[at]], axis=1), do_aug, 1, 1)
            dsT = (pT * dpT).astype(bf16)
            dv_b = dot(pT.astype(bf16), do_j)
            dk_b = dot(dsT, q_j)
            dq_b = dot(dsT, k_blk, 0, 0)
            dv[b] = dv_b if dv[b] is None else dv[b] + dv_b
            dk[b] = dk_b if dk[b] is None else dk[b] + dk_b
            dq[j] = dq_b if dq[j] is None else dq[j] + dq_b
    for b in range(tokens // block):
        at = slice(b * block, (b + 1) * block)
        d_ref[1, at, :] = dk[b].astype(bf16)
        d_ref[2, at, :] = dv[b].astype(bf16)
    d_ref[0] = (jnp.where(lane < half, dq[0], dq[1]) * scale).astype(bf16)


def attn_bwd(qkv, do, o, qx, kx, scale):
    tokens = qkv.shape[0]
    width = qkv.shape[1] // 3
    pairs = HEADS // 2
    pw = width // pairs
    spec = lambda part: pl.BlockSpec((tokens, pw), lambda h, part=part: (0, part * pairs + h))
    one = pl.BlockSpec((tokens, pw), lambda h: (0, h))
    return pl.pallas_call(
        functools.partial(attn_bwd_kernel, block=token_block(tokens), scale=scale),
        grid=(pairs,),
        in_specs=[spec(0), spec(1), spec(2), one, one,
                  pl.BlockSpec((2, tokens, pw), lambda h: (h, 0, 0)), whole(kx.shape)],
        out_specs=pl.BlockSpec((3, tokens, pw), lambda h: (0, 0, h)),
        out_shape=jax.ShapeDtypeStruct((3, tokens, width), bf16),
        compiler_params=params(),
        cost_estimate=cost(2 * 5 * HEADS * tokens * tokens * 256, qkv.size * 2 + tokens * width * 10),
        name="attn_bwd",
    )(qkv, qkv, qkv, do, o, qx, kx)


def proj_kernel(o_ref, w_ref, h0_ref, vec_ref, h1_ref, c_ref):
    hidden = h0_ref[...] + dot(o_ref[...], square(w_ref))
    h1_ref[...] = hidden
    xhat, _ = norm_parts(hidden)
    c_ref[...] = (xhat * vec_ref[2:3, :] + vec_ref[3:4, :]).astype(bf16)


def proj_norm(o, proj_w, h0, vec):
    tokens, width = o.shape
    tb = token_block(tokens)
    return pl.pallas_call(
        proj_kernel,
        grid=(tokens // tb,),
        in_specs=[rows(tb, width), last_part(proj_w, width), rows(tb, width), whole(vec.shape)],
        out_specs=[rows(tb, width), rows(tb, width)],
        out_shape=[jax.ShapeDtypeStruct((tokens, width), f32),
                   jax.ShapeDtypeStruct((tokens, width), bf16)],
        compiler_params=params(),
        cost_estimate=cost(2 * tokens * width * width, tokens * width * 12 + width * width * 2),
        name="proj_norm",
    )(o, proj_w, h0, vec)


def mlp_weight_specs(gathered, width):
    shares, parts, _, _ = gathered.shape
    each = width // shares
    return [pl.BlockSpec((shares, 1, each, width), lambda i, *_: (0, i, 0, 0)),
            pl.BlockSpec((shares // parts, parts, each, width), lambda i, *_: (i, 0, 1, 0))]


def mlp_fwd_kernel(c_ref, fc1_ref, b_ref, fc2_ref, h1_ref, u_ref, g_ref, h2_ref, acc_ref):
    step = pl.program_id(0)
    pre = dot(c_ref[...], square(fc1_ref)) + b_ref[...]
    cdf = 0.5 * (1.0 + lax.erf(pre * np.float32(0.5 ** 0.5)))
    act = (pre * cdf).astype(bf16)
    u_ref[...] = act
    g_ref[...] = (cdf + pre * jnp.exp(-0.5 * pre * pre) * np.float32((2 * np.pi) ** -0.5)).astype(bf16)
    part = dot(act, square(fc2_ref))

    @pl.when(step == 0)
    def _():
        acc_ref[...] = h1_ref[...] + part

    @pl.when(step > 0)
    def _():
        acc_ref[...] += part

    @pl.when(step == pl.num_programs(0) - 1)
    def _():
        h2_ref[...] = acc_ref[...].astype(bf16)


def mlp_fwd(c, gathered, bias, h1):
    tokens, width = c.shape
    parts, block = gathered.shape[1], width
    ff = parts * block
    fc1_spec, fc2_spec = mlp_weight_specs(gathered, width)
    cols = lambda n: pl.BlockSpec((n, block), lambda i: (0, i))
    return pl.pallas_call(
        mlp_fwd_kernel,
        grid=(ff // block,),
        in_specs=[whole(c.shape), fc1_spec, cols(1), fc2_spec, whole(h1.shape)],
        out_specs=[cols(tokens), cols(tokens), whole(c.shape)],
        out_shape=[jax.ShapeDtypeStruct((tokens, ff), bf16), jax.ShapeDtypeStruct((tokens, ff), bf16),
                   jax.ShapeDtypeStruct((tokens, width), bf16)],
        scratch_shapes=[pltpu.VMEM((tokens, width), f32)],
        compiler_params=params(),
        cost_estimate=cost(4 * tokens * width * ff, tokens * ff * 4 + width * ff * 4 + tokens * width * 8),
        name="mlp_fwd",
    )(c, gathered, bias, gathered, h1)


def split_rows(value, core, keep_ref, send_ref, chips):
    width = value.shape[1]
    value = value.astype(bf16).reshape(chips, 2, value.shape[0] // chips // 2, width)
    even, odd = value[:, 0], value[:, 1]
    keep_ref[...] = jnp.where(core == 0, even, odd)
    send_ref[...] = jnp.where(core == 0, odd, even)


def mlp_bwd_kernel(pos_ref, dm_ref, c_ref, u_ref, g_ref, fc1_ref, fc2_ref, dc_ref, gb_ref, k1_ref, s1_ref, k2_ref, s2_ref, *, chips):
    step = pl.program_id(0)
    core = pos_ref[2]
    dm = dm_ref[...]
    df32 = dot(dm, square(fc2_ref), 1, 1) * g_ref[...].astype(f32)
    df = df32.astype(bf16)
    gb_ref[...] = jnp.sum(df.astype(f32), axis=0, keepdims=True)
    parts, rows_each = k2_ref.shape[0], k2_ref.shape[2]
    width = dm.shape[1]
    grad2 = dot(u_ref[...], dm, 0, 0).astype(bf16).reshape(2, parts, rows_each, width)
    split_two(grad2, core, k2_ref, s2_ref)
    split_rows(dot(c_ref[...], df, 0, 0), core, k1_ref.at[0], s1_ref.at[0], chips)
    part = dot(df, square(fc1_ref), 1, 1)

    @pl.when(step == 0)
    def _():
        dc_ref[...] = part

    @pl.when(step > 0)
    def _():
        dc_ref[...] += part


def split_two(pair, core, keep_ref, send_ref):
    keep_ref[:, 0] = jnp.where(core == 0, pair[0], pair[1])
    send_ref[:, 0] = jnp.where(core == 0, pair[1], pair[0])


def mlp_bwd(pos, dm, c, u, g, gathered, chips):
    tokens, width = c.shape
    parts, block = gathered.shape[1], width
    ff = parts * block
    rows1, rows2 = width // chips // 2, ff // chips // 2 // parts
    cols = lambda n: pl.BlockSpec((n, block), lambda i, _: (0, i))
    by_part = pl.BlockSpec((1, chips, rows1, block), lambda i, _: (i, 0, 0, 0))
    by_chip = pl.BlockSpec((parts, 1, rows2, width), lambda i, _: (0, i, 0, 0))
    grad1 = jax.ShapeDtypeStruct((parts, chips, rows1, block), bf16)
    grad2 = jax.ShapeDtypeStruct((parts, chips, rows2, width), bf16)
    return pl.pallas_call(
        functools.partial(mlp_bwd_kernel, chips=chips),
        grid_spec=pltpu.PrefetchScalarGridSpec(
            num_scalar_prefetch=1,
            grid=(parts,),
            in_specs=[whole(dm.shape), whole(c.shape), cols(tokens), cols(tokens), *mlp_weight_specs(gathered, width)],
            out_specs=[whole(c.shape), cols(1), by_part, by_part, by_chip, by_chip],
        ),
        out_shape=[jax.ShapeDtypeStruct((tokens, width), f32), jax.ShapeDtypeStruct((1, ff), f32),
                   grad1, grad1, grad2, grad2],
        compiler_params=params(),
        cost_estimate=cost(8 * tokens * width * ff, tokens * ff * 4 + width * ff * 8 + tokens * width * 8),
        name="mlp_bwd",
    )(pos, dm, c, u, g, gathered, gathered)


def qkvo_grad_kernel(pos_ref, a_ref, d_ref, o_ref, dattn_ref, keep_ref, send_ref, *, chips):
    part = pl.program_id(0)
    core = pos_ref[2]

    @pl.when(part < 3)
    def _():
        split_rows(dot(a_ref[...], d_ref[0], 0, 0), core, keep_ref.at[0], send_ref.at[0], chips)

    @pl.when(part == 3)
    def _():
        split_rows(dot(o_ref[...], dattn_ref[...], 0, 0), core, keep_ref.at[0], send_ref.at[0], chips)


def qkvo_grad(pos, a, dqkv, o, dattn, chips):
    tokens, width = a.shape
    each = width // chips // 2
    out = pl.BlockSpec((1, chips, each, width), lambda i, _: (i, 0, 0, 0))
    shape = jax.ShapeDtypeStruct((4, chips, each, width), bf16)
    return pl.pallas_call(
        functools.partial(qkvo_grad_kernel, chips=chips),
        grid_spec=pltpu.PrefetchScalarGridSpec(
            num_scalar_prefetch=1,
            grid=(4,),
            in_specs=[whole(a.shape), pl.BlockSpec((1, tokens, width), lambda i, _: (jnp.minimum(i, 2), 0, 0)),
                      whole(a.shape), whole(a.shape)],
            out_specs=[out, out],
        ),
        out_shape=[shape, shape],
        compiler_params=params(),
        cost_estimate=cost(8 * tokens * width * width, tokens * width * 12 + width * width * 8),
        name="qkvo_grad",
    )(pos, a, dqkv, o, dattn)


def patch_grad_kernel(pos_ref, ext_ref, demb_ref, bias_ref, *refs):
    core = pos_ref[2]
    *vector_refs, keep_ref, send_ref = refs
    parts, _, each, width = keep_ref.shape
    grad = dot(ext_ref[...], demb_ref[...], 0, 0).astype(bf16)
    depth = grad.shape[0] // 2 // parts
    spare = each - depth
    grad = grad.reshape(2, parts, depth, width)
    small = [ref[...] for ref in vector_refs]
    small += [bias_ref[:, i * width : (i + 1) * width] for i in range(bias_ref.shape[1] // width)]
    row = lax.broadcasted_iota(jnp.int32, (spare, width), 0)
    block = jnp.zeros((spare, width), f32)
    for i, value in enumerate(small):
        block = jnp.where(row == i, value, block)
    block = block.astype(bf16)

    def put(ref, value):
        ref[:, 0, :depth, :] = value
        for part in range(parts):
            ref[part, 0, depth:, :] = block

    put(keep_ref, jnp.where(core == 0, grad[0], grad[1]))
    put(send_ref, jnp.where(core == 0, grad[1], grad[0]))


def patch_grad(pos, ext, demb, bias, vectors, parts, chips):
    tokens, depth = ext.shape
    width = demb.shape[1]
    each = depth // (2 * chips) // parts + 16
    out = pl.BlockSpec((parts, 1, each, width), lambda i, _: (0, i, 0, 0))
    shape = jax.ShapeDtypeStruct((parts, chips, each, width), bf16)
    return pl.pallas_call(
        patch_grad_kernel,
        grid_spec=pltpu.PrefetchScalarGridSpec(
            num_scalar_prefetch=1,
            grid=(chips,),
            in_specs=[pl.BlockSpec((tokens, depth // chips), lambda i, _: (0, i)), whole(demb.shape), whole(bias.shape)]
            + [whole(v.shape) for v in vectors],
            out_specs=[out, out],
        ),
        out_shape=[shape, shape],
        compiler_params=params(),
        cost_estimate=cost(2 * tokens * depth * width, ext.size * 2 + demb.size * 2 + depth * width * 2),
        name="patch_grad",
    )(pos, ext, demb, bias, *vectors)


def pixel_grad_kernel(d_ref, w_ref, shown_ref, out_ref):
    out_ref[...] = dot(d_ref[...], square(w_ref), 1, 1) * shown_ref[...]


def pixel_back(dmasked, patch, shown, depth):
    own, width = dmasked.shape
    tb = token_block(own)
    return pl.pallas_call(
        pixel_grad_kernel,
        grid=(own // tb,),
        in_specs=[rows(tb, width), patch_part(patch, depth), rows(tb, 1)],
        out_specs=rows(tb, depth),
        out_shape=jax.ShapeDtypeStruct((own, depth), f32),
        compiler_params=params(),
        cost_estimate=cost(2 * own * depth * width, own * depth * 4 + depth * width * 2),
        name="pixel_back",
    )(dmasked, patch, shown)


def place_kernel(pos_ref, *refs, kinds):
    out_ref = refs[-1]
    z, g, core = pos_ref[0], pos_ref[1], pos_ref[2]
    width = out_ref.shape[3]
    count = len(kinds)
    each = out_ref.shape[2] // count
    for rel in range(2):
        cc = core ^ rel
        mine = refs[rel * (count + 4) : (rel + 1) * (count + 4)]
        for m, kind in enumerate(kinds):
            for part in range(4):
                if kind == "wide":
                    value = mine[m][:, part * width : (part + 1) * width]
                else:
                    value = mine[m][part * each : (part + 1) * each, :]
                out_ref[z * 2 + cc, part, m * each : (m + 1) * each, :] = value
        for turn in range(4):
            for k in range(3):
                out_ref[((z - k - 1) & 3) * 2 + cc, g ^ turn] = mine[count + turn][k]


def place(pos, pieces, others, kinds):
    args = (*pieces, *others)
    shape = (8, 4, pieces[-1].shape[1], pieces[-1].shape[2])
    return pl.pallas_call(
        functools.partial(place_kernel, kinds=kinds),
        grid_spec=pltpu.PrefetchScalarGridSpec(
            num_scalar_prefetch=1,
            grid=(1,),
            in_specs=[whole(p.shape) for p in args],
            out_specs=whole(shape),
        ),
        out_shape=jax.ShapeDtypeStruct(shape, bf16),
        compiler_params=params(),
        cost_estimate=cost(0, 4 * np.prod(shape)),
        name="place",
    )(pos, *args)


def norm_back(dnormed, hidden, gain):
    xhat, rstd = norm_parts(hidden)
    dxhat = dnormed * gain
    mean_d = jnp.mean(dxhat, axis=-1, keepdims=True)
    mean_dx = jnp.mean(dxhat * xhat, axis=-1, keepdims=True)
    grad = rstd * (dxhat - mean_d - xhat * mean_dx)
    return grad, jnp.sum(dnormed * xhat, axis=0, keepdims=True), jnp.sum(dnormed, axis=0, keepdims=True)


def sum_rows(step, ref, part):
    @pl.when(step == 0)
    def _():
        ref[...] = part

    @pl.when(step > 0)
    def _():
        ref[...] += part


def norm2_back_kernel(dc_ref, h1_ref, dh2_ref, gain_ref, w_ref, dh1_ref, da_ref, do_ref, gg_ref, gs_ref):
    step = pl.program_id(0)
    grad, ggain, gshift = norm_back(dc_ref[...], h1_ref[...], gain_ref[2:3, :])
    dh1 = dh2_ref[...] + grad
    dh1_ref[...] = dh1
    dattn = dh1.astype(bf16)
    da_ref[...] = dattn
    do_ref[...] = dot(dattn, square(w_ref), 1, 1).astype(bf16)
    sum_rows(step, gg_ref, ggain)
    sum_rows(step, gs_ref, gshift)


def norm2_back(dc, h1, dh2, gain, proj_w):
    tokens, width = dc.shape
    tb = tokens // 2 if tokens % 32 == 0 else token_block(tokens)
    blk = rows(tb, width)
    vec = whole((1, width))
    return pl.pallas_call(
        norm2_back_kernel,
        grid=(tokens // tb,),
        in_specs=[blk, blk, blk, whole(gain.shape), last_part(proj_w, width)],
        out_specs=[blk, blk, blk, vec, vec],
        out_shape=[jax.ShapeDtypeStruct((tokens, width), f32), jax.ShapeDtypeStruct((tokens, width), bf16),
                   jax.ShapeDtypeStruct((tokens, width), bf16),
                   jax.ShapeDtypeStruct((1, width), f32), jax.ShapeDtypeStruct((1, width), f32)],
        compiler_params=params(),
        cost_estimate=cost(2 * tokens * width * width, tokens * width * 20 + width * width * 2),
        name="norm2_back",
    )(dc, h1, dh2, gain, proj_w)


def norm1_back_kernel(d_ref, w_ref, h0_ref, dh1_ref, gain_ref, de_ref, gg_ref, gs_ref):
    step = pl.program_id(0)
    width = h0_ref.shape[1]
    da = sum(dot(d_ref[p], w_ref[:, p].reshape(width, width), 1, 1) for p in range(3))
    grad, ggain, gshift = norm_back(da, h0_ref[...], gain_ref[0:1, :])
    de_ref[...] = (dh1_ref[...] + grad).astype(bf16)
    sum_rows(step, gg_ref, ggain)
    sum_rows(step, gs_ref, gshift)


def norm1_back(dqkv, qkv_w, h0, dh1, gain):
    tokens, width = h0.shape
    tb = token_block(tokens)
    blk = rows(tb, width)
    vec = whole((1, width))
    return pl.pallas_call(
        norm1_back_kernel,
        grid=(tokens // tb,),
        in_specs=[pl.BlockSpec((3, tb, width), lambda i: (0, i, 0)), pl.BlockSpec((qkv_w.shape[0], 3, width // qkv_w.shape[0], width), lambda i: (0, 0, 0, 0)), blk, blk, whole(gain.shape)],
        out_specs=[blk, vec, vec],
        out_shape=[jax.ShapeDtypeStruct((tokens, width), bf16),
                   jax.ShapeDtypeStruct((1, width), f32), jax.ShapeDtypeStruct((1, width), f32)],
        compiler_params=params(),
        cost_estimate=cost(6 * tokens * width * width, tokens * width * 16 + width * width * 6),
        name="norm1_back",
    )(dqkv, qkv_w, h0, dh1, gain)


def part_slices(side):
    low, own, high = slice(0, MARGIN), slice(MARGIN, MARGIN + side), slice(MARGIN + side, 2 * MARGIN + side)
    return [(own, own), (own, low), (own, high), (low, own), (low, low), (low, high),
            (high, own), (high, low), (high, high)]


@functools.lru_cache(None)
def token_places(dates, side):
    extent = side + 2 * MARGIN
    grid = np.stack(np.meshgrid(np.arange(dates), np.arange(extent), np.arange(extent), indexing="ij"), -1)
    return np.concatenate([grid[:, r, c].reshape(-1, 3) for r, c in part_slices(side)])


@functools.lru_cache(None)
def halo_tables(dates, side):
    places = token_places(dates, side)
    extent = side + 2 * MARGIN
    own = dates * side * side
    edge = dates * side * MARGIN
    index = {tuple(p): i for i, p in enumerate(places)}

    def table(wanted, count):
        out = np.zeros((len(wanted), count), np.float32)
        out[np.arange(len(wanted)), [index[w] for w in wanted]] = 1
        return out

    def shifted(part, dr, dc):
        r, c = part_slices(side)[part]
        grid = np.stack(np.meshgrid(np.arange(dates), np.arange(extent)[r], np.arange(extent)[c], indexing="ij"), -1)
        return [(d, y + dr, x + dc) for d, y, x in grid.reshape(-1, 3)]

    first = table(shifted(1, 0, side) + shifted(2, 0, -side), own)
    north = shifted(3, side, 0) + shifted(4, side, 0) + shifted(5, side, 0)
    south = shifted(6, -side, 0) + shifted(7, -side, 0) + shifted(8, -side, 0)
    second = table(north + south, own + 2 * edge)
    return first, second


def chain(axis, step):
    count = lax.axis_size(axis)
    return [(i, i + step) for i in range(count) if 0 <= i + step < count]


def pick(table, values):
    return lax.dot(jnp.asarray(table, bf16), values, preferred_element_type=f32)


def to_neighbours(low, high, axis):
    return lax.ppermute(low, axis, chain(axis, -1)), lax.ppermute(high, axis, chain(axis, 1))


def margin_first(own, dates, side):
    first, _ = halo_tables(dates, side)
    edge = dates * side * MARGIN
    sent = pick(first, own).astype(bf16)
    return sent[edge:], sent[:edge]


def margin_second(own, right, left, dates, side):
    _, second = halo_tables(dates, side)
    both = dates * side * MARGIN + 2 * dates * MARGIN * MARGIN
    middle = jnp.concatenate([own, left, right])
    sent = pick(second, middle).astype(bf16)
    return middle, sent[both:], sent[:both]


def give_margin_and_sum(own, dates, side, weight, *ready):
    first, second = halo_tables(dates, side)
    edge = dates * side * MARGIN
    corner = dates * MARGIN * MARGIN
    width = own.shape[1]

    def with_rows(strip, values):
        values = values.reshape(1, -1).astype(bf16)
        return jnp.concatenate([strip, jnp.pad(values, ((0, 15), (0, width - values.shape[1])))])

    def values_of(strip, *shape):
        return strip[-16, : np.prod(shape)].reshape(shape).astype(f32)

    sent = pick(first, own).astype(bf16)
    right, left = to_neighbours(with_rows(sent[edge:], weight[:, :MARGIN]), with_rows(sent[:edge], weight[:, -MARGIN:]), "gx")
    right, left, *_ = tied(right, left, *ready)
    extent = side + 2 * MARGIN
    total = weight[:, MARGIN:-MARGIN]
    total = total + jnp.pad(values_of(left, extent, MARGIN), ((0, 0), (0, side - MARGIN)))
    total = total + jnp.pad(values_of(right, extent, MARGIN), ((0, 0), (side - MARGIN, 0)))
    middle = jnp.concatenate([own, left[:edge], right[:edge]])
    sent = pick(second, middle).astype(bf16)
    lower, upper = to_neighbours(with_rows(sent[edge + 2 * corner :], total[:MARGIN]),
                                 with_rows(sent[: edge + 2 * corner], total[-MARGIN:]), "gy")
    total = total[MARGIN:-MARGIN]
    total = total + jnp.pad(values_of(upper, MARGIN, side), ((0, side - MARGIN), (0, 0)))
    total = total + jnp.pad(values_of(lower, MARGIN, side), ((side - MARGIN, 0), (0, 0)))
    return (own, left, right, upper, lower), total


def fold_first(every, dates, side):
    edge = dates * side * MARGIN
    middle = dates * side * side + 2 * edge
    both = edge + 2 * dates * MARGIN * MARGIN
    return every[middle : middle + both], every[middle + both :]


def fold_second(every, below, above, dates, side):
    _, second = halo_tables(dates, side)
    own = dates * side * side
    edge = dates * side * MARGIN
    middle = every[: own + 2 * edge].astype(f32) + pick(second.T, jnp.concatenate([below, above]))
    sides = middle[own:].astype(bf16)
    return middle[:own], sides[:edge], sides[edge:]


def fold_third(part, east, west, dates, side):
    first, _ = halo_tables(dates, side)
    return (part + pick(first.T, jnp.concatenate([east, west]))).astype(bf16)


def sincos(places, span_width):
    half_width = span_width // 2
    omega = 1.0 / 10000.0 ** (jnp.arange(half_width, dtype=f32) / half_width)
    angles = places[:, None] * omega[None, :]
    return jnp.concatenate([jnp.sin(angles), jnp.cos(angles)], axis=1)


def position_parts(tile_row, tile_col, stamps, side, width):
    side_width = width // 16 * 6
    time_width = width - 2 * side_width
    extent = side + 2 * MARGIN
    dates = stamps.shape[0]
    offsets = jnp.arange(extent, dtype=jnp.int32) - MARGIN
    table = jnp.concatenate([
        jnp.pad(sincos(stamps.astype(f32), time_width), ((0, 0), (0, 2 * side_width))),
        jnp.pad(sincos((tile_row * side + offsets).astype(f32), side_width), ((0, 0), (time_width, side_width))),
        jnp.pad(sincos((tile_col * side + offsets).astype(f32), side_width), ((0, 0), (time_width + side_width, 0))),
    ])
    places = token_places(dates, side)
    hot = np.zeros((len(places), dates + 2 * extent), np.float32)
    spots = np.arange(len(places))
    hot[spots, places[:, 0]] = 1
    hot[spots, dates + places[:, 1]] = 1
    hot[spots, dates + extent + places[:, 2]] = 1
    hot = np.concatenate([hot] * 3, axis=1)
    spare = -hot.shape[1] % 128
    hot = np.pad(hot, ((0, 0), (0, spare)))
    parts = jnp.concatenate(three_parts(table))
    return jnp.asarray(hot, bf16), jnp.pad(parts, ((0, spare), (0, 0)))


def dense(left, right, ca=1, cb=0):
    return lax.dot_general(left, right, (((ca,), (cb,)), ((), ())), preferred_element_type=f32)


def gather(shard):
    return lax.all_gather(shard, "gx", axis=0, tiled=True)


def swap(value, axis, bit):
    return lax.ppermute(value, axis, [(i, i ^ bit) for i in range(lax.axis_size(axis))])


def turn(value, step):
    count = lax.axis_size("gx")
    return lax.ppermute(value, "gx", [(i, (i + 2 * step) % count) for i in range(count)])


def after(value, *earlier):
    return lax.optimization_barrier((value, *earlier))[0]


def along_z(mine):
    return jnp.stack([turn(mine, k) for k in (1, 2, 3)])


def tied(*values):
    return lax.optimization_barrier(values)


def along_gy(got):
    return got, swap(got, "gy", 1), swap(got, "gy", 2), swap(got, "gy", 3)


def core_swap(pieces):
    return tuple(swap(p, "gx", 1) for p in pieces)


def added(*values):
    return sum(v.astype(f32) for v in values).astype(bf16)


def at(value, index, axis=0):
    return lax.dynamic_index_in_dim(value, index, axis, keepdims=False)


def folded_gy(value):
    return value.reshape(2, 2, *value.shape[1:])


def near_sum(keep, got, first, g):
    keep, got = folded_gy(keep), folded_gy(got)
    dim, b = (1, g & 1) if first == 1 else (0, g >> 1)
    return added(at(keep, 1 - b, dim), at(got, 1 - b, dim)), added(at(keep, b, dim), at(got, b, dim))


def far_sum(keep, got, first, g):
    b = (g >> 1) if first == 1 else (g & 1)
    return added(at(keep, 1 - b), at(got, 1 - b)), (at(keep, b), at(got, b))


def to_each(keep, got, g):
    return [added(at(keep, g ^ m), at(got, g ^ m)) for m in (1, 2, 3)], (at(keep, g), at(got, g))


def swap_each(values):
    return [swap(v, "gy", m) for v, m in zip(values, (1, 2, 3))]


def scatter_z(mine):
    count = lax.axis_size("gx")
    groups = [list(range(core, count, 2)) for core in range(2)]
    return lax.psum_scatter(mine, "gx", scatter_dimension=0, axis_index_groups=groups, tiled=False)


def along_z_sum(mine, z):
    came = [turn(at(mine, (z + k) % 4), k) for k in (1, 2, 3)]
    return at(mine, z), came


def side_by_side(value):
    half = value.shape[1] // 2
    return jnp.concatenate([value[:, :half], value[:, half:]], axis=2)


def stacked_again(value):
    half = value.shape[1] // 2
    return jnp.concatenate([value[:, :half], value[:, half:]])


def to_all_gy(mine):
    return [mine] + [swap(mine, "gy", m) for m in (1, 2, 3)]


def in_order(every, g):
    every = jnp.stack(every)
    return [at(every, p ^ g) for p in range(4)]


def gather_apart(shard):
    return lax.all_gather(shard, "gx", axis=0, tiled=False)


def collect_all(keep, send, tall):
    both = jnp.stack([keep, send], axis=2)
    parts, chips, _, rows_each, width = both.shape
    if tall:
        grad = both.transpose(1, 2, 0, 3, 4).reshape(-1, width)
    else:
        grad = both.transpose(1, 2, 3, 0, 4).reshape(-1, parts * width)
    grad = lax.psum(scatter(grad), "gy").astype(f32)
    return jnp.split(grad, parts, axis=0 if tall else 1)


def scatter(grad):
    return lax.psum_scatter(grad.astype(bf16), "gx", scatter_dimension=0, tiled=True)


def on_device(pixels, pad_mask, timestamps, scene_dates, scene_map, blend_weight, cotangent, patch_w, norm1_gain,
              norm1_bias, qkv_w, proj_w, norm2_gain, norm2_bias, fc1_w, fc1_b, fc2_w, dec_w, head_w):
    dates, side, _, pixel_width = pixels.shape
    own = dates * side * side
    extent = side + 2 * MARGIN
    places = token_places(dates, side)
    tokens = len(places)
    model_width = patch_w.shape[1]
    scale = float(model_width // HEADS) ** (-0.5)
    tile_row = lax.axis_index("gy")
    tile_col = lax.axis_index("gx")
    split = lax.axis_size("gx") == 8 and lax.axis_size("gy") == 4
    chip, core = (tile_col >> 1, tile_col & 1) if split else (0, 0)
    pos = jnp.stack([jnp.int32(chip), tile_row, jnp.int32(core)]).astype(jnp.int32)

    nearby = lax.dynamic_slice(jnp.pad(scene_map, 1, constant_values=-1), (tile_row, tile_col), (3, 3))
    own_scene = nearby[1, 1]
    bands = np.array([0] * MARGIN + [1] * side + [2] * MARGIN)
    same = (nearby == own_scene)[bands][:, bands].astype(f32)
    weight = blend_weight.astype(f32) * same
    masked = (pixels * pad_mask.astype(bf16)[..., None]).reshape(own, pixel_width)
    each = norm1_gain.shape[0]
    vectors = jnp.concatenate([jnp.stack([norm1_gain, norm1_bias, norm2_gain, norm2_bias]), fc1_b.reshape(-1, each)])
    vectors = jnp.pad(vectors, ((0, 16 - vectors.shape[0]), (0, model_width - each)))
    dec_rows, dec_width = dec_w.shape
    head_rows, slabs = head_w.shape[0], pixel_width // dec_width
    share_p = jnp.concatenate([patch_w, vectors])
    share_a = jnp.concatenate([qkv_w, proj_w], axis=1)
    slabs_of = head_w.reshape(head_rows, slabs, dec_width).transpose(1, 0, 2).reshape(-1, dec_width)
    share_d = jnp.concatenate([dec_w, slabs_of])
    front_p = gather_apart(share_p)
    quarter = patch_w.shape[0] // 4
    parts_of = lambda m: m.reshape(8, model_width // 8, 4, model_width).transpose(0, 2, 1, 3)
    if split:
        row = tile_row
        got_a = along_z(lax.dynamic_slice_in_dim(share_a, row * model_width, model_width, axis=1))
        mine_b = jnp.concatenate([lax.dynamic_slice_in_dim(fc1_w, row * model_width, model_width, axis=1),
                                  lax.dynamic_slice_in_dim(fc2_w, row * each, each, axis=0)])
        strips, denom = give_margin_and_sum(masked, dates, side, weight, got_a)
        got_b = along_z(after(mine_b, front_p, *strips[1:]))
        pieces_a = (share_a, *along_gy(got_a))
        others_a = core_swap(pieces_a)
        share_d = after(share_d, got_b, *pieces_a)
    else:
        strips, denom = give_margin_and_sum(masked, dates, side, weight)
        front_a = parts_of(jnp.concatenate([gather(qkv_w), gather(proj_w)], axis=1))
        quarters_of = lambda m: m.reshape(8, 4, -1, model_width)
        full_mlp = jnp.concatenate([parts_of(gather(fc1_w)), quarters_of(gather(fc2_w))], axis=2)
    small = front_p[:, patch_w.shape[0] :]
    own_dates = scene_dates[own_scene]
    stamps = timestamps[own_scene]
    date_ok = jnp.arange(dates, dtype=jnp.int32) < own_dates
    spot_hot = np.zeros((tokens, extent * extent), np.float32)
    spot_hot[np.arange(tokens), places[:, 1] * extent + places[:, 2]] = 1
    per_token = pick(spot_hot, jnp.stack([weight.reshape(-1), same.reshape(-1)], axis=1).astype(bf16))
    weight_tok = per_token[:, :1]
    seen = per_token[:, 1:] * (jnp.asarray(places[:, :1], jnp.int32) < own_dates).astype(f32)
    lane = np.arange(128)[None, :]
    kx = jnp.where(lane < 3, 1.0, jnp.where(lane == 3, (1.0 - seen) * -1e9, 0.0)).astype(bf16)
    denom = jnp.broadcast_to(denom[None], (dates, side, side)).reshape(own, 1)

    hot, table = position_parts(tile_row, tile_col, stamps, side, model_width)
    small = small[:, :8, :each].astype(f32)
    vec = small[:, :4].transpose(1, 0, 2).reshape(4, -1)
    full_b = small[:, 4:].reshape(1, -1)

    shown = pad_mask.reshape(own, 1).astype(f32)
    valid = (pad_mask.astype(f32) * date_ok.astype(f32)[:, None, None]).reshape(own, 1)
    ratio = valid / denom
    gr = (cotangent.reshape(own, pixel_width).astype(f32) * ratio).astype(bf16)
    ext, h0, a = embed(strips, front_p, hot, table, vec)
    share_d = after(share_d, a)
    tops = gather_apart(share_d)
    full_dec = tops[:, :dec_rows].reshape(-1, dec_width)
    full_head = tops[:, dec_rows:].reshape(-1, slabs, head_rows, dec_width).transpose(0, 2, 1, 3).reshape(-1, pixel_width)
    if split:
        front_a = place(pos, pieces_a, (*others_a[:-1], after(others_a[-1], a)), ("wide",))
        a, got_b = tied(a, got_b)
        pieces_b = (fc1_w, fc2_w, *along_gy(got_b))
    qkv = project(a, front_a, 3)
    o, qx = attn_fwd(qkv, kx, scale)
    if split:
        o, *pieces_b = tied(o, *pieces_b)
        others_b = core_swap(pieces_b)
    h1, c = proj_norm(o, front_a, h0, vec)
    gz = dense(after(gr, c), full_head, 1, 1).astype(bf16)
    west, east = margin_first(gz, dates, side)
    c, west, east = tied(c, west, east)
    right, left = to_neighbours(west, east, "gx")
    if split:
        full_mlp = place(pos, pieces_b, (*others_b[:-1], after(others_b[-1], c)), ("wide", "tall"))
        full_mlp, right, left = tied(full_mlp, right, left)
    middle, north, south = margin_second(gz, right, left, dates, side)
    full_mlp, north, south = tied(full_mlp, north, south)
    lower, upper = to_neighbours(north, south, "gy")
    u, slope, h2r = mlp_fwd(c, full_mlp, full_b, h1)
    z = dense(h2r, full_dec).astype(bf16)
    every = (z.astype(f32) * weight_tok).astype(bf16)
    north, south = fold_first(every, dates, side)
    below, above = to_neighbours(north, south, "gy")

    lower, upper, north, south = tied(lower, upper, north, south)
    dz_every = jnp.concatenate([middle, upper, lower])
    dz = (dz_every.astype(f32) * weight_tok).astype(bf16)
    dh2 = dense(dz, full_dec, 1, 1)
    dm, north, south = tied(dh2.astype(bf16), north, south)
    dc, grad_fc1_b, keep1, send1, keep2, send2 = mlp_bwd(pos, dm, c, u, slope, full_mlp, 4)
    g = tile_row
    if split:
        got1, got2 = swap(send1, "gx", 1), swap(send2, "gx", 1)
    grad_dec = dense(h2r, dz, 0, 0)
    dc, grad_dec = tied(dc, grad_dec.astype(bf16))
    grad_dec = scatter(grad_dec)
    dh1, dattn, do, grad_gain2, grad_shift2 = norm2_back(dc, h1, dh2, vec, front_a)
    below, above, do = tied(below, above, do)
    folded, west, east = fold_second(every, below, above, dates, side)
    do, west, east = tied(do, west, east)
    right, left = to_neighbours(west, east, "gx")
    if split:
        got1, got2 = after(got1, do), after(got2, do)
        out1, keep1 = near_sum(keep1, got1, 1, g)
        out2, keep2 = near_sum(keep2, got2, 2, g)
        do, out1, out2 = tied(do, out1, out2)
        got1, got2 = swap(out1, "gy", 1), swap(out2, "gy", 2)
    dqkv = attn_bwd(qkv, do, o, qx, kx, scale)
    right, left = after(right, dqkv), after(left, dqkv)
    folded = fold_third(folded, right, left, dates, side)
    grad_head = dense(folded, gr, 0, 0)
    dqkv, grad_head = tied(dqkv, grad_head.astype(bf16))
    grad_head = scatter(grad_head)
    if split:
        got1, got2 = after(got1, dqkv), after(got2, dqkv)
        out1, keep1 = far_sum(keep1, got1, 1, g)
        out2, keep2 = far_sum(keep2, got2, 2, g)
        dqkv, out1, out2 = tied(dqkv, out1, out2)
        got1, got2 = swap(out1, "gy", 2), swap(out2, "gy", 1)
    keep3, send3 = qkvo_grad(pos, a, dqkv, o, dattn, 4)
    if split:
        got3 = swap(send3, "gx", 1)
    demb, grad_gain1, grad_shift1 = norm1_back(dqkv, front_a, h0, dh1, vec)
    vectors = (grad_gain1, grad_shift1, grad_gain2, grad_shift2)
    north, south = fold_first(demb, dates, side)
    ends = jnp.concatenate([after(grad_dec, demb), after(grad_head, demb).reshape(-1, dec_width)])
    if split:
        got3, got1, got2 = after(got3, demb), after(got1, demb), after(got2, demb)
        outs3, keep3 = to_each(keep3, got3, g)
        mine1 = jnp.concatenate([added(*keep1, got1), added(*keep2, got2)], axis=1)
        demb, mine1 = tied(demb, mine1)
        done1 = scatter_z(mine1)
        demb, north, south, *outs3 = tied(demb, north, south, *outs3)
    below, above = to_neighbours(north, south, "gy")
    if split:
        got3 = swap_each(outs3)
        keep4, send4 = patch_grad(pos, ext, demb, grad_fc1_b, vectors, 4, 4)
        got4 = swap(send4, "gx", 1)
        got3 = [after(v, keep4) for v in got3]
        mine3 = added(*keep3, *got3)
        below, above, got4 = after(below, mine3), after(above, mine3), after(got4, mine3)
    part, west, east = fold_second(demb, below, above, dates, side)
    right, left = to_neighbours(west, east, "gx")
    if split:
        outs4, keep4 = to_each(keep4, got4, g)
        right, left, *outs4 = tied(right, left, *outs4)
        got4 = swap_each(outs4)
        dmasked = fold_third(part, right, left, dates, side)
        dmasked, done1 = tied(dmasked, done1)
        every1 = to_all_gy(jnp.concatenate([done1, ends.reshape(-1, model_width)]))
        pixel_grad = pixel_back(dmasked, front_p, shown, pixel_width)
        got4 = [after(v, pixel_grad) for v in got4]
        mine4, came4 = along_z_sum(jnp.concatenate([mine3, added(*keep4, *got4)], axis=1), chip)
        folded, mine4 = tied(folded, mine4)
        recon = (dense(folded, full_head) * ratio).astype(bf16)
        came4 = [after(v, recon) for v in came4]
        done4 = added(mine4, *came4)
        every1 = tied(*every1, done4)[:-1]
        every4 = to_all_gy(done4)
        ends = added(*[v[2 * each :] for v in every1]).astype(f32).reshape(-1, dec_width)
        every1 = in_order([v[: 2 * each] for v in every1], g)
        sum1 = jnp.concatenate([v[:each] for v in every1], axis=1).astype(f32)
        sum2 = jnp.concatenate([v[each:] for v in every1], axis=0).astype(f32)
        every4 = tied(*every4, sum1, sum2, ends)[:-3]
        every4 = in_order(every4, g)
        sum1, sum2 = jnp.split(sum1, 4, axis=1), jnp.split(sum2, 4, axis=0)
        sum3 = [v[:each] for v in every4]
        grad_patch = jnp.concatenate([v[each : each + quarter] for v in every4])
        small = every4[0][each + quarter :]
    else:
        recon = (dense(folded, full_head) * ratio).astype(bf16)
        dmasked = fold_third(part, right, left, dates, side)
        sum1, sum2 = collect_all(keep1, send1, False), collect_all(keep2, send2, True)
        sum3 = collect_all(keep3, send3, False)
        pixel_grad = pixel_back(dmasked, front_p, shown, pixel_width)
        grad_patch = lax.psum(scatter(dense(ext, demb, 0, 0)), "gy")
        small = lax.psum(jnp.concatenate([*vectors, grad_fc1_b.reshape(-1, model_width)]), ("gy", "gx"))
        ends = lax.psum(ends, "gy")
    small = small.astype(f32)
    mine_of = lambda value, count: lax.dynamic_slice_in_dim(value.reshape(-1), tile_col * count, count)
    grad_bias = mine_of(small[4 : 4 + full_b.shape[1] // model_width], fc1_b.shape[0])
    return (
        recon.reshape(pixels.shape),
        pixel_grad.reshape(pixels.shape),
        grad_patch.astype(f32),
        mine_of(small[0], each),
        mine_of(small[1], each),
        jnp.concatenate(sum3[:3], axis=1).astype(f32),
        sum3[3].astype(f32),
        mine_of(small[2], each),
        mine_of(small[3], each),
        jnp.concatenate(sum1, axis=1).astype(f32),
        grad_bias,
        jnp.concatenate(sum2, axis=0).astype(f32),
        ends[:dec_rows].astype(f32),
        ends[dec_rows:].reshape(head_rows, pixel_width).astype(f32),
    )


def solution(mesh):
    in_specs = (
        P(None, "gy", "gx", None),
        P(None, "gy", "gx"),
        P(),
        P(),
        P(),
        P("gy", "gx"),
        P(None, "gy", "gx", None),
        P("gx", None),
        P("gx"),
        P("gx"),
        P("gx", None),
        P("gx", None),
        P("gx"),
        P("gx"),
        P("gx", None),
        P("gx"),
        P("gx", None),
        P("gx", None),
        P("gx", None),
    )
    out_specs = (
        P(None, "gy", "gx", None),
        P(None, "gy", "gx", None),
        P("gx", None),
        P("gx"),
        P("gx"),
        P("gx", None),
        P("gx", None),
        P("gx"),
        P("gx"),
        P("gx", None),
        P("gx"),
        P("gx", None),
        P("gx", None),
        P("gx", None),
    )
    return jax.shard_map(
        on_device, mesh=mesh, in_specs=in_specs, out_specs=out_specs, check_vma=False
    )
```

```python
import functools
import jax
import jax.numpy as jnp
import numpy as np
from jax import lax
from jax.experimental import pallas as pl
from jax.experimental.pallas import tpu as pltpu
from jax.sharding import PartitionSpec as P

HEADS = 12
MARGIN = 2
norm_eps = 1e-06
VMEM_BYTES = 56 * 1024 * 1024
f32, bf16 = jnp.float32, jnp.bfloat16


def params():
    return pltpu.CompilerParams(vmem_limit_bytes=VMEM_BYTES)


def cost(flops, nbytes):
    return pl.CostEstimate(flops=int(flops), bytes_accessed=int(nbytes), transcendentals=0)


def dot(a, b, ca=1, cb=0):
    return lax.dot_general(a, b, (((ca,), (cb,)), ((), ())), preferred_element_type=f32)


def whole(shape):
    return pl.BlockSpec(shape, lambda *_: (0,) * len(shape))


def rows(block, width):
    return pl.BlockSpec((block, width), lambda i: (i, 0))


def last_part(gathered, width):
    shares = gathered.shape[0]
    return pl.BlockSpec((shares, 1, width // shares, width), lambda i: (0, 3, 0, 0))


def patch_part(gathered, depth):
    shares, _, width = gathered.shape
    return pl.BlockSpec((shares, depth // shares, width), lambda i: (0, 0, 0))


def square(ref):
    return ref[...].reshape(-1, ref.shape[-1])


def norm_parts(hidden):
    center = jnp.mean(hidden, axis=-1, keepdims=True)
    centered = hidden - center
    spread = jnp.mean(centered * centered, axis=-1, keepdims=True)
    rstd = lax.rsqrt(spread + norm_eps)
    return centered * rstd, rstd


def token_block(tokens):
    for parts in (3, 2):
        if tokens % (16 * parts) == 0:
            return tokens // parts
    return tokens


def embed_kernel(own_ref, left_ref, right_ref, upper_ref, lower_ref, w_ref, pick_ref, table_ref, vec_ref, ext_ref, h0_ref, a_ref, *, pieces):
    refs = (own_ref, left_ref, right_ref, upper_ref, lower_ref)
    for step, held in enumerate(pieces):
        @pl.when(pl.program_id(0) == step)
        def _(held=held):
            spot = 0
            for i, start, count in held:
                ext_ref[spot : spot + count, :] = refs[i][start : start + count, :]
                spot += count
    hidden = dot(ext_ref[...], square(w_ref)) + dot(pick_ref[...], table_ref[...])
    h0_ref[...] = hidden
    xhat, _ = norm_parts(hidden)
    a_ref[...] = (xhat * vec_ref[0:1, :] + vec_ref[1:2, :]).astype(bf16)


def embed(strips, gathered, pick, table, vec):
    tokens = pick.shape[0]
    depth = strips[0].shape[1]
    width = gathered.shape[2]
    tb = token_block(tokens)
    sizes = [strips[0].shape[0]] + [s.shape[0] - 16 for s in strips[1:]]
    pieces, room = [[]], tb
    for i, size in enumerate(sizes):
        start = 0
        while start < size:
            if room == 0:
                pieces.append([])
                room = tb
            count = min(size - start, room)
            pieces[-1].append((i, start, count))
            start, room = start + count, room - count
    return pl.pallas_call(
        functools.partial(embed_kernel, pieces=pieces),
        grid=(tokens // tb,),
        in_specs=[whole(s.shape) for s in strips] + [patch_part(gathered, depth), rows(tb, pick.shape[1]),
                  whole(table.shape), whole(vec.shape)],
        out_specs=[rows(tb, depth), rows(tb, width), rows(tb, width)],
        out_shape=[jax.ShapeDtypeStruct((tokens, depth), bf16), jax.ShapeDtypeStruct((tokens, width), f32),
                   jax.ShapeDtypeStruct((tokens, width), bf16)],
        compiler_params=params(),
        cost_estimate=cost(2 * tokens * depth * width, tokens * depth * 4 + depth * width * 2 + tokens * width * 6),
        name="embed",
    )(*strips, gathered, pick, table, vec)


def columns_kernel(a_ref, w_ref, o_ref):
    o_ref[...] = dot(a_ref[...], square(w_ref)).astype(o_ref.dtype)


def project(a, gathered, count):
    tokens, width = a.shape
    half = width // 2
    return pl.pallas_call(
        columns_kernel,
        grid=(2 * count,),
        in_specs=[whole(a.shape), pl.BlockSpec((gathered.shape[0], 1, width // gathered.shape[0], half), lambda i: (0, i // 2, 0, i % 2))],
        out_specs=pl.BlockSpec((tokens, half), lambda i: (0, i)),
        out_shape=jax.ShapeDtypeStruct((tokens, count * width), bf16),
        compiler_params=params(),
        cost_estimate=cost(2 * tokens * width * width * count, a.size * 2 + width * width * count * 2 + tokens * width * count * 2),
        name="project",
    )(a, gathered)


def three_parts(value):
    first = value.astype(bf16)
    rest = value - first.astype(f32)
    second = rest.astype(bf16)
    third = (rest - second.astype(f32)).astype(bf16)
    return first, second, third


def in_lanes(parts, lane, tail):
    out = tail
    for spot, part in reversed(list(enumerate(parts))):
        out = jnp.where(lane == spot, part.astype(f32), out)
    return out.astype(bf16)


def attn_fwd_kernel(q_ref, k_ref, v_ref, kx_ref, o_ref, qx_ref, *, block, scale):
    tokens, pair = q_ref.shape
    half = pair // 2
    k_aug = jnp.concatenate([k_ref[...], kx_ref[...]], axis=1)
    v_aug = jnp.concatenate([v_ref[...], jnp.ones((tokens, pair), bf16)], axis=1)
    lane = lax.broadcasted_iota(jnp.int32, (block, pair), 1)
    for start in range(0, tokens, block):
        q_blk = q_ref[start : start + block, :].astype(f32) * scale
        outs = []
        for j in range(2):
            mine = (lane >= half) if j else (lane < half)
            q_aug = jnp.concatenate(
                [jnp.where(mine, q_blk, 0.0).astype(bf16),
                 jnp.where(lane == 3, 1.0, 0.0).astype(bf16)], axis=1)
            s = dot(q_aug, k_aug, 1, 1)
            top = jnp.max(s, axis=1, keepdims=True)
            p = jnp.exp(s - top).astype(bf16)
            mixed = dot(p, v_aug)
            total = mixed[:, pair:]
            outs.append(mixed[:, :pair] / total)
            lse = jnp.log(total) + top
            qx_ref[j, start : start + block, :] = in_lanes(
                three_parts(-lse), lane, jnp.where(lane == 3, 1.0, 0.0))
        o_ref[start : start + block, :] = jnp.where(lane < half, outs[0], outs[1]).astype(bf16)


def attn_fwd(qkv, kx, scale):
    tokens = qkv.shape[0]
    width = qkv.shape[1] // 3
    pairs = HEADS // 2
    pw = width // pairs
    spec = lambda part: pl.BlockSpec((tokens, pw), lambda h, part=part: (0, part * pairs + h))
    return pl.pallas_call(
        functools.partial(attn_fwd_kernel, block=token_block(tokens), scale=scale),
        grid=(pairs,),
        in_specs=[spec(0), spec(1), spec(2), whole(kx.shape)],
        out_specs=[pl.BlockSpec((tokens, pw), lambda h: (0, h)),
                   pl.BlockSpec((2, tokens, pw), lambda h: (h, 0, 0))],
        out_shape=[jax.ShapeDtypeStruct((tokens, width), bf16),
                   jax.ShapeDtypeStruct((HEADS, tokens, pw), bf16)],
        compiler_params=params(),
        cost_estimate=cost(2 * 4 * HEADS * tokens * tokens * 256, qkv.size * 2 + tokens * width * 2),
        name="attn_fwd",
    )(qkv, qkv, qkv, kx)


def attn_bwd_kernel(q_ref, k_ref, v_ref, do_ref, o_ref, qx_ref, kx_ref, d_ref, *, block, scale):
    tokens, pair = q_ref.shape
    half = pair // 2
    lane = lax.broadcasted_iota(jnp.int32, (tokens, pair), 1)
    q_all = q_ref[...].astype(f32) * scale
    do_all = do_ref[...].astype(f32)
    prod = do_all * o_ref[...].astype(f32)
    kx = kx_ref[...]
    dq = [None, None]
    dk = [None] * (tokens // block)
    dv = [None] * (tokens // block)
    for j in range(2):
        mine = (lane >= half) if j else (lane < half)
        q_j = jnp.where(mine, q_all, 0.0).astype(bf16)
        do_j = jnp.where(mine, do_all, 0.0).astype(bf16)
        delta = jnp.sum(jnp.where(mine, prod, 0.0), axis=1, keepdims=True)
        dox = in_lanes(three_parts(-delta), lane, jnp.zeros_like(prod))
        q_aug = jnp.concatenate([q_j, qx_ref[j]], axis=1)
        do_aug = jnp.concatenate([do_j, dox], axis=1)
        for b in range(tokens // block):
            at = slice(b * block, (b + 1) * block)
            k_blk = k_ref[at, :]
            sT = dot(jnp.concatenate([k_blk, kx[at]], axis=1), q_aug, 1, 1)
            pT = jnp.exp(sT)
            dpT = dot(jnp.concatenate([v_ref[at, :], kx[at]], axis=1), do_aug, 1, 1)
            dsT = (pT * dpT).astype(bf16)
            dv_b = dot(pT.astype(bf16), do_j)
            dk_b = dot(dsT, q_j)
            dq_b = dot(dsT, k_blk, 0, 0)
            dv[b] = dv_b if dv[b] is None else dv[b] + dv_b
            dk[b] = dk_b if dk[b] is None else dk[b] + dk_b
            dq[j] = dq_b if dq[j] is None else dq[j] + dq_b
    for b in range(tokens // block):
        at = slice(b * block, (b + 1) * block)
        d_ref[1, at, :] = dk[b].astype(bf16)
        d_ref[2, at, :] = dv[b].astype(bf16)
    d_ref[0] = (jnp.where(lane < half, dq[0], dq[1]) * scale).astype(bf16)


def attn_bwd(qkv, do, o, qx, kx, scale):
    tokens = qkv.shape[0]
    width = qkv.shape[1] // 3
    pairs = HEADS // 2
    pw = width // pairs
    spec = lambda part: pl.BlockSpec((tokens, pw), lambda h, part=part: (0, part * pairs + h))
    one = pl.BlockSpec((tokens, pw), lambda h: (0, h))
    return pl.pallas_call(
        functools.partial(attn_bwd_kernel, block=token_block(tokens), scale=scale),
        grid=(pairs,),
        in_specs=[spec(0), spec(1), spec(2), one, one,
                  pl.BlockSpec((2, tokens, pw), lambda h: (h, 0, 0)), whole(kx.shape)],
        out_specs=pl.BlockSpec((3, tokens, pw), lambda h: (0, 0, h)),
        out_shape=jax.ShapeDtypeStruct((3, tokens, width), bf16),
        compiler_params=params(),
        cost_estimate=cost(2 * 5 * HEADS * tokens * tokens * 256, qkv.size * 2 + tokens * width * 10),
        name="attn_bwd",
    )(qkv, qkv, qkv, do, o, qx, kx)


def proj_kernel(o_ref, w_ref, h0_ref, vec_ref, h1_ref, c_ref):
    hidden = h0_ref[...] + dot(o_ref[...], square(w_ref))
    h1_ref[...] = hidden
    xhat, _ = norm_parts(hidden)
    c_ref[...] = (xhat * vec_ref[2:3, :] + vec_ref[3:4, :]).astype(bf16)


def proj_norm(o, proj_w, h0, vec):
    tokens, width = o.shape
    tb = token_block(tokens)
    return pl.pallas_call(
        proj_kernel,
        grid=(tokens // tb,),
        in_specs=[rows(tb, width), last_part(proj_w, width), rows(tb, width), whole(vec.shape)],
        out_specs=[rows(tb, width), rows(tb, width)],
        out_shape=[jax.ShapeDtypeStruct((tokens, width), f32),
                   jax.ShapeDtypeStruct((tokens, width), bf16)],
        compiler_params=params(),
        cost_estimate=cost(2 * tokens * width * width, tokens * width * 12 + width * width * 2),
        name="proj_norm",
    )(o, proj_w, h0, vec)


def mlp_weight_specs(gathered, width):
    shares, parts, _, _ = gathered.shape
    each = width // shares
    return [pl.BlockSpec((shares, 1, each, width), lambda i, *_: (0, i, 0, 0)),
            pl.BlockSpec((shares // parts, parts, each, width), lambda i, *_: (i, 0, 1, 0))]


def mlp_fwd_kernel(c_ref, fc1_ref, b_ref, fc2_ref, h1_ref, u_ref, g_ref, h2_ref, acc_ref):
    step = pl.program_id(0)
    pre = dot(c_ref[...], square(fc1_ref)) + b_ref[...]
    cdf = 0.5 * (1.0 + lax.erf(pre * np.float32(0.5 ** 0.5)))
    act = (pre * cdf).astype(bf16)
    u_ref[...] = act
    g_ref[...] = (cdf + pre * jnp.exp(-0.5 * pre * pre) * np.float32((2 * np.pi) ** -0.5)).astype(bf16)
    part = dot(act, square(fc2_ref))

    @pl.when(step == 0)
    def _():
        acc_ref[...] = h1_ref[...] + part

    @pl.when(step > 0)
    def _():
        acc_ref[...] += part

    @pl.when(step == pl.num_programs(0) - 1)
    def _():
        h2_ref[...] = acc_ref[...].astype(bf16)


def mlp_fwd(c, gathered, bias, h1):
    tokens, width = c.shape
    parts, block = gathered.shape[1], width
    ff = parts * block
    fc1_spec, fc2_spec = mlp_weight_specs(gathered, width)
    cols = lambda n: pl.BlockSpec((n, block), lambda i: (0, i))
    return pl.pallas_call(
        mlp_fwd_kernel,
        grid=(ff // block,),
        in_specs=[whole(c.shape), fc1_spec, cols(1), fc2_spec, whole(h1.shape)],
        out_specs=[cols(tokens), cols(tokens), whole(c.shape)],
        out_shape=[jax.ShapeDtypeStruct((tokens, ff), bf16), jax.ShapeDtypeStruct((tokens, ff), bf16),
                   jax.ShapeDtypeStruct((tokens, width), bf16)],
        scratch_shapes=[pltpu.VMEM((tokens, width), f32)],
        compiler_params=params(),
        cost_estimate=cost(4 * tokens * width * ff, tokens * ff * 4 + width * ff * 4 + tokens * width * 8),
        name="mlp_fwd",
    )(c, gathered, bias, gathered, h1)


def split_rows(value, core, keep_ref, send_ref, chips):
    width = value.shape[1]
    value = value.astype(bf16).reshape(chips, 2, value.shape[0] // chips // 2, width)
    even, odd = value[:, 0], value[:, 1]
    keep_ref[...] = jnp.where(core == 0, even, odd)
    send_ref[...] = jnp.where(core == 0, odd, even)


def mlp_bwd_kernel(pos_ref, dm_ref, c_ref, u_ref, g_ref, fc1_ref, fc2_ref, dc_ref, gb_ref, k1_ref, s1_ref, k2_ref, s2_ref, *, chips):
    step = pl.program_id(0)
    core = pos_ref[2]
    dm = dm_ref[...]
    df32 = dot(dm, square(fc2_ref), 1, 1) * g_ref[...].astype(f32)
    df = df32.astype(bf16)
    gb_ref[...] = jnp.sum(df.astype(f32), axis=0, keepdims=True)
    parts, rows_each = k2_ref.shape[0], k2_ref.shape[2]
    width = dm.shape[1]
    grad2 = dot(u_ref[...], dm, 0, 0).astype(bf16).reshape(2, parts, rows_each, width)
    split_two(grad2, core, k2_ref, s2_ref)
    split_rows(dot(c_ref[...], df, 0, 0), core, k1_ref.at[0], s1_ref.at[0], chips)
    part = dot(df, square(fc1_ref), 1, 1)

    @pl.when(step == 0)
    def _():
        dc_ref[...] = part

    @pl.when(step > 0)
    def _():
        dc_ref[...] += part


def split_two(pair, core, keep_ref, send_ref):
    keep_ref[:, 0] = jnp.where(core == 0, pair[0], pair[1])
    send_ref[:, 0] = jnp.where(core == 0, pair[1], pair[0])


def mlp_bwd(pos, dm, c, u, g, gathered, chips):
    tokens, width = c.shape
    parts, block = gathered.shape[1], width
    ff = parts * block
    rows1, rows2 = width // chips // 2, ff // chips // 2 // parts
    cols = lambda n: pl.BlockSpec((n, block), lambda i, _: (0, i))
    by_part = pl.BlockSpec((1, chips, rows1, block), lambda i, _: (i, 0, 0, 0))
    by_chip = pl.BlockSpec((parts, 1, rows2, width), lambda i, _: (0, i, 0, 0))
    grad1 = jax.ShapeDtypeStruct((parts, chips, rows1, block), bf16)
    grad2 = jax.ShapeDtypeStruct((parts, chips, rows2, width), bf16)
    return pl.pallas_call(
        functools.partial(mlp_bwd_kernel, chips=chips),
        grid_spec=pltpu.PrefetchScalarGridSpec(
            num_scalar_prefetch=1,
            grid=(parts,),
            in_specs=[whole(dm.shape), whole(c.shape), cols(tokens), cols(tokens), *mlp_weight_specs(gathered, width)],
            out_specs=[whole(c.shape), cols(1), by_part, by_part, by_chip, by_chip],
        ),
        out_shape=[jax.ShapeDtypeStruct((tokens, width), f32), jax.ShapeDtypeStruct((1, ff), f32),
                   grad1, grad1, grad2, grad2],
        compiler_params=params(),
        cost_estimate=cost(8 * tokens * width * ff, tokens * ff * 4 + width * ff * 8 + tokens * width * 8),
        name="mlp_bwd",
    )(pos, dm, c, u, g, gathered, gathered)


def qkvo_grad_kernel(pos_ref, a_ref, d_ref, o_ref, dattn_ref, keep_ref, send_ref, *, chips):
    part = pl.program_id(0)
    core = pos_ref[2]

    @pl.when(part < 3)
    def _():
        split_rows(dot(a_ref[...], d_ref[0], 0, 0), core, keep_ref.at[0], send_ref.at[0], chips)

    @pl.when(part == 3)
    def _():
        split_rows(dot(o_ref[...], dattn_ref[...], 0, 0), core, keep_ref.at[0], send_ref.at[0], chips)


def qkvo_grad(pos, a, dqkv, o, dattn, chips):
    tokens, width = a.shape
    each = width // chips // 2
    out = pl.BlockSpec((1, chips, each, width), lambda i, _: (i, 0, 0, 0))
    shape = jax.ShapeDtypeStruct((4, chips, each, width), bf16)
    return pl.pallas_call(
        functools.partial(qkvo_grad_kernel, chips=chips),
        grid_spec=pltpu.PrefetchScalarGridSpec(
            num_scalar_prefetch=1,
            grid=(4,),
            in_specs=[whole(a.shape), pl.BlockSpec((1, tokens, width), lambda i, _: (jnp.minimum(i, 2), 0, 0)),
                      whole(a.shape), whole(a.shape)],
            out_specs=[out, out],
        ),
        out_shape=[shape, shape],
        compiler_params=params(),
        cost_estimate=cost(8 * tokens * width * width, tokens * width * 12 + width * width * 8),
        name="qkvo_grad",
    )(pos, a, dqkv, o, dattn)


def patch_grad_kernel(pos_ref, ext_ref, demb_ref, bias_ref, *refs):
    core = pos_ref[2]
    *vector_refs, keep_ref, send_ref = refs
    parts, _, each, width = keep_ref.shape
    grad = dot(ext_ref[...], demb_ref[...], 0, 0).astype(bf16)
    depth = grad.shape[0] // 2 // parts
    spare = each - depth
    grad = grad.reshape(2, parts, depth, width)
    small = [ref[...] for ref in vector_refs]
    small += [bias_ref[:, i * width : (i + 1) * width] for i in range(bias_ref.shape[1] // width)]
    row = lax.broadcasted_iota(jnp.int32, (spare, width), 0)
    block = jnp.zeros((spare, width), f32)
    for i, value in enumerate(small):
        block = jnp.where(row == i, value, block)
    block = block.astype(bf16)

    def put(ref, value):
        ref[:, 0, :depth, :] = value
        for part in range(parts):
            ref[part, 0, depth:, :] = block

    put(keep_ref, jnp.where(core == 0, grad[0], grad[1]))
    put(send_ref, jnp.where(core == 0, grad[1], grad[0]))


def patch_grad(pos, ext, demb, bias, vectors, parts, chips):
    tokens, depth = ext.shape
    width = demb.shape[1]
    each = depth // (2 * chips) // parts + 16
    out = pl.BlockSpec((parts, 1, each, width), lambda i, _: (0, i, 0, 0))
    shape = jax.ShapeDtypeStruct((parts, chips, each, width), bf16)
    return pl.pallas_call(
        patch_grad_kernel,
        grid_spec=pltpu.PrefetchScalarGridSpec(
            num_scalar_prefetch=1,
            grid=(chips,),
            in_specs=[pl.BlockSpec((tokens, depth // chips), lambda i, _: (0, i)), whole(demb.shape), whole(bias.shape)]
            + [whole(v.shape) for v in vectors],
            out_specs=[out, out],
        ),
        out_shape=[shape, shape],
        compiler_params=params(),
        cost_estimate=cost(2 * tokens * depth * width, ext.size * 2 + demb.size * 2 + depth * width * 2),
        name="patch_grad",
    )(pos, ext, demb, bias, *vectors)


def pixel_grad_kernel(d_ref, w_ref, shown_ref, out_ref):
    out_ref[...] = dot(d_ref[...], square(w_ref), 1, 1) * shown_ref[...]


def pixel_back(dmasked, patch, shown, depth):
    own, width = dmasked.shape
    tb = token_block(own)
    return pl.pallas_call(
        pixel_grad_kernel,
        grid=(own // tb,),
        in_specs=[rows(tb, width), patch_part(patch, depth), rows(tb, 1)],
        out_specs=rows(tb, depth),
        out_shape=jax.ShapeDtypeStruct((own, depth), f32),
        compiler_params=params(),
        cost_estimate=cost(2 * own * depth * width, own * depth * 4 + depth * width * 2),
        name="pixel_back",
    )(dmasked, patch, shown)


def place_kernel(pos_ref, *refs, kinds):
    out_ref = refs[-1]
    z, g, core = pos_ref[0], pos_ref[1], pos_ref[2]
    width = out_ref.shape[3]
    count = len(kinds)
    each = out_ref.shape[2] // count
    for rel in range(2):
        cc = core ^ rel
        mine = refs[rel * (count + 4) : (rel + 1) * (count + 4)]
        for m, kind in enumerate(kinds):
            for part in range(4):
                if kind == "wide":
                    value = mine[m][:, part * width : (part + 1) * width]
                else:
                    value = mine[m][part * each : (part + 1) * each, :]
                out_ref[z * 2 + cc, part, m * each : (m + 1) * each, :] = value
        for turn in range(4):
            for k in range(3):
                out_ref[((z - k - 1) & 3) * 2 + cc, g ^ turn] = mine[count + turn][k]


def place(pos, pieces, others, kinds):
    args = (*pieces, *others)
    shape = (8, 4, pieces[-1].shape[1], pieces[-1].shape[2])
    return pl.pallas_call(
        functools.partial(place_kernel, kinds=kinds),
        grid_spec=pltpu.PrefetchScalarGridSpec(
            num_scalar_prefetch=1,
            grid=(1,),
            in_specs=[whole(p.shape) for p in args],
            out_specs=whole(shape),
        ),
        out_shape=jax.ShapeDtypeStruct(shape, bf16),
        compiler_params=params(),
        cost_estimate=cost(0, 4 * np.prod(shape)),
        name="place",
    )(pos, *args)


def norm_back(dnormed, hidden, gain):
    xhat, rstd = norm_parts(hidden)
    dxhat = dnormed * gain
    mean_d = jnp.mean(dxhat, axis=-1, keepdims=True)
    mean_dx = jnp.mean(dxhat * xhat, axis=-1, keepdims=True)
    grad = rstd * (dxhat - mean_d - xhat * mean_dx)
    return grad, jnp.sum(dnormed * xhat, axis=0, keepdims=True), jnp.sum(dnormed, axis=0, keepdims=True)


def sum_rows(step, ref, part):
    @pl.when(step == 0)
    def _():
        ref[...] = part

    @pl.when(step > 0)
    def _():
        ref[...] += part


def norm2_back_kernel(dc_ref, h1_ref, dh2_ref, gain_ref, w_ref, dh1_ref, da_ref, do_ref, gg_ref, gs_ref):
    step = pl.program_id(0)
    grad, ggain, gshift = norm_back(dc_ref[...], h1_ref[...], gain_ref[2:3, :])
    dh1 = dh2_ref[...] + grad
    dh1_ref[...] = dh1
    dattn = dh1.astype(bf16)
    da_ref[...] = dattn
    do_ref[...] = dot(dattn, square(w_ref), 1, 1).astype(bf16)
    sum_rows(step, gg_ref, ggain)
    sum_rows(step, gs_ref, gshift)


def norm2_back(dc, h1, dh2, gain, proj_w):
    tokens, width = dc.shape
    tb = tokens // 2 if tokens % 32 == 0 else token_block(tokens)
    blk = rows(tb, width)
    vec = whole((1, width))
    return pl.pallas_call(
        norm2_back_kernel,
        grid=(tokens // tb,),
        in_specs=[blk, blk, blk, whole(gain.shape), last_part(proj_w, width)],
        out_specs=[blk, blk, blk, vec, vec],
        out_shape=[jax.ShapeDtypeStruct((tokens, width), f32), jax.ShapeDtypeStruct((tokens, width), bf16),
                   jax.ShapeDtypeStruct((tokens, width), bf16),
                   jax.ShapeDtypeStruct((1, width), f32), jax.ShapeDtypeStruct((1, width), f32)],
        compiler_params=params(),
        cost_estimate=cost(2 * tokens * width * width, tokens * width * 20 + width * width * 2),
        name="norm2_back",
    )(dc, h1, dh2, gain, proj_w)


def norm1_back_kernel(d_ref, w_ref, h0_ref, dh1_ref, gain_ref, de_ref, gg_ref, gs_ref):
    step = pl.program_id(0)
    width = h0_ref.shape[1]
    da = sum(dot(d_ref[p], w_ref[:, p].reshape(width, width), 1, 1) for p in range(3))
    grad, ggain, gshift = norm_back(da, h0_ref[...], gain_ref[0:1, :])
    de_ref[...] = (dh1_ref[...] + grad).astype(bf16)
    sum_rows(step, gg_ref, ggain)
    sum_rows(step, gs_ref, gshift)


def norm1_back(dqkv, qkv_w, h0, dh1, gain):
    tokens, width = h0.shape
    tb = token_block(tokens)
    blk = rows(tb, width)
    vec = whole((1, width))
    return pl.pallas_call(
        norm1_back_kernel,
        grid=(tokens // tb,),
        in_specs=[pl.BlockSpec((3, tb, width), lambda i: (0, i, 0)), pl.BlockSpec((qkv_w.shape[0], 3, width // qkv_w.shape[0], width), lambda i: (0, 0, 0, 0)), blk, blk, whole(gain.shape)],
        out_specs=[blk, vec, vec],
        out_shape=[jax.ShapeDtypeStruct((tokens, width), bf16),
                   jax.ShapeDtypeStruct((1, width), f32), jax.ShapeDtypeStruct((1, width), f32)],
        compiler_params=params(),
        cost_estimate=cost(6 * tokens * width * width, tokens * width * 16 + width * width * 6),
        name="norm1_back",
    )(dqkv, qkv_w, h0, dh1, gain)


def part_slices(side):
    low, own, high = slice(0, MARGIN), slice(MARGIN, MARGIN + side), slice(MARGIN + side, 2 * MARGIN + side)
    return [(own, own), (own, low), (own, high), (low, own), (low, low), (low, high),
            (high, own), (high, low), (high, high)]


@functools.lru_cache(None)
def token_places(dates, side):
    extent = side + 2 * MARGIN
    grid = np.stack(np.meshgrid(np.arange(dates), np.arange(extent), np.arange(extent), indexing="ij"), -1)
    return np.concatenate([grid[:, r, c].reshape(-1, 3) for r, c in part_slices(side)])


@functools.lru_cache(None)
def halo_tables(dates, side):
    places = token_places(dates, side)
    extent = side + 2 * MARGIN
    own = dates * side * side
    edge = dates * side * MARGIN
    index = {tuple(p): i for i, p in enumerate(places)}

    def table(wanted, count):
        out = np.zeros((len(wanted), count), np.float32)
        out[np.arange(len(wanted)), [index[w] for w in wanted]] = 1
        return out

    def shifted(part, dr, dc):
        r, c = part_slices(side)[part]
        grid = np.stack(np.meshgrid(np.arange(dates), np.arange(extent)[r], np.arange(extent)[c], indexing="ij"), -1)
        return [(d, y + dr, x + dc) for d, y, x in grid.reshape(-1, 3)]

    first = table(shifted(1, 0, side) + shifted(2, 0, -side), own)
    north = shifted(3, side, 0) + shifted(4, side, 0) + shifted(5, side, 0)
    south = shifted(6, -side, 0) + shifted(7, -side, 0) + shifted(8, -side, 0)
    second = table(north + south, own + 2 * edge)
    return first, second


def chain(axis, step):
    count = lax.axis_size(axis)
    return [(i, i + step) for i in range(count) if 0 <= i + step < count]


def pick(table, values):
    return lax.dot(jnp.asarray(table, bf16), values, preferred_element_type=f32)


def to_neighbours(low, high, axis):
    return lax.ppermute(low, axis, chain(axis, -1)), lax.ppermute(high, axis, chain(axis, 1))


def margin_first(own, dates, side):
    first, _ = halo_tables(dates, side)
    edge = dates * side * MARGIN
    sent = pick(first, own).astype(bf16)
    return sent[edge:], sent[:edge]


def margin_second(own, right, left, dates, side):
    _, second = halo_tables(dates, side)
    both = dates * side * MARGIN + 2 * dates * MARGIN * MARGIN
    middle = jnp.concatenate([own, left, right])
    sent = pick(second, middle).astype(bf16)
    return middle, sent[both:], sent[:both]


def give_margin_and_sum(own, dates, side, weight, *ready):
    first, second = halo_tables(dates, side)
    edge = dates * side * MARGIN
    corner = dates * MARGIN * MARGIN
    width = own.shape[1]

    def with_rows(strip, values):
        values = values.reshape(1, -1).astype(bf16)
        return jnp.concatenate([strip, jnp.pad(values, ((0, 15), (0, width - values.shape[1])))])

    def values_of(strip, *shape):
        return strip[-16, : np.prod(shape)].reshape(shape).astype(f32)

    sent = pick(first, own).astype(bf16)
    right, left = to_neighbours(with_rows(sent[edge:], weight[:, :MARGIN]), with_rows(sent[:edge], weight[:, -MARGIN:]), "gx")
    right, left, *_ = tied(right, left, *ready)
    extent = side + 2 * MARGIN
    total = weight[:, MARGIN:-MARGIN]
    total = total + jnp.pad(values_of(left, extent, MARGIN), ((0, 0), (0, side - MARGIN)))
    total = total + jnp.pad(values_of(right, extent, MARGIN), ((0, 0), (side - MARGIN, 0)))
    middle = jnp.concatenate([own, left[:edge], right[:edge]])
    sent = pick(second, middle).astype(bf16)
    lower, upper = to_neighbours(with_rows(sent[edge + 2 * corner :], total[:MARGIN]),
                                 with_rows(sent[: edge + 2 * corner], total[-MARGIN:]), "gy")
    total = total[MARGIN:-MARGIN]
    total = total + jnp.pad(values_of(upper, MARGIN, side), ((0, side - MARGIN), (0, 0)))
    total = total + jnp.pad(values_of(lower, MARGIN, side), ((side - MARGIN, 0), (0, 0)))
    return (own, left, right, upper, lower), total


def fold_first(every, dates, side):
    edge = dates * side * MARGIN
    middle = dates * side * side + 2 * edge
    both = edge + 2 * dates * MARGIN * MARGIN
    return every[middle : middle + both], every[middle + both :]


def fold_second(every, below, above, dates, side):
    _, second = halo_tables(dates, side)
    own = dates * side * side
    edge = dates * side * MARGIN
    middle = every[: own + 2 * edge].astype(f32) + pick(second.T, jnp.concatenate([below, above]))
    sides = middle[own:].astype(bf16)
    return middle[:own], sides[:edge], sides[edge:]


def fold_third(part, east, west, dates, side):
    first, _ = halo_tables(dates, side)
    return (part + pick(first.T, jnp.concatenate([east, west]))).astype(bf16)


def sincos(places, span_width):
    half_width = span_width // 2
    omega = 1.0 / 10000.0 ** (jnp.arange(half_width, dtype=f32) / half_width)
    angles = places[:, None] * omega[None, :]
    return jnp.concatenate([jnp.sin(angles), jnp.cos(angles)], axis=1)


def position_parts(tile_row, tile_col, stamps, side, width):
    side_width = width // 16 * 6
    time_width = width - 2 * side_width
    extent = side + 2 * MARGIN
    dates = stamps.shape[0]
    offsets = jnp.arange(extent, dtype=jnp.int32) - MARGIN
    table = jnp.concatenate([
        jnp.pad(sincos(stamps.astype(f32), time_width), ((0, 0), (0, 2 * side_width))),
        jnp.pad(sincos((tile_row * side + offsets).astype(f32), side_width), ((0, 0), (time_width, side_width))),
        jnp.pad(sincos((tile_col * side + offsets).astype(f32), side_width), ((0, 0), (time_width + side_width, 0))),
    ])
    places = token_places(dates, side)
    hot = np.zeros((len(places), dates + 2 * extent), np.float32)
    spots = np.arange(len(places))
    hot[spots, places[:, 0]] = 1
    hot[spots, dates + places[:, 1]] = 1
    hot[spots, dates + extent + places[:, 2]] = 1
    hot = np.concatenate([hot] * 3, axis=1)
    spare = -hot.shape[1] % 128
    hot = np.pad(hot, ((0, 0), (0, spare)))
    parts = jnp.concatenate(three_parts(table))
    return jnp.asarray(hot, bf16), jnp.pad(parts, ((0, spare), (0, 0)))


def dense(left, right, ca=1, cb=0):
    return lax.dot_general(left, right, (((ca,), (cb,)), ((), ())), preferred_element_type=f32)


def gather(shard):
    return lax.all_gather(shard, "gx", axis=0, tiled=True)


def swap(value, axis, bit):
    return lax.ppermute(value, axis, [(i, i ^ bit) for i in range(lax.axis_size(axis))])


def turn(value, step):
    count = lax.axis_size("gx")
    return lax.ppermute(value, "gx", [(i, (i + 2 * step) % count) for i in range(count)])


def after(value, *earlier):
    return lax.optimization_barrier((value, *earlier))[0]


def along_z(mine):
    return jnp.stack([turn(mine, k) for k in (1, 2, 3)])


def tied(*values):
    return lax.optimization_barrier(values)


def along_gy(got):
    return got, swap(got, "gy", 1), swap(got, "gy", 2), swap(got, "gy", 3)


def core_swap(pieces):
    return tuple(swap(p, "gx", 1) for p in pieces)


def added(*values):
    return sum(v.astype(f32) for v in values).astype(bf16)


def at(value, index, axis=0):
    return lax.dynamic_index_in_dim(value, index, axis, keepdims=False)


def folded_gy(value):
    return value.reshape(2, 2, *value.shape[1:])


def near_sum(keep, got, first, g):
    keep, got = folded_gy(keep), folded_gy(got)
    dim, b = (1, g & 1) if first == 1 else (0, g >> 1)
    return added(at(keep, 1 - b, dim), at(got, 1 - b, dim)), added(at(keep, b, dim), at(got, b, dim))


def far_sum(keep, got, first, g):
    b = (g >> 1) if first == 1 else (g & 1)
    return added(at(keep, 1 - b), at(got, 1 - b)), (at(keep, b), at(got, b))


def to_each(keep, got, g):
    return [added(at(keep, g ^ m), at(got, g ^ m)) for m in (1, 2, 3)], (at(keep, g), at(got, g))


def swap_each(values):
    return [swap(v, "gy", m) for v, m in zip(values, (1, 2, 3))]


def scatter_z(mine):
    count = lax.axis_size("gx")
    groups = [list(range(core, count, 2)) for core in range(2)]
    return lax.psum_scatter(mine, "gx", scatter_dimension=0, axis_index_groups=groups, tiled=False)


def along_z_sum(mine, z):
    came = [turn(at(mine, (z + k) % 4), k) for k in (1, 2, 3)]
    return at(mine, z), came


def side_by_side(value):
    half = value.shape[1] // 2
    return jnp.concatenate([value[:, :half], value[:, half:]], axis=2)


def stacked_again(value):
    half = value.shape[1] // 2
    return jnp.concatenate([value[:, :half], value[:, half:]])


def to_all_gy(mine):
    return [mine] + [swap(mine, "gy", m) for m in (1, 2, 3)]


def in_order(every, g):
    every = jnp.stack(every)
    return [at(every, p ^ g) for p in range(4)]


def gather_apart(shard):
    return lax.all_gather(shard, "gx", axis=0, tiled=False)


def collect_all(keep, send, tall):
    both = jnp.stack([keep, send], axis=2)
    parts, chips, _, rows_each, width = both.shape
    if tall:
        grad = both.transpose(1, 2, 0, 3, 4).reshape(-1, width)
    else:
        grad = both.transpose(1, 2, 3, 0, 4).reshape(-1, parts * width)
    grad = lax.psum(scatter(grad), "gy").astype(f32)
    return jnp.split(grad, parts, axis=0 if tall else 1)


def scatter(grad):
    return lax.psum_scatter(grad.astype(bf16), "gx", scatter_dimension=0, tiled=True)


def on_device(pixels, pad_mask, timestamps, scene_dates, scene_map, blend_weight, cotangent, patch_w, norm1_gain,
              norm1_bias, qkv_w, proj_w, norm2_gain, norm2_bias, fc1_w, fc1_b, fc2_w, dec_w, head_w):
    dates, side, _, pixel_width = pixels.shape
    own = dates * side * side
    extent = side + 2 * MARGIN
    places = token_places(dates, side)
    tokens = len(places)
    model_width = patch_w.shape[1]
    scale = float(model_width // HEADS) ** (-0.5)
    tile_row = lax.axis_index("gy")
    tile_col = lax.axis_index("gx")
    split = lax.axis_size("gx") == 8 and lax.axis_size("gy") == 4
    chip, core = (tile_col >> 1, tile_col & 1) if split else (0, 0)
    pos = jnp.stack([jnp.int32(chip), tile_row, jnp.int32(core)]).astype(jnp.int32)

    nearby = lax.dynamic_slice(jnp.pad(scene_map, 1, constant_values=-1), (tile_row, tile_col), (3, 3))
    own_scene = nearby[1, 1]
    bands = np.array([0] * MARGIN + [1] * side + [2] * MARGIN)
    same = (nearby == own_scene)[bands][:, bands].astype(f32)
    weight = blend_weight.astype(f32) * same
    masked = (pixels * pad_mask.astype(bf16)[..., None]).reshape(own, pixel_width)
    each = norm1_gain.shape[0]
    vectors = jnp.concatenate([jnp.stack([norm1_gain, norm1_bias, norm2_gain, norm2_bias]), fc1_b.reshape(-1, each)])
    vectors = jnp.pad(vectors, ((0, 16 - vectors.shape[0]), (0, model_width - each)))
    dec_rows, dec_width = dec_w.shape
    head_rows, slabs = head_w.shape[0], pixel_width // dec_width
    share_p = jnp.concatenate([patch_w, vectors])
    share_a = jnp.concatenate([qkv_w, proj_w], axis=1)
    slabs_of = head_w.reshape(head_rows, slabs, dec_width).transpose(1, 0, 2).reshape(-1, dec_width)
    share_d = jnp.concatenate([dec_w, slabs_of])
    front_p = gather_apart(share_p)
    quarter = patch_w.shape[0] // 4
    parts_of = lambda m: m.reshape(8, model_width // 8, 4, model_width).transpose(0, 2, 1, 3)
    if split:
        row = tile_row
        got_a = along_z(lax.dynamic_slice_in_dim(share_a, row * model_width, model_width, axis=1))
        mine_b = jnp.concatenate([lax.dynamic_slice_in_dim(fc1_w, row * model_width, model_width, axis=1),
                                  lax.dynamic_slice_in_dim(fc2_w, row * each, each, axis=0)])
        strips, denom = give_margin_and_sum(masked, dates, side, weight, got_a)
        got_b = along_z(after(mine_b, front_p, *strips[1:]))
        pieces_a = (share_a, *along_gy(got_a))
        others_a = core_swap(pieces_a)
        share_d = after(share_d, got_b, *pieces_a)
    else:
        strips, denom = give_margin_and_sum(masked, dates, side, weight)
        front_a = parts_of(jnp.concatenate([gather(qkv_w), gather(proj_w)], axis=1))
        quarters_of = lambda m: m.reshape(8, 4, -1, model_width)
        full_mlp = jnp.concatenate([parts_of(gather(fc1_w)), quarters_of(gather(fc2_w))], axis=2)
    small = front_p[:, patch_w.shape[0] :]
    own_dates = scene_dates[own_scene]
    stamps = timestamps[own_scene]
    date_ok = jnp.arange(dates, dtype=jnp.int32) < own_dates
    spot_hot = np.zeros((tokens, extent * extent), np.float32)
    spot_hot[np.arange(tokens), places[:, 1] * extent + places[:, 2]] = 1
    per_token = pick(spot_hot, jnp.stack([weight.reshape(-1), same.reshape(-1)], axis=1).astype(bf16))
    weight_tok = per_token[:, :1]
    seen = per_token[:, 1:] * (jnp.asarray(places[:, :1], jnp.int32) < own_dates).astype(f32)
    lane = np.arange(128)[None, :]
    kx = jnp.where(lane < 3, 1.0, jnp.where(lane == 3, (1.0 - seen) * -1e9, 0.0)).astype(bf16)
    denom = jnp.broadcast_to(denom[None], (dates, side, side)).reshape(own, 1)

    hot, table = position_parts(tile_row, tile_col, stamps, side, model_width)
    small = small[:, :8, :each].astype(f32)
    vec = small[:, :4].transpose(1, 0, 2).reshape(4, -1)
    full_b = small[:, 4:].reshape(1, -1)

    shown = pad_mask.reshape(own, 1).astype(f32)
    valid = (pad_mask.astype(f32) * date_ok.astype(f32)[:, None, None]).reshape(own, 1)
    ratio = valid / denom
    gr = (cotangent.reshape(own, pixel_width).astype(f32) * ratio).astype(bf16)
    ext, h0, a = embed(strips, front_p, hot, table, vec)
    share_d = after(share_d, a)
    tops = gather_apart(share_d)
    full_dec = tops[:, :dec_rows].reshape(-1, dec_width)
    full_head = tops[:, dec_rows:].reshape(-1, slabs, head_rows, dec_width).transpose(0, 2, 1, 3).reshape(-1, pixel_width)
    if split:
        front_a = place(pos, pieces_a, (*others_a[:-1], after(others_a[-1], a)), ("wide",))
        a, got_b = tied(a, got_b)
        pieces_b = (fc1_w, fc2_w, *along_gy(got_b))
    qkv = project(a, front_a, 3)
    o, qx = attn_fwd(qkv, kx, scale)
    gz = dense(after(gr, o), full_head, 1, 1).astype(bf16)
    west, east = margin_first(gz, dates, side)
    o, west, east, full_dec = tied(o, west, east, full_dec)
    right, left = to_neighbours(west, east, "gx")
    if split:
        o, *pieces_b = tied(o, *pieces_b)
        others_b = core_swap(pieces_b)
    h1, c = proj_norm(o, front_a, h0, vec)
    if split:
        full_mlp = place(pos, pieces_b, (*others_b[:-1], after(others_b[-1], c)), ("wide", "tall"))
        full_mlp, right, left = tied(full_mlp, right, left)
    middle, north, south = margin_second(gz, right, left, dates, side)
    full_mlp, north, south = tied(full_mlp, north, south)
    lower, upper = to_neighbours(north, south, "gy")
    u, slope, h2r = mlp_fwd(c, full_mlp, full_b, h1)
    z = dense(h2r, full_dec).astype(bf16)
    every = (z.astype(f32) * weight_tok).astype(bf16)
    north, south = fold_first(every, dates, side)
    below, above = to_neighbours(north, south, "gy")

    lower, upper, north, south = tied(lower, upper, north, south)
    dz_every = jnp.concatenate([middle, upper, lower])
    dz = (dz_every.astype(f32) * weight_tok).astype(bf16)
    dh2 = dense(dz, full_dec, 1, 1)
    dm, north, south = tied(dh2.astype(bf16), north, south)
    dc, grad_fc1_b, keep1, send1, keep2, send2 = mlp_bwd(pos, dm, c, u, slope, full_mlp, 4)
    g = tile_row
    if split:
        got1, got2 = swap(send1, "gx", 1), swap(send2, "gx", 1)
    grad_dec = dense(h2r, dz, 0, 0)
    dc, grad_dec = tied(dc, grad_dec.astype(bf16))
    grad_dec = scatter(grad_dec)
    dh1, dattn, do, grad_gain2, grad_shift2 = norm2_back(dc, h1, dh2, vec, front_a)
    below, above, do = tied(below, above, do)
    folded, west, east = fold_second(every, below, above, dates, side)
    do, west, east = tied(do, west, east)
    right, left = to_neighbours(west, east, "gx")
    if split:
        got1, got2 = after(got1, do), after(got2, do)
        out1, keep1 = near_sum(keep1, got1, 1, g)
        out2, keep2 = near_sum(keep2, got2, 2, g)
        do, out1, out2 = tied(do, out1, out2)
        got1, got2 = swap(out1, "gy", 1), swap(out2, "gy", 2)
    dqkv = attn_bwd(qkv, do, o, qx, kx, scale)
    right, left = after(right, dqkv), after(left, dqkv)
    folded = fold_third(folded, right, left, dates, side)
    grad_head = dense(folded, gr, 0, 0)
    dqkv, grad_head = tied(dqkv, grad_head.astype(bf16))
    grad_head = scatter(grad_head)
    if split:
        got1, got2 = after(got1, dqkv), after(got2, dqkv)
        out1, keep1 = far_sum(keep1, got1, 1, g)
        out2, keep2 = far_sum(keep2, got2, 2, g)
        dqkv, out1, out2 = tied(dqkv, out1, out2)
        got1, got2 = swap(out1, "gy", 2), swap(out2, "gy", 1)
    keep3, send3 = qkvo_grad(pos, a, dqkv, o, dattn, 4)
    if split:
        got3 = swap(send3, "gx", 1)
    demb, grad_gain1, grad_shift1 = norm1_back(dqkv, front_a, h0, dh1, vec)
    vectors = (grad_gain1, grad_shift1, grad_gain2, grad_shift2)
    north, south = fold_first(demb, dates, side)
    ends = jnp.concatenate([after(grad_dec, demb), after(grad_head, demb).reshape(-1, dec_width)])
    if split:
        got3, got1, got2 = after(got3, demb), after(got1, demb), after(got2, demb)
        outs3, keep3 = to_each(keep3, got3, g)
        mine1 = jnp.concatenate([added(*keep1, got1), added(*keep2, got2)], axis=1)
        demb, mine1 = tied(demb, mine1)
        done1 = scatter_z(mine1)
        demb, north, south, *outs3 = tied(demb, north, south, *outs3)
    below, above = to_neighbours(north, south, "gy")
    if split:
        got3 = swap_each(outs3)
        keep4, send4 = patch_grad(pos, ext, demb, grad_fc1_b, vectors, 4, 4)
        got4 = swap(send4, "gx", 1)
        got3 = [after(v, keep4) for v in got3]
        mine3 = added(*keep3, *got3)
        below, above, got4 = after(below, mine3), after(above, mine3), after(got4, mine3)
    part, west, east = fold_second(demb, below, above, dates, side)
    right, left = to_neighbours(west, east, "gx")
    if split:
        outs4, keep4 = to_each(keep4, got4, g)
        right, left, *outs4 = tied(right, left, *outs4)
        got4 = swap_each(outs4)
        dmasked = fold_third(part, right, left, dates, side)
        dmasked, done1 = tied(dmasked, done1)
        every1 = to_all_gy(jnp.concatenate([done1, ends.reshape(-1, model_width)]))
        pixel_grad = pixel_back(dmasked, front_p, shown, pixel_width)
        got4 = [after(v, pixel_grad) for v in got4]
        mine4, came4 = along_z_sum(jnp.concatenate([mine3, added(*keep4, *got4)], axis=1), chip)
        folded, mine4 = tied(folded, mine4)
        recon = (dense(folded, full_head) * ratio).astype(bf16)
        came4 = [after(v, recon) for v in came4]
        done4 = added(mine4, *came4)
        every1 = tied(*every1, done4)[:-1]
        every4 = to_all_gy(done4)
        ends = added(*[v[2 * each :] for v in every1]).astype(f32).reshape(-1, dec_width)
        every1 = in_order([v[: 2 * each] for v in every1], g)
        sum1 = jnp.concatenate([v[:each] for v in every1], axis=1).astype(f32)
        sum2 = jnp.concatenate([v[each:] for v in every1], axis=0).astype(f32)
        every4 = tied(*every4, sum1, sum2, ends)[:-3]
        every4 = in_order(every4, g)
        sum1, sum2 = jnp.split(sum1, 4, axis=1), jnp.split(sum2, 4, axis=0)
        sum3 = [v[:each] for v in every4]
        grad_patch = jnp.concatenate([v[each : each + quarter] for v in every4])
        small = every4[0][each + quarter :]
    else:
        recon = (dense(folded, full_head) * ratio).astype(bf16)
        dmasked = fold_third(part, right, left, dates, side)
        sum1, sum2 = collect_all(keep1, send1, False), collect_all(keep2, send2, True)
        sum3 = collect_all(keep3, send3, False)
        pixel_grad = pixel_back(dmasked, front_p, shown, pixel_width)
        grad_patch = lax.psum(scatter(dense(ext, demb, 0, 0)), "gy")
        small = lax.psum(jnp.concatenate([*vectors, grad_fc1_b.reshape(-1, model_width)]), ("gy", "gx"))
        ends = lax.psum(ends, "gy")
    small = small.astype(f32)
    mine_of = lambda value, count: lax.dynamic_slice_in_dim(value.reshape(-1), tile_col * count, count)
    grad_bias = mine_of(small[4 : 4 + full_b.shape[1] // model_width], fc1_b.shape[0])
    return (
        recon.reshape(pixels.shape),
        pixel_grad.reshape(pixels.shape),
        grad_patch.astype(f32),
        mine_of(small[0], each),
        mine_of(small[1], each),
        jnp.concatenate(sum3[:3], axis=1).astype(f32),
        sum3[3].astype(f32),
        mine_of(small[2], each),
        mine_of(small[3], each),
        jnp.concatenate(sum1, axis=1).astype(f32),
        grad_bias,
        jnp.concatenate(sum2, axis=0).astype(f32),
        ends[:dec_rows].astype(f32),
        ends[dec_rows:].reshape(head_rows, pixel_width).astype(f32),
    )


def solution(mesh):
    in_specs = (
        P(None, "gy", "gx", None),
        P(None, "gy", "gx"),
        P(),
        P(),
        P(),
        P("gy", "gx"),
        P(None, "gy", "gx", None),
        P("gx", None),
        P("gx"),
        P("gx"),
        P("gx", None),
        P("gx", None),
        P("gx"),
        P("gx"),
        P("gx", None),
        P("gx"),
        P("gx", None),
        P("gx", None),
        P("gx", None),
    )
    out_specs = (
        P(None, "gy", "gx", None),
        P(None, "gy", "gx", None),
        P("gx", None),
        P("gx"),
        P("gx"),
        P("gx", None),
        P("gx", None),
        P("gx"),
        P("gx"),
        P("gx", None),
        P("gx"),
        P("gx", None),
        P("gx", None),
        P("gx", None),
    )
    return jax.shard_map(
        on_device, mesh=mesh, in_specs=in_specs, out_specs=out_specs, check_vma=False
    )
```

```python
import functools
import jax
import jax.numpy as jnp
import numpy as np
from jax import lax
from jax.experimental import pallas as pl
from jax.experimental.pallas import tpu as pltpu
from jax.sharding import PartitionSpec as P

HEADS = 12
MARGIN = 2
norm_eps = 1e-06
VMEM_BYTES = 56 * 1024 * 1024
f32, bf16 = jnp.float32, jnp.bfloat16


def params():
    return pltpu.CompilerParams(vmem_limit_bytes=VMEM_BYTES)


def cost(flops, nbytes):
    return pl.CostEstimate(flops=int(flops), bytes_accessed=int(nbytes), transcendentals=0)


def dot(a, b, ca=1, cb=0):
    return lax.dot_general(a, b, (((ca,), (cb,)), ((), ())), preferred_element_type=f32)


def whole(shape):
    return pl.BlockSpec(shape, lambda *_: (0,) * len(shape))


def rows(block, width):
    return pl.BlockSpec((block, width), lambda i: (i, 0))


def last_part(gathered, width):
    shares = gathered.shape[0]
    return pl.BlockSpec((shares, 1, width // shares, width), lambda i: (0, 3, 0, 0))


def patch_part(gathered, depth):
    shares, _, width = gathered.shape
    return pl.BlockSpec((shares, depth // shares, width), lambda i: (0, 0, 0))


def square(ref):
    return ref[...].reshape(-1, ref.shape[-1])


def norm_parts(hidden):
    center = jnp.mean(hidden, axis=-1, keepdims=True)
    centered = hidden - center
    spread = jnp.mean(centered * centered, axis=-1, keepdims=True)
    rstd = lax.rsqrt(spread + norm_eps)
    return centered * rstd, rstd


def token_block(tokens):
    for parts in (3, 2):
        if tokens % (16 * parts) == 0:
            return tokens // parts
    return tokens


def embed_kernel(own_ref, left_ref, right_ref, upper_ref, lower_ref, w_ref, pick_ref, table_ref, vec_ref, ext_ref, h0_ref, a_ref, *, pieces):
    refs = (own_ref, left_ref, right_ref, upper_ref, lower_ref)
    for step, held in enumerate(pieces):
        @pl.when(pl.program_id(0) == step)
        def _(held=held):
            spot = 0
            for i, start, count in held:
                ext_ref[spot : spot + count, :] = refs[i][start : start + count, :]
                spot += count
    hidden = dot(ext_ref[...], square(w_ref)) + dot(pick_ref[...], table_ref[...])
    h0_ref[...] = hidden
    xhat, _ = norm_parts(hidden)
    a_ref[...] = (xhat * vec_ref[0:1, :] + vec_ref[1:2, :]).astype(bf16)


def embed(strips, gathered, pick, table, vec):
    tokens = pick.shape[0]
    depth = strips[0].shape[1]
    width = gathered.shape[2]
    tb = token_block(tokens)
    sizes = [strips[0].shape[0]] + [s.shape[0] - 16 for s in strips[1:]]
    pieces, room = [[]], tb
    for i, size in enumerate(sizes):
        start = 0
        while start < size:
            if room == 0:
                pieces.append([])
                room = tb
            count = min(size - start, room)
            pieces[-1].append((i, start, count))
            start, room = start + count, room - count
    return pl.pallas_call(
        functools.partial(embed_kernel, pieces=pieces),
        grid=(tokens // tb,),
        in_specs=[whole(s.shape) for s in strips] + [patch_part(gathered, depth), rows(tb, pick.shape[1]),
                  whole(table.shape), whole(vec.shape)],
        out_specs=[rows(tb, depth), rows(tb, width), rows(tb, width)],
        out_shape=[jax.ShapeDtypeStruct((tokens, depth), bf16), jax.ShapeDtypeStruct((tokens, width), f32),
                   jax.ShapeDtypeStruct((tokens, width), bf16)],
        compiler_params=params(),
        cost_estimate=cost(2 * tokens * depth * width, tokens * depth * 4 + depth * width * 2 + tokens * width * 6),
        name="embed",
    )(*strips, gathered, pick, table, vec)


def columns_kernel(a_ref, w_ref, o_ref):
    o_ref[...] = dot(a_ref[...], square(w_ref)).astype(o_ref.dtype)


def project(a, gathered, count):
    tokens, width = a.shape
    half = width // 2
    return pl.pallas_call(
        columns_kernel,
        grid=(2 * count,),
        in_specs=[whole(a.shape), pl.BlockSpec((gathered.shape[0], 1, width // gathered.shape[0], half), lambda i: (0, i // 2, 0, i % 2))],
        out_specs=pl.BlockSpec((tokens, half), lambda i: (0, i)),
        out_shape=jax.ShapeDtypeStruct((tokens, count * width), bf16),
        compiler_params=params(),
        cost_estimate=cost(2 * tokens * width * width * count, a.size * 2 + width * width * count * 2 + tokens * width * count * 2),
        name="project",
    )(a, gathered)


def three_parts(value):
    first = value.astype(bf16)
    rest = value - first.astype(f32)
    second = rest.astype(bf16)
    third = (rest - second.astype(f32)).astype(bf16)
    return first, second, third


def in_lanes(parts, lane, tail):
    out = tail
    for spot, part in reversed(list(enumerate(parts))):
        out = jnp.where(lane == spot, part.astype(f32), out)
    return out.astype(bf16)


def attn_fwd_kernel(q_ref, k_ref, v_ref, kx_ref, o_ref, qx_ref, *, block, scale):
    tokens, pair = q_ref.shape
    half = pair // 2
    k_aug = jnp.concatenate([k_ref[...], kx_ref[...]], axis=1)
    v_aug = jnp.concatenate([v_ref[...], jnp.ones((tokens, pair), bf16)], axis=1)
    lane = lax.broadcasted_iota(jnp.int32, (block, pair), 1)
    for start in range(0, tokens, block):
        q_blk = q_ref[start : start + block, :].astype(f32) * scale
        outs = []
        for j in range(2):
            mine = (lane >= half) if j else (lane < half)
            q_aug = jnp.concatenate(
                [jnp.where(mine, q_blk, 0.0).astype(bf16),
                 jnp.where(lane == 3, 1.0, 0.0).astype(bf16)], axis=1)
            s = dot(q_aug, k_aug, 1, 1)
            top = jnp.max(s, axis=1, keepdims=True)
            p = jnp.exp(s - top).astype(bf16)
            mixed = dot(p, v_aug)
            total = mixed[:, pair:]
            outs.append(mixed[:, :pair] / total)
            lse = jnp.log(total) + top
            qx_ref[j, start : start + block, :] = in_lanes(
                three_parts(-lse), lane, jnp.where(lane == 3, 1.0, 0.0))
        o_ref[start : start + block, :] = jnp.where(lane < half, outs[0], outs[1]).astype(bf16)


def attn_fwd(qkv, kx, scale):
    tokens = qkv.shape[0]
    width = qkv.shape[1] // 3
    pairs = HEADS // 2
    pw = width // pairs
    spec = lambda part: pl.BlockSpec((tokens, pw), lambda h, part=part: (0, part * pairs + h))
    return pl.pallas_call(
        functools.partial(attn_fwd_kernel, block=token_block(tokens), scale=scale),
        grid=(pairs,),
        in_specs=[spec(0), spec(1), spec(2), whole(kx.shape)],
        out_specs=[pl.BlockSpec((tokens, pw), lambda h: (0, h)),
                   pl.BlockSpec((2, tokens, pw), lambda h: (h, 0, 0))],
        out_shape=[jax.ShapeDtypeStruct((tokens, width), bf16),
                   jax.ShapeDtypeStruct((HEADS, tokens, pw), bf16)],
        compiler_params=params(),
        cost_estimate=cost(2 * 4 * HEADS * tokens * tokens * 256, qkv.size * 2 + tokens * width * 2),
        name="attn_fwd",
    )(qkv, qkv, qkv, kx)


def attn_bwd_kernel(q_ref, k_ref, v_ref, do_ref, o_ref, qx_ref, kx_ref, d_ref, *, block, scale):
    tokens, pair = q_ref.shape
    half = pair // 2
    lane = lax.broadcasted_iota(jnp.int32, (tokens, pair), 1)
    q_all = q_ref[...].astype(f32) * scale
    do_all = do_ref[...].astype(f32)
    prod = do_all * o_ref[...].astype(f32)
    kx = kx_ref[...]
    dq = [None, None]
    dk = [None] * (tokens // block)
    dv = [None] * (tokens // block)
    for j in range(2):
        mine = (lane >= half) if j else (lane < half)
        q_j = jnp.where(mine, q_all, 0.0).astype(bf16)
        do_j = jnp.where(mine, do_all, 0.0).astype(bf16)
        delta = jnp.sum(jnp.where(mine, prod, 0.0), axis=1, keepdims=True)
        dox = in_lanes(three_parts(-delta), lane, jnp.zeros_like(prod))
        q_aug = jnp.concatenate([q_j, qx_ref[j]], axis=1)
        do_aug = jnp.concatenate([do_j, dox], axis=1)
        for b in range(tokens // block):
            at = slice(b * block, (b + 1) * block)
            k_blk = k_ref[at, :]
            sT = dot(jnp.concatenate([k_blk, kx[at]], axis=1), q_aug, 1, 1)
            pT = jnp.exp(sT)
            dpT = dot(jnp.concatenate([v_ref[at, :], kx[at]], axis=1), do_aug, 1, 1)
            dsT = (pT * dpT).astype(bf16)
            dv_b = dot(pT.astype(bf16), do_j)
            dk_b = dot(dsT, q_j)
            dq_b = dot(dsT, k_blk, 0, 0)
            dv[b] = dv_b if dv[b] is None else dv[b] + dv_b
            dk[b] = dk_b if dk[b] is None else dk[b] + dk_b
            dq[j] = dq_b if dq[j] is None else dq[j] + dq_b
    for b in range(tokens // block):
        at = slice(b * block, (b + 1) * block)
        d_ref[1, at, :] = dk[b].astype(bf16)
        d_ref[2, at, :] = dv[b].astype(bf16)
    d_ref[0] = (jnp.where(lane < half, dq[0], dq[1]) * scale).astype(bf16)


def attn_bwd(qkv, do, o, qx, kx, scale):
    tokens = qkv.shape[0]
    width = qkv.shape[1] // 3
    pairs = HEADS // 2
    pw = width // pairs
    spec = lambda part: pl.BlockSpec((tokens, pw), lambda h, part=part: (0, part * pairs + h))
    one = pl.BlockSpec((tokens, pw), lambda h: (0, h))
    return pl.pallas_call(
        functools.partial(attn_bwd_kernel, block=token_block(tokens), scale=scale),
        grid=(pairs,),
        in_specs=[spec(0), spec(1), spec(2), one, one,
                  pl.BlockSpec((2, tokens, pw), lambda h: (h, 0, 0)), whole(kx.shape)],
        out_specs=pl.BlockSpec((3, tokens, pw), lambda h: (0, 0, h)),
        out_shape=jax.ShapeDtypeStruct((3, tokens, width), bf16),
        compiler_params=params(),
        cost_estimate=cost(2 * 5 * HEADS * tokens * tokens * 256, qkv.size * 2 + tokens * width * 10),
        name="attn_bwd",
    )(qkv, qkv, qkv, do, o, qx, kx)


def proj_kernel(o_ref, w_ref, h0_ref, vec_ref, h1_ref, c_ref):
    hidden = h0_ref[...] + dot(o_ref[...], square(w_ref))
    h1_ref[...] = hidden
    xhat, _ = norm_parts(hidden)
    c_ref[...] = (xhat * vec_ref[2:3, :] + vec_ref[3:4, :]).astype(bf16)


def proj_norm(o, proj_w, h0, vec):
    tokens, width = o.shape
    tb = token_block(tokens)
    return pl.pallas_call(
        proj_kernel,
        grid=(tokens // tb,),
        in_specs=[rows(tb, width), last_part(proj_w, width), rows(tb, width), whole(vec.shape)],
        out_specs=[rows(tb, width), rows(tb, width)],
        out_shape=[jax.ShapeDtypeStruct((tokens, width), f32),
                   jax.ShapeDtypeStruct((tokens, width), bf16)],
        compiler_params=params(),
        cost_estimate=cost(2 * tokens * width * width, tokens * width * 12 + width * width * 2),
        name="proj_norm",
    )(o, proj_w, h0, vec)


def mlp_weight_specs(gathered, width):
    shares, parts, _, _ = gathered.shape
    each = width // shares
    return [pl.BlockSpec((shares, 1, each, width), lambda i, *_: (0, i, 0, 0)),
            pl.BlockSpec((shares // parts, parts, each, width), lambda i, *_: (i, 0, 1, 0))]


def mlp_fwd_kernel(c_ref, fc1_ref, b_ref, fc2_ref, h1_ref, u_ref, g_ref, h2_ref, acc_ref):
    step = pl.program_id(0)
    pre = dot(c_ref[...], square(fc1_ref)) + b_ref[...]
    cdf = 0.5 * (1.0 + lax.erf(pre * np.float32(0.5 ** 0.5)))
    act = (pre * cdf).astype(bf16)
    u_ref[...] = act
    g_ref[...] = (cdf + pre * jnp.exp(-0.5 * pre * pre) * np.float32((2 * np.pi) ** -0.5)).astype(bf16)
    part = dot(act, square(fc2_ref))

    @pl.when(step == 0)
    def _():
        acc_ref[...] = h1_ref[...] + part

    @pl.when(step > 0)
    def _():
        acc_ref[...] += part

    @pl.when(step == pl.num_programs(0) - 1)
    def _():
        h2_ref[...] = acc_ref[...].astype(bf16)


def mlp_fwd(c, gathered, bias, h1):
    tokens, width = c.shape
    parts, block = gathered.shape[1], width
    ff = parts * block
    fc1_spec, fc2_spec = mlp_weight_specs(gathered, width)
    cols = lambda n: pl.BlockSpec((n, block), lambda i: (0, i))
    return pl.pallas_call(
        mlp_fwd_kernel,
        grid=(ff // block,),
        in_specs=[whole(c.shape), fc1_spec, cols(1), fc2_spec, whole(h1.shape)],
        out_specs=[cols(tokens), cols(tokens), whole(c.shape)],
        out_shape=[jax.ShapeDtypeStruct((tokens, ff), bf16), jax.ShapeDtypeStruct((tokens, ff), bf16),
                   jax.ShapeDtypeStruct((tokens, width), bf16)],
        scratch_shapes=[pltpu.VMEM((tokens, width), f32)],
        compiler_params=params(),
        cost_estimate=cost(4 * tokens * width * ff, tokens * ff * 4 + width * ff * 4 + tokens * width * 8),
        name="mlp_fwd",
    )(c, gathered, bias, gathered, h1)


def split_rows(value, core, keep_ref, send_ref, chips):
    width = value.shape[1]
    value = value.astype(bf16).reshape(chips, 2, value.shape[0] // chips // 2, width)
    even, odd = value[:, 0], value[:, 1]
    keep_ref[...] = jnp.where(core == 0, even, odd)
    send_ref[...] = jnp.where(core == 0, odd, even)


def mlp_bwd_kernel(pos_ref, dm_ref, c_ref, u_ref, g_ref, fc1_ref, fc2_ref, dc_ref, gb_ref, k1_ref, s1_ref, k2_ref, s2_ref, *, chips):
    step = pl.program_id(0)
    core = pos_ref[2]
    dm = dm_ref[...]
    df32 = dot(dm, square(fc2_ref), 1, 1) * g_ref[...].astype(f32)
    df = df32.astype(bf16)
    gb_ref[...] = jnp.sum(df.astype(f32), axis=0, keepdims=True)
    parts, rows_each = k2_ref.shape[0], k2_ref.shape[2]
    width = dm.shape[1]
    grad2 = dot(u_ref[...], dm, 0, 0).astype(bf16).reshape(2, parts, rows_each, width)
    split_two(grad2, core, k2_ref, s2_ref)
    split_rows(dot(c_ref[...], df, 0, 0), core, k1_ref.at[0], s1_ref.at[0], chips)
    part = dot(df, square(fc1_ref), 1, 1)

    @pl.when(step == 0)
    def _():
        dc_ref[...] = part

    @pl.when(step > 0)
    def _():
        dc_ref[...] += part


def split_two(pair, core, keep_ref, send_ref):
    keep_ref[:, 0] = jnp.where(core == 0, pair[0], pair[1])
    send_ref[:, 0] = jnp.where(core == 0, pair[1], pair[0])


def mlp_bwd(pos, dm, c, u, g, gathered, chips):
    tokens, width = c.shape
    parts, block = gathered.shape[1], width
    ff = parts * block
    rows1, rows2 = width // chips // 2, ff // chips // 2 // parts
    cols = lambda n: pl.BlockSpec((n, block), lambda i, _: (0, i))
    by_part = pl.BlockSpec((1, chips, rows1, block), lambda i, _: (i, 0, 0, 0))
    by_chip = pl.BlockSpec((parts, 1, rows2, width), lambda i, _: (0, i, 0, 0))
    grad1 = jax.ShapeDtypeStruct((parts, chips, rows1, block), bf16)
    grad2 = jax.ShapeDtypeStruct((parts, chips, rows2, width), bf16)
    return pl.pallas_call(
        functools.partial(mlp_bwd_kernel, chips=chips),
        grid_spec=pltpu.PrefetchScalarGridSpec(
            num_scalar_prefetch=1,
            grid=(parts,),
            in_specs=[whole(dm.shape), whole(c.shape), cols(tokens), cols(tokens), *mlp_weight_specs(gathered, width)],
            out_specs=[whole(c.shape), cols(1), by_part, by_part, by_chip, by_chip],
        ),
        out_shape=[jax.ShapeDtypeStruct((tokens, width), f32), jax.ShapeDtypeStruct((1, ff), f32),
                   grad1, grad1, grad2, grad2],
        compiler_params=params(),
        cost_estimate=cost(8 * tokens * width * ff, tokens * ff * 4 + width * ff * 8 + tokens * width * 8),
        name="mlp_bwd",
    )(pos, dm, c, u, g, gathered, gathered)


def qkvo_grad_kernel(pos_ref, a_ref, d_ref, o_ref, dattn_ref, keep_ref, send_ref, *, chips):
    part = pl.program_id(0)
    core = pos_ref[2]

    @pl.when(part < 3)
    def _():
        split_rows(dot(a_ref[...], d_ref[0], 0, 0), core, keep_ref.at[0], send_ref.at[0], chips)

    @pl.when(part == 3)
    def _():
        split_rows(dot(o_ref[...], dattn_ref[...], 0, 0), core, keep_ref.at[0], send_ref.at[0], chips)


def qkvo_grad(pos, a, dqkv, o, dattn, chips):
    tokens, width = a.shape
    each = width // chips // 2
    out = pl.BlockSpec((1, chips, each, width), lambda i, _: (i, 0, 0, 0))
    shape = jax.ShapeDtypeStruct((4, chips, each, width), bf16)
    return pl.pallas_call(
        functools.partial(qkvo_grad_kernel, chips=chips),
        grid_spec=pltpu.PrefetchScalarGridSpec(
            num_scalar_prefetch=1,
            grid=(4,),
            in_specs=[whole(a.shape), pl.BlockSpec((1, tokens, width), lambda i, _: (jnp.minimum(i, 2), 0, 0)),
                      whole(a.shape), whole(a.shape)],
            out_specs=[out, out],
        ),
        out_shape=[shape, shape],
        compiler_params=params(),
        cost_estimate=cost(8 * tokens * width * width, tokens * width * 12 + width * width * 8),
        name="qkvo_grad",
    )(pos, a, dqkv, o, dattn)


def patch_grad_kernel(pos_ref, ext_ref, demb_ref, bias_ref, *refs):
    core = pos_ref[2]
    *vector_refs, keep_ref, send_ref = refs
    parts, _, each, width = keep_ref.shape
    grad = dot(ext_ref[...], demb_ref[...], 0, 0).astype(bf16)
    depth = grad.shape[0] // 2 // parts
    spare = each - depth
    grad = grad.reshape(2, parts, depth, width)
    small = [ref[...] for ref in vector_refs]
    small += [bias_ref[:, i * width : (i + 1) * width] for i in range(bias_ref.shape[1] // width)]
    row = lax.broadcasted_iota(jnp.int32, (spare, width), 0)
    block = jnp.zeros((spare, width), f32)
    for i, value in enumerate(small):
        block = jnp.where(row == i, value, block)
    block = block.astype(bf16)

    def put(ref, value):
        ref[:, 0, :depth, :] = value
        for part in range(parts):
            ref[part, 0, depth:, :] = block

    put(keep_ref, jnp.where(core == 0, grad[0], grad[1]))
    put(send_ref, jnp.where(core == 0, grad[1], grad[0]))


def patch_grad(pos, ext, demb, bias, vectors, parts, chips):
    tokens, depth = ext.shape
    width = demb.shape[1]
    each = depth // (2 * chips) // parts + 16
    out = pl.BlockSpec((parts, 1, each, width), lambda i, _: (0, i, 0, 0))
    shape = jax.ShapeDtypeStruct((parts, chips, each, width), bf16)
    return pl.pallas_call(
        patch_grad_kernel,
        grid_spec=pltpu.PrefetchScalarGridSpec(
            num_scalar_prefetch=1,
            grid=(chips,),
            in_specs=[pl.BlockSpec((tokens, depth // chips), lambda i, _: (0, i)), whole(demb.shape), whole(bias.shape)]
            + [whole(v.shape) for v in vectors],
            out_specs=[out, out],
        ),
        out_shape=[shape, shape],
        compiler_params=params(),
        cost_estimate=cost(2 * tokens * depth * width, ext.size * 2 + demb.size * 2 + depth * width * 2),
        name="patch_grad",
    )(pos, ext, demb, bias, *vectors)


def pixel_grad_kernel(d_ref, w_ref, shown_ref, out_ref):
    out_ref[...] = dot(d_ref[...], square(w_ref), 1, 1) * shown_ref[...]


def pixel_back(dmasked, patch, shown, depth):
    own, width = dmasked.shape
    tb = token_block(own)
    return pl.pallas_call(
        pixel_grad_kernel,
        grid=(own // tb,),
        in_specs=[rows(tb, width), patch_part(patch, depth), rows(tb, 1)],
        out_specs=rows(tb, depth),
        out_shape=jax.ShapeDtypeStruct((own, depth), f32),
        compiler_params=params(),
        cost_estimate=cost(2 * own * depth * width, own * depth * 4 + depth * width * 2),
        name="pixel_back",
    )(dmasked, patch, shown)


def place_kernel(pos_ref, *refs, kinds):
    out_ref = refs[-1]
    z, g, core = pos_ref[0], pos_ref[1], pos_ref[2]
    width = out_ref.shape[3]
    count = len(kinds)
    each = out_ref.shape[2] // count
    for rel in range(2):
        cc = core ^ rel
        mine = refs[rel * (count + 4) : (rel + 1) * (count + 4)]
        for m, kind in enumerate(kinds):
            for part in range(4):
                if kind == "wide":
                    value = mine[m][:, part * width : (part + 1) * width]
                else:
                    value = mine[m][part * each : (part + 1) * each, :]
                out_ref[z * 2 + cc, part, m * each : (m + 1) * each, :] = value
        for turn in range(4):
            for k in range(3):
                out_ref[((z - k - 1) & 3) * 2 + cc, g ^ turn] = mine[count + turn][k]


def place(pos, pieces, others, kinds):
    args = (*pieces, *others)
    shape = (8, 4, pieces[-1].shape[1], pieces[-1].shape[2])
    return pl.pallas_call(
        functools.partial(place_kernel, kinds=kinds),
        grid_spec=pltpu.PrefetchScalarGridSpec(
            num_scalar_prefetch=1,
            grid=(1,),
            in_specs=[whole(p.shape) for p in args],
            out_specs=whole(shape),
        ),
        out_shape=jax.ShapeDtypeStruct(shape, bf16),
        compiler_params=params(),
        cost_estimate=cost(0, 4 * np.prod(shape)),
        name="place",
    )(pos, *args)


def norm_back(dnormed, hidden, gain):
    xhat, rstd = norm_parts(hidden)
    dxhat = dnormed * gain
    mean_d = jnp.mean(dxhat, axis=-1, keepdims=True)
    mean_dx = jnp.mean(dxhat * xhat, axis=-1, keepdims=True)
    grad = rstd * (dxhat - mean_d - xhat * mean_dx)
    return grad, jnp.sum(dnormed * xhat, axis=0, keepdims=True), jnp.sum(dnormed, axis=0, keepdims=True)


def sum_rows(step, ref, part):
    @pl.when(step == 0)
    def _():
        ref[...] = part

    @pl.when(step > 0)
    def _():
        ref[...] += part


def norm2_back_kernel(dc_ref, h1_ref, dh2_ref, gain_ref, w_ref, dh1_ref, da_ref, do_ref, gg_ref, gs_ref):
    step = pl.program_id(0)
    grad, ggain, gshift = norm_back(dc_ref[...], h1_ref[...], gain_ref[2:3, :])
    dh1 = dh2_ref[...] + grad
    dh1_ref[...] = dh1
    dattn = dh1.astype(bf16)
    da_ref[...] = dattn
    do_ref[...] = dot(dattn, square(w_ref), 1, 1).astype(bf16)
    sum_rows(step, gg_ref, ggain)
    sum_rows(step, gs_ref, gshift)


def norm2_back(dc, h1, dh2, gain, proj_w):
    tokens, width = dc.shape
    tb = tokens // 2 if tokens % 32 == 0 else token_block(tokens)
    blk = rows(tb, width)
    vec = whole((1, width))
    return pl.pallas_call(
        norm2_back_kernel,
        grid=(tokens // tb,),
        in_specs=[blk, blk, blk, whole(gain.shape), last_part(proj_w, width)],
        out_specs=[blk, blk, blk, vec, vec],
        out_shape=[jax.ShapeDtypeStruct((tokens, width), f32), jax.ShapeDtypeStruct((tokens, width), bf16),
                   jax.ShapeDtypeStruct((tokens, width), bf16),
                   jax.ShapeDtypeStruct((1, width), f32), jax.ShapeDtypeStruct((1, width), f32)],
        compiler_params=params(),
        cost_estimate=cost(2 * tokens * width * width, tokens * width * 20 + width * width * 2),
        name="norm2_back",
    )(dc, h1, dh2, gain, proj_w)


def norm1_back_kernel(d_ref, w_ref, h0_ref, dh1_ref, gain_ref, de_ref, gg_ref, gs_ref):
    step = pl.program_id(0)
    width = h0_ref.shape[1]
    da = sum(dot(d_ref[p], w_ref[:, p].reshape(width, width), 1, 1) for p in range(3))
    grad, ggain, gshift = norm_back(da, h0_ref[...], gain_ref[0:1, :])
    de_ref[...] = (dh1_ref[...] + grad).astype(bf16)
    sum_rows(step, gg_ref, ggain)
    sum_rows(step, gs_ref, gshift)


def norm1_back(dqkv, qkv_w, h0, dh1, gain):
    tokens, width = h0.shape
    tb = token_block(tokens)
    blk = rows(tb, width)
    vec = whole((1, width))
    return pl.pallas_call(
        norm1_back_kernel,
        grid=(tokens // tb,),
        in_specs=[pl.BlockSpec((3, tb, width), lambda i: (0, i, 0)), pl.BlockSpec((qkv_w.shape[0], 3, width // qkv_w.shape[0], width), lambda i: (0, 0, 0, 0)), blk, blk, whole(gain.shape)],
        out_specs=[blk, vec, vec],
        out_shape=[jax.ShapeDtypeStruct((tokens, width), bf16),
                   jax.ShapeDtypeStruct((1, width), f32), jax.ShapeDtypeStruct((1, width), f32)],
        compiler_params=params(),
        cost_estimate=cost(6 * tokens * width * width, tokens * width * 16 + width * width * 6),
        name="norm1_back",
    )(dqkv, qkv_w, h0, dh1, gain)


def part_slices(side):
    low, own, high = slice(0, MARGIN), slice(MARGIN, MARGIN + side), slice(MARGIN + side, 2 * MARGIN + side)
    return [(own, own), (own, low), (own, high), (low, own), (low, low), (low, high),
            (high, own), (high, low), (high, high)]


@functools.lru_cache(None)
def token_places(dates, side):
    extent = side + 2 * MARGIN
    grid = np.stack(np.meshgrid(np.arange(dates), np.arange(extent), np.arange(extent), indexing="ij"), -1)
    return np.concatenate([grid[:, r, c].reshape(-1, 3) for r, c in part_slices(side)])


@functools.lru_cache(None)
def halo_tables(dates, side):
    places = token_places(dates, side)
    extent = side + 2 * MARGIN
    own = dates * side * side
    edge = dates * side * MARGIN
    index = {tuple(p): i for i, p in enumerate(places)}

    def table(wanted, count):
        out = np.zeros((len(wanted), count), np.float32)
        out[np.arange(len(wanted)), [index[w] for w in wanted]] = 1
        return out

    def shifted(part, dr, dc):
        r, c = part_slices(side)[part]
        grid = np.stack(np.meshgrid(np.arange(dates), np.arange(extent)[r], np.arange(extent)[c], indexing="ij"), -1)
        return [(d, y + dr, x + dc) for d, y, x in grid.reshape(-1, 3)]

    first = table(shifted(1, 0, side) + shifted(2, 0, -side), own)
    north = shifted(3, side, 0) + shifted(4, side, 0) + shifted(5, side, 0)
    south = shifted(6, -side, 0) + shifted(7, -side, 0) + shifted(8, -side, 0)
    second = table(north + south, own + 2 * edge)
    return first, second


def chain(axis, step):
    count = lax.axis_size(axis)
    return [(i, i + step) for i in range(count) if 0 <= i + step < count]


def pick(table, values):
    return lax.dot(jnp.asarray(table, bf16), values, preferred_element_type=f32)


def to_neighbours(low, high, axis):
    return lax.ppermute(low, axis, chain(axis, -1)), lax.ppermute(high, axis, chain(axis, 1))


def margin_first(own, dates, side):
    first, _ = halo_tables(dates, side)
    edge = dates * side * MARGIN
    sent = pick(first, own).astype(bf16)
    return sent[edge:], sent[:edge]


def margin_second(own, right, left, dates, side):
    _, second = halo_tables(dates, side)
    both = dates * side * MARGIN + 2 * dates * MARGIN * MARGIN
    middle = jnp.concatenate([own, left, right])
    sent = pick(second, middle).astype(bf16)
    return middle, sent[both:], sent[:both]


def give_margin_and_sum(own, dates, side, weight, *ready):
    first, second = halo_tables(dates, side)
    edge = dates * side * MARGIN
    corner = dates * MARGIN * MARGIN
    width = own.shape[1]

    def with_rows(strip, values):
        values = values.reshape(1, -1).astype(bf16)
        return jnp.concatenate([strip, jnp.pad(values, ((0, 15), (0, width - values.shape[1])))])

    def values_of(strip, *shape):
        return strip[-16, : np.prod(shape)].reshape(shape).astype(f32)

    sent = pick(first, own).astype(bf16)
    right, left = to_neighbours(with_rows(sent[edge:], weight[:, :MARGIN]), with_rows(sent[:edge], weight[:, -MARGIN:]), "gx")
    right, left, *_ = tied(right, left, *ready)
    extent = side + 2 * MARGIN
    total = weight[:, MARGIN:-MARGIN]
    total = total + jnp.pad(values_of(left, extent, MARGIN), ((0, 0), (0, side - MARGIN)))
    total = total + jnp.pad(values_of(right, extent, MARGIN), ((0, 0), (side - MARGIN, 0)))
    middle = jnp.concatenate([own, left[:edge], right[:edge]])
    sent = pick(second, middle).astype(bf16)
    lower, upper = to_neighbours(with_rows(sent[edge + 2 * corner :], total[:MARGIN]),
                                 with_rows(sent[: edge + 2 * corner], total[-MARGIN:]), "gy")
    total = total[MARGIN:-MARGIN]
    total = total + jnp.pad(values_of(upper, MARGIN, side), ((0, side - MARGIN), (0, 0)))
    total = total + jnp.pad(values_of(lower, MARGIN, side), ((side - MARGIN, 0), (0, 0)))
    return (own, left, right, upper, lower), total


def fold_first(every, dates, side):
    edge = dates * side * MARGIN
    middle = dates * side * side + 2 * edge
    both = edge + 2 * dates * MARGIN * MARGIN
    return every[middle : middle + both], every[middle + both :]


def fold_second(every, below, above, dates, side):
    _, second = halo_tables(dates, side)
    own = dates * side * side
    edge = dates * side * MARGIN
    middle = every[: own + 2 * edge].astype(f32) + pick(second.T, jnp.concatenate([below, above]))
    sides = middle[own:].astype(bf16)
    return middle[:own], sides[:edge], sides[edge:]


def fold_third(part, east, west, dates, side):
    first, _ = halo_tables(dates, side)
    return (part + pick(first.T, jnp.concatenate([east, west]))).astype(bf16)


def sincos(places, span_width):
    half_width = span_width // 2
    omega = 1.0 / 10000.0 ** (jnp.arange(half_width, dtype=f32) / half_width)
    angles = places[:, None] * omega[None, :]
    return jnp.concatenate([jnp.sin(angles), jnp.cos(angles)], axis=1)


def position_parts(tile_row, tile_col, stamps, side, width):
    side_width = width // 16 * 6
    time_width = width - 2 * side_width
    extent = side + 2 * MARGIN
    dates = stamps.shape[0]
    offsets = jnp.arange(extent, dtype=jnp.int32) - MARGIN
    table = jnp.concatenate([
        jnp.pad(sincos(stamps.astype(f32), time_width), ((0, 0), (0, 2 * side_width))),
        jnp.pad(sincos((tile_row * side + offsets).astype(f32), side_width), ((0, 0), (time_width, side_width))),
        jnp.pad(sincos((tile_col * side + offsets).astype(f32), side_width), ((0, 0), (time_width + side_width, 0))),
    ])
    places = token_places(dates, side)
    hot = np.zeros((len(places), dates + 2 * extent), np.float32)
    spots = np.arange(len(places))
    hot[spots, places[:, 0]] = 1
    hot[spots, dates + places[:, 1]] = 1
    hot[spots, dates + extent + places[:, 2]] = 1
    hot = np.concatenate([hot] * 3, axis=1)
    spare = -hot.shape[1] % 128
    hot = np.pad(hot, ((0, 0), (0, spare)))
    parts = jnp.concatenate(three_parts(table))
    return jnp.asarray(hot, bf16), jnp.pad(parts, ((0, spare), (0, 0)))


def dense(left, right, ca=1, cb=0):
    return lax.dot_general(left, right, (((ca,), (cb,)), ((), ())), preferred_element_type=f32)


def gather(shard):
    return lax.all_gather(shard, "gx", axis=0, tiled=True)


def swap(value, axis, bit):
    return lax.ppermute(value, axis, [(i, i ^ bit) for i in range(lax.axis_size(axis))])


def turn(value, step):
    count = lax.axis_size("gx")
    return lax.ppermute(value, "gx", [(i, (i + 2 * step) % count) for i in range(count)])


def after(value, *earlier):
    return lax.optimization_barrier((value, *earlier))[0]


def along_z(mine):
    return jnp.stack([turn(mine, k) for k in (1, 2, 3)])


def tied(*values):
    return lax.optimization_barrier(values)


def along_gy(got):
    return got, swap(got, "gy", 1), swap(got, "gy", 2), swap(got, "gy", 3)


def core_swap(pieces):
    return tuple(swap(p, "gx", 1) for p in pieces)


def added(*values):
    return sum(v.astype(f32) for v in values).astype(bf16)


def at(value, index, axis=0):
    return lax.dynamic_index_in_dim(value, index, axis, keepdims=False)


def folded_gy(value):
    return value.reshape(2, 2, *value.shape[1:])


def near_sum(keep, got, first, g):
    keep, got = folded_gy(keep), folded_gy(got)
    dim, b = (1, g & 1) if first == 1 else (0, g >> 1)
    return added(at(keep, 1 - b, dim), at(got, 1 - b, dim)), added(at(keep, b, dim), at(got, b, dim))


def far_sum(keep, got, first, g):
    b = (g >> 1) if first == 1 else (g & 1)
    return added(at(keep, 1 - b), at(got, 1 - b)), (at(keep, b), at(got, b))


def to_each(keep, got, g):
    return [added(at(keep, g ^ m), at(got, g ^ m)) for m in (1, 2, 3)], (at(keep, g), at(got, g))


def swap_each(values):
    return [swap(v, "gy", m) for v, m in zip(values, (1, 2, 3))]


def scatter_z(mine):
    count = lax.axis_size("gx")
    groups = [list(range(core, count, 2)) for core in range(2)]
    return lax.psum_scatter(mine, "gx", scatter_dimension=0, axis_index_groups=groups, tiled=False)


def along_z_sum(mine, z):
    came = [turn(at(mine, (z + k) % 4), k) for k in (1, 2, 3)]
    return at(mine, z), came


def side_by_side(value):
    half = value.shape[1] // 2
    return jnp.concatenate([value[:, :half], value[:, half:]], axis=2)


def stacked_again(value):
    half = value.shape[1] // 2
    return jnp.concatenate([value[:, :half], value[:, half:]])


def to_all_gy(mine):
    return [mine] + [swap(mine, "gy", m) for m in (1, 2, 3)]


def in_order(every, g):
    every = jnp.stack(every)
    return [at(every, p ^ g) for p in range(4)]


def gather_apart(shard):
    return lax.all_gather(shard, "gx", axis=0, tiled=False)


def collect_all(keep, send, tall):
    both = jnp.stack([keep, send], axis=2)
    parts, chips, _, rows_each, width = both.shape
    if tall:
        grad = both.transpose(1, 2, 0, 3, 4).reshape(-1, width)
    else:
        grad = both.transpose(1, 2, 3, 0, 4).reshape(-1, parts * width)
    grad = lax.psum(scatter(grad), "gy").astype(f32)
    return jnp.split(grad, parts, axis=0 if tall else 1)


def scatter(grad):
    return lax.psum_scatter(grad.astype(bf16), "gx", scatter_dimension=0, tiled=True)


def on_device(pixels, pad_mask, timestamps, scene_dates, scene_map, blend_weight, cotangent, patch_w, norm1_gain,
              norm1_bias, qkv_w, proj_w, norm2_gain, norm2_bias, fc1_w, fc1_b, fc2_w, dec_w, head_w):
    dates, side, _, pixel_width = pixels.shape
    own = dates * side * side
    extent = side + 2 * MARGIN
    places = token_places(dates, side)
    tokens = len(places)
    model_width = patch_w.shape[1]
    scale = float(model_width // HEADS) ** (-0.5)
    tile_row = lax.axis_index("gy")
    tile_col = lax.axis_index("gx")
    split = lax.axis_size("gx") == 8 and lax.axis_size("gy") == 4
    chip, core = (tile_col >> 1, tile_col & 1) if split else (0, 0)
    pos = jnp.stack([jnp.int32(chip), tile_row, jnp.int32(core)]).astype(jnp.int32)

    nearby = lax.dynamic_slice(jnp.pad(scene_map, 1, constant_values=-1), (tile_row, tile_col), (3, 3))
    own_scene = nearby[1, 1]
    bands = np.array([0] * MARGIN + [1] * side + [2] * MARGIN)
    same = (nearby == own_scene)[bands][:, bands].astype(f32)
    weight = blend_weight.astype(f32) * same
    masked = (pixels * pad_mask.astype(bf16)[..., None]).reshape(own, pixel_width)
    each = norm1_gain.shape[0]
    vectors = jnp.concatenate([jnp.stack([norm1_gain, norm1_bias, norm2_gain, norm2_bias]), fc1_b.reshape(-1, each)])
    vectors = jnp.pad(vectors, ((0, 16 - vectors.shape[0]), (0, model_width - each)))
    dec_rows, dec_width = dec_w.shape
    head_rows, slabs = head_w.shape[0], pixel_width // dec_width
    share_p = jnp.concatenate([patch_w, vectors])
    share_a = jnp.concatenate([qkv_w, proj_w], axis=1)
    slabs_of = head_w.reshape(head_rows, slabs, dec_width).transpose(1, 0, 2).reshape(-1, dec_width)
    share_d = jnp.concatenate([dec_w, slabs_of])
    front_p = gather_apart(share_p)
    quarter = patch_w.shape[0] // 4
    parts_of = lambda m: m.reshape(8, model_width // 8, 4, model_width).transpose(0, 2, 1, 3)
    if split:
        row = tile_row
        got_a = along_z(lax.dynamic_slice_in_dim(share_a, row * model_width, model_width, axis=1))
        mine_b = jnp.concatenate([lax.dynamic_slice_in_dim(fc1_w, row * model_width, model_width, axis=1),
                                  lax.dynamic_slice_in_dim(fc2_w, row * each, each, axis=0)])
        strips, denom = give_margin_and_sum(masked, dates, side, weight, got_a)
        got_b = along_z(after(mine_b, front_p, *strips[1:]))
        pieces_a = (share_a, *along_gy(got_a))
        others_a = core_swap(pieces_a)
        share_d = after(share_d, got_b, *pieces_a)
    else:
        strips, denom = give_margin_and_sum(masked, dates, side, weight)
        front_a = parts_of(jnp.concatenate([gather(qkv_w), gather(proj_w)], axis=1))
        quarters_of = lambda m: m.reshape(8, 4, -1, model_width)
        full_mlp = jnp.concatenate([parts_of(gather(fc1_w)), quarters_of(gather(fc2_w))], axis=2)
    small = front_p[:, patch_w.shape[0] :]
    own_dates = scene_dates[own_scene]
    stamps = timestamps[own_scene]
    date_ok = jnp.arange(dates, dtype=jnp.int32) < own_dates
    spot_hot = np.zeros((tokens, extent * extent), np.float32)
    spot_hot[np.arange(tokens), places[:, 1] * extent + places[:, 2]] = 1
    per_token = pick(spot_hot, jnp.stack([weight.reshape(-1), same.reshape(-1)], axis=1).astype(bf16))
    weight_tok = per_token[:, :1]
    seen = per_token[:, 1:] * (jnp.asarray(places[:, :1], jnp.int32) < own_dates).astype(f32)
    lane = np.arange(128)[None, :]
    kx = jnp.where(lane < 3, 1.0, jnp.where(lane == 3, (1.0 - seen) * -1e9, 0.0)).astype(bf16)
    denom = jnp.broadcast_to(denom[None], (dates, side, side)).reshape(own, 1)

    hot, table = position_parts(tile_row, tile_col, stamps, side, model_width)
    small = small[:, :8, :each].astype(f32)
    vec = small[:, :4].transpose(1, 0, 2).reshape(4, -1)
    full_b = small[:, 4:].reshape(1, -1)

    shown = pad_mask.reshape(own, 1).astype(f32)
    valid = (pad_mask.astype(f32) * date_ok.astype(f32)[:, None, None]).reshape(own, 1)
    ratio = valid / denom
    gr = (cotangent.reshape(own, pixel_width).astype(f32) * ratio).astype(bf16)
    ext, h0, a = embed(strips, front_p, hot, table, vec)
    share_d = after(share_d, a)
    tops = gather_apart(share_d)
    full_dec = tops[:, :dec_rows].reshape(-1, dec_width)
    full_head = tops[:, dec_rows:].reshape(-1, slabs, head_rows, dec_width).transpose(0, 2, 1, 3).reshape(-1, pixel_width)
    if split:
        front_a = place(pos, pieces_a, (*others_a[:-1], after(others_a[-1], a)), ("wide",))
        a, got_b = tied(a, got_b)
        pieces_b = (fc1_w, fc2_w, *along_gy(got_b))
    qkv = project(a, front_a, 3)
    o, qx = attn_fwd(qkv, kx, scale)
    gz = dense(after(gr, o), full_head, 1, 1).astype(bf16)
    west, east = margin_first(gz, dates, side)
    o, west, east, full_dec = tied(o, west, east, full_dec)
    right, left = to_neighbours(west, east, "gx")
    if split:
        o, *pieces_b = tied(o, *pieces_b)
        others_b = core_swap(pieces_b)
    h1, c = proj_norm(o, front_a, h0, vec)
    if split:
        full_mlp = place(pos, pieces_b, (*others_b[:-1], after(others_b[-1], c)), ("wide", "tall"))
        full_mlp, right, left = tied(full_mlp, right, left)
    middle, north, south = margin_second(gz, right, left, dates, side)
    full_mlp, north, south = tied(full_mlp, north, south)
    lower, upper = to_neighbours(north, south, "gy")
    u, slope, h2r = mlp_fwd(c, full_mlp, full_b, h1)
    lower, upper, h2r = tied(lower, upper, h2r)
    z = dense(h2r, full_dec).astype(bf16)
    every = (z.astype(f32) * weight_tok).astype(bf16)
    north, south = fold_first(every, dates, side)
    below, above = to_neighbours(north, south, "gy")

    dz_every = jnp.concatenate([middle, upper, lower])
    dz = (dz_every.astype(f32) * weight_tok).astype(bf16)
    dh2 = dense(dz, full_dec, 1, 1)
    dm, north, south = tied(dh2.astype(bf16), north, south)
    dc, grad_fc1_b, keep1, send1, keep2, send2 = mlp_bwd(pos, dm, c, u, slope, full_mlp, 4)
    g = tile_row
    if split:
        got1, got2 = swap(send1, "gx", 1), swap(send2, "gx", 1)
    grad_dec = dense(h2r, dz, 0, 0)
    dc, grad_dec = tied(dc, grad_dec.astype(bf16))
    grad_dec = scatter(grad_dec)
    dh1, dattn, do, grad_gain2, grad_shift2 = norm2_back(dc, h1, dh2, vec, front_a)
    below, above, do = tied(below, above, do)
    folded, west, east = fold_second(every, below, above, dates, side)
    do, west, east = tied(do, west, east)
    right, left = to_neighbours(west, east, "gx")
    if split:
        got1, got2 = after(got1, do), after(got2, do)
        out1, keep1 = near_sum(keep1, got1, 1, g)
        out2, keep2 = near_sum(keep2, got2, 2, g)
        do, out1, out2 = tied(do, out1, out2)
        got1, got2 = swap(out1, "gy", 1), swap(out2, "gy", 2)
    dqkv = attn_bwd(qkv, do, o, qx, kx, scale)
    right, left = after(right, dqkv), after(left, dqkv)
    folded = fold_third(folded, right, left, dates, side)
    grad_head = dense(folded, gr, 0, 0)
    dqkv, grad_head = tied(dqkv, grad_head.astype(bf16))
    grad_head = scatter(grad_head)
    if split:
        got1, got2 = after(got1, dqkv), after(got2, dqkv)
        out1, keep1 = far_sum(keep1, got1, 1, g)
        out2, keep2 = far_sum(keep2, got2, 2, g)
        dqkv, out1, out2 = tied(dqkv, out1, out2)
        got1, got2 = swap(out1, "gy", 2), swap(out2, "gy", 1)
    keep3, send3 = qkvo_grad(pos, a, dqkv, o, dattn, 4)
    if split:
        got3 = swap(send3, "gx", 1)
    demb, grad_gain1, grad_shift1 = norm1_back(dqkv, front_a, h0, dh1, vec)
    vectors = (grad_gain1, grad_shift1, grad_gain2, grad_shift2)
    north, south = fold_first(demb, dates, side)
    ends = jnp.concatenate([after(grad_dec, demb), after(grad_head, demb).reshape(-1, dec_width)])
    if split:
        got3, got1, got2 = after(got3, demb), after(got1, demb), after(got2, demb)
        outs3, keep3 = to_each(keep3, got3, g)
        mine1 = jnp.concatenate([added(*keep1, got1), added(*keep2, got2)], axis=1)
        demb, mine1 = tied(demb, mine1)
        done1 = scatter_z(mine1)
        demb, north, south, *outs3 = tied(demb, north, south, *outs3)
    below, above = to_neighbours(north, south, "gy")
    if split:
        got3 = swap_each(outs3)
        keep4, send4 = patch_grad(pos, ext, demb, grad_fc1_b, vectors, 4, 4)
        got4 = swap(send4, "gx", 1)
        got3 = [after(v, keep4) for v in got3]
        mine3 = added(*keep3, *got3)
        below, above, got4 = after(below, mine3), after(above, mine3), after(got4, mine3)
    part, west, east = fold_second(demb, below, above, dates, side)
    right, left = to_neighbours(west, east, "gx")
    if split:
        outs4, keep4 = to_each(keep4, got4, g)
        right, left, *outs4 = tied(right, left, *outs4)
        got4 = swap_each(outs4)
        dmasked = fold_third(part, right, left, dates, side)
        dmasked, done1 = tied(dmasked, done1)
        every1 = to_all_gy(jnp.concatenate([done1, ends.reshape(-1, model_width)]))
        pixel_grad = pixel_back(dmasked, front_p, shown, pixel_width)
        got4 = [after(v, pixel_grad) for v in got4]
        mine4, came4 = along_z_sum(jnp.concatenate([mine3, added(*keep4, *got4)], axis=1), chip)
        folded, mine4 = tied(folded, mine4)
        recon = (dense(folded, full_head) * ratio).astype(bf16)
        came4 = [after(v, recon) for v in came4]
        done4 = added(mine4, *came4)
        every1 = tied(*every1, done4)[:-1]
        every4 = to_all_gy(done4)
        ends = added(*[v[2 * each :] for v in every1]).astype(f32).reshape(-1, dec_width)
        every1 = in_order([v[: 2 * each] for v in every1], g)
        sum1 = jnp.concatenate([v[:each] for v in every1], axis=1).astype(f32)
        sum2 = jnp.concatenate([v[each:] for v in every1], axis=0).astype(f32)
        every4 = tied(*every4, sum1, sum2, ends)[:-3]
        every4 = in_order(every4, g)
        sum1, sum2 = jnp.split(sum1, 4, axis=1), jnp.split(sum2, 4, axis=0)
        sum3 = [v[:each] for v in every4]
        grad_patch = jnp.concatenate([v[each : each + quarter] for v in every4])
        small = every4[0][each + quarter :]
    else:
        recon = (dense(folded, full_head) * ratio).astype(bf16)
        dmasked = fold_third(part, right, left, dates, side)
        sum1, sum2 = collect_all(keep1, send1, False), collect_all(keep2, send2, True)
        sum3 = collect_all(keep3, send3, False)
        pixel_grad = pixel_back(dmasked, front_p, shown, pixel_width)
        grad_patch = lax.psum(scatter(dense(ext, demb, 0, 0)), "gy")
        small = lax.psum(jnp.concatenate([*vectors, grad_fc1_b.reshape(-1, model_width)]), ("gy", "gx"))
        ends = lax.psum(ends, "gy")
    small = small.astype(f32)
    mine_of = lambda value, count: lax.dynamic_slice_in_dim(value.reshape(-1), tile_col * count, count)
    grad_bias = mine_of(small[4 : 4 + full_b.shape[1] // model_width], fc1_b.shape[0])
    return (
        recon.reshape(pixels.shape),
        pixel_grad.reshape(pixels.shape),
        grad_patch.astype(f32),
        mine_of(small[0], each),
        mine_of(small[1], each),
        jnp.concatenate(sum3[:3], axis=1).astype(f32),
        sum3[3].astype(f32),
        mine_of(small[2], each),
        mine_of(small[3], each),
        jnp.concatenate(sum1, axis=1).astype(f32),
        grad_bias,
        jnp.concatenate(sum2, axis=0).astype(f32),
        ends[:dec_rows].astype(f32),
        ends[dec_rows:].reshape(head_rows, pixel_width).astype(f32),
    )


def solution(mesh):
    in_specs = (
        P(None, "gy", "gx", None),
        P(None, "gy", "gx"),
        P(),
        P(),
        P(),
        P("gy", "gx"),
        P(None, "gy", "gx", None),
        P("gx", None),
        P("gx"),
        P("gx"),
        P("gx", None),
        P("gx", None),
        P("gx"),
        P("gx"),
        P("gx", None),
        P("gx"),
        P("gx", None),
        P("gx", None),
        P("gx", None),
    )
    out_specs = (
        P(None, "gy", "gx", None),
        P(None, "gy", "gx", None),
        P("gx", None),
        P("gx"),
        P("gx"),
        P("gx", None),
        P("gx", None),
        P("gx"),
        P("gx"),
        P("gx", None),
        P("gx"),
        P("gx", None),
        P("gx", None),
        P("gx", None),
    )
    return jax.shard_map(
        on_device, mesh=mesh, in_specs=in_specs, out_specs=out_specs, check_vma=False
    )
```
